128 devices in a mesh: ctx: 16 (over y, z_hi, core), exp: 8 (over z_lo, x).
Axes of the slice: x: 4, y: 4, z: 4 (z_hi: 2, z_lo: 2; z = z_hi * 2 + z_lo), core: 2. Of those that a mesh axis runs over, the one named last changes fastest.
Arguments:
- queries: bfloat16 [2048, 6144], P('ctx', 'exp'), may hold values from -16 to 16
- keys: bfloat16 [2048, 1024], P('ctx', 'exp'), may hold values from -4 to 4
- values: bfloat16 [2048, 1024], P('ctx', 'exp'), may hold values from -6 to 6
- residual: bfloat16 [2048, 6144], P('ctx', 'exp'), may hold values from -16 to 16
- ln_gain: float32 [6144], P('exp'), may hold values from 0.5 to 1.5
- out_weight: bfloat16 [6144, 6144], P('exp'), may hold values from -0.3125 to 0.3125
- gate_weight: bfloat16 [8, 6144, 5376], P('exp', None, 'ctx'), may hold values from -0.078125 to 0.078125
- up_weight: bfloat16 [8, 6144, 5376], P('exp', None, 'ctx'), may hold values from -0.078125 to 0.078125
- down_weight: bfloat16 [8, 5376, 6144], P('exp', 'ctx'), may hold values from -0.078125 to 0.078125
- expert_ids: int32 [2048, 4], P('ctx'), may hold values from 0 to 7, all different within a row; in each aligned block of 128 rows (0 to 127, 128 to 255, ...) at most 80 rows name the same one
- gate_scores: float32 [2048, 4], P('ctx'), may hold values from 0.1 to 1
Outputs:
- mixed: bfloat16 [2048, 6144], P('ctx', 'exp')
The draws below stay inside these ranges and needn't reach their ends.
Inputs may be any that keep to these rules, and one draw needn't show every extreme that they name: `expert_ids`: each token names 4 different experts. Among the 128 tokens of one context shard (aligned blocks of rows) no expert is named more than 80 times, and in every draw some expert is named exactly 80 times in some shard.
All inputs are finite; a program needn't handle non-finite values.
Results may differ from the reference program's by a relative error of at most 0.0095.
Values may be sent and summed in bfloat16 or wider, within the bound.
No kernel may reach another device: no remote copies, remote signals or barrier semaphores. Data moves between devices by JAX's collectives and lax.ppermute only.
A program may use at most 128 MiB of HBM per device.

```python
import math
import jax
import jax.numpy as jnp
import numpy as np
from jax import lax

D = 6144
QH = 48
KVH = 8
HD = 128
EXPERTS = 8
FFW = 5376
TOPK = 4
TOK_CTX = 128
CAP = 80
TOKENS = 2048
N_CTX = 16


def draw_queries(key, part):
    key = jax.random.fold_in(key, 5)
    result = jnp.clip(2.0 * jax.random.normal(key, (TOKENS, QH * HD), jnp.float32), -12.0, 12.0)
    return result.astype(jnp.bfloat16)


def draw_keys(key, part):
    key = jax.random.fold_in(key, 7)
    result = jnp.clip(jax.random.normal(key, (TOKENS, KVH * HD), jnp.float32), -4.0, 4.0)
    return result.astype(jnp.bfloat16)


def column_scales(key, rise):
    place = lax.iota(jnp.int32, D).astype(jnp.float32) / D
    rough = jnp.exp(jax.random.uniform(key, (D,), jnp.float32, math.log(0.7), math.log(1.4)))
    return (jnp.exp(math.log(0.4) + math.log(rise) * place) * rough)[None, :]


def draw_residual(key, part):
    key = jax.random.fold_in(key, 9)
    key_rows, key_cols, key_vals = jax.random.split(key, 3)
    rows = jnp.exp(jax.random.uniform(key_rows, (TOKENS, 1), jnp.float32, math.log(0.3), math.log(3.0)))
    cols = column_scales(key_cols, 12.0)
    drawn = 0.5 * jnp.clip(jax.random.normal(key_vals, (TOKENS, D), jnp.float32), -3.0, 3.0)
    return jnp.clip(drawn * rows * cols, -16.0, 16.0).astype(jnp.bfloat16)


def shard_levels(rng, extent, shards, smallest, high):
    def one(dim, shards_of):
        steps = jax.random.uniform(jax.random.fold_in(jax.random.fold_in(rng, 6), dim), (shards_of,), jnp.float32, smallest / len(shards), high / len(shards))
        return jnp.repeat(jnp.exp(steps), extent[dim] // shards_of).reshape((-1,) + (1,) * (len(extent) - dim - 1))

    loudness = one(*shards[0])
    for cut in shards[1:]:
        loudness = loudness * one(*cut)
    return loudness


def deal_out(rng, own, number, rows, count, top, most, lean):
    ranking = jax.random.permutation(rng, count)
    packed, usual = shares(count, rows * top, most, lean, True), shares(count, rows * top, most, lean, False)
    places = jnp.arange(count)

    def named(tallies, offset_by):
        used = int((tallies > 0).sum())
        fixed = max(1, used // 4)
        moved = fixed + (places - fixed + offset_by * (used - fixed)) % max(1, count - fixed)
        return jnp.zeros((count,), jnp.int32).at[ranking[jnp.where(places < fixed, places, moved)]].set(jnp.asarray(tallies, jnp.int32))

    tallies = jnp.where(number % 4 == 0, named(packed, number // 4), named(usual, number - number // 4 - 1))
    mixed = jax.random.permutation(jax.random.fold_in(own, 3), count)
    giver, sink = mixed[0:count // 2 * 2:2], mixed[1:count // 2 * 2:2]
    margin = jnp.minimum(tallies[giver] - 1, most - tallies[sink]) // 2
    margin = jnp.where((giver == ranking[0]) | (sink == ranking[0]) | (tallies[sink] == 0), 0, jnp.maximum(margin, 0))
    moved = jax.random.randint(jax.random.fold_in(own, 4), (count // 2,), 0, 1 << 20) % (margin + 1)
    tallies = tallies.at[giver].add(-moved).at[sink].add(moved)
    items = jnp.searchsorted(jnp.cumsum(tallies), jnp.arange(rows * top), side="right").astype(jnp.int32)
    table = items.reshape(top, rows).T
    table = table[jax.random.permutation(jax.random.fold_in(own, 1), rows)]
    offset_by = jax.random.randint(jax.random.fold_in(own, 2), (rows, 1), 0, top)
    return jnp.take_along_axis(table, (jnp.arange(top)[None, :] + offset_by) % top, axis=1)


def shares(number_of, total, most, lean, full):
    weights = [(1 << 20) // math.isqrt(rank ** lean) + 1 for rank in range(1, number_of + 1)]
    largest = most if full else min(most, max(-(-total // number_of), total * weights[0] // sum(weights)))
    least = 1 if total - largest >= number_of - 1 else 0
    holding, surplus = [largest] + [least] * (number_of - 1), total - largest - least * (number_of - 1)
    while surplus > 0:
        free = [i for i in range(1, number_of) if holding[i] < largest] or [i for i in range(1, number_of) if holding[i] < most]
        whole, left = sum([weights[i] for i in free]), surplus
        for i in free:
            extra = min(most - holding[i], max(1, left * weights[i] // whole), surplus)
            holding[i] = holding[i] + extra
            surplus = surplus - extra
    return np.array(holding)


def normal_values(key, dims, deviation, most, cuts=(), kind=jnp.bfloat16):
    entries = deviation * jax.random.normal(key, dims, jnp.float32)
    if cuts:
        entries = entries * shard_levels(key, dims, cuts, -0.22, 0.18)
    return jnp.clip(entries, -most, most).astype(kind)


def setup_inputs(seed: int = 0) -> dict:
    key_list = jax.random.split(jax.random.key(seed), 12)
    queries = draw_queries(jax.random.fold_in(key_list[11], 71), 0)
    keys = draw_keys(jax.random.fold_in(key_list[11], 71), 0)
    values = normal_values(key_list[2], (TOKENS, KVH * HD), 1.0, 6.0, ((0, 16), (1, 8)))
    residual = draw_residual(jax.random.fold_in(key_list[11], 71), 0)
    ln_gain = jnp.clip(1.0 + 0.1 * jax.random.normal(key_list[4], (D,), jnp.float32), 0.5, 1.5)
    out_weight = normal_values(key_list[5], (QH * HD, D), (QH * HD // 16) ** -0.5, 0.3125, ((0, 8),))
    gate_weight = normal_values(key_list[6], (EXPERTS, D, FFW), D ** -0.5, 0.078125, ((0, 8), (2, 16)))
    up_weight = normal_values(key_list[7], (EXPERTS, D, FFW), D ** -0.5, 0.078125, ((0, 8), (2, 16)))
    down_weight = normal_values(key_list[8], (EXPERTS, FFW, D), FFW ** -0.5, 0.078125, ((0, 8), (1, 16)))
    expert_ids_keys = jax.random.split(jax.random.fold_in(key_list[9], 1), TOKENS // TOK_CTX)
    expert_ids_turns = jax.random.permutation(jax.random.fold_in(key_list[9], 3), TOKENS // TOK_CTX)
    expert_ids = jax.vmap(lambda own, number: deal_out(jax.random.fold_in(key_list[9], 2), own, number, TOK_CTX, EXPERTS, TOPK, CAP, 2))(expert_ids_keys, expert_ids_turns).reshape((TOKENS, TOPK))
    gate_scores = jnp.clip(0.1 + 0.9 * jax.random.uniform(key_list[10], (TOKENS, TOPK), jnp.float32) ** shard_levels(key_list[10], (TOKENS, TOPK), ((0, 16),), -0.2, 0.2), 0.1, 1.0)
    return {"queries": queries, "keys": keys, "values": values, "residual": residual, "ln_gain": ln_gain, "out_weight": out_weight, "gate_weight": gate_weight, "up_weight": up_weight, "down_weight": down_weight, "expert_ids": expert_ids, "gate_scores": gate_scores}


EPS = 1e-05

def head_attention(q_head, k_head, v_head):
    scores = jnp.dot(q_head, k_head.T, preferred_element_type=jnp.float32) * HD ** (-0.5)
    rows = lax.broadcasted_iota(jnp.int32, scores.shape, 0)
    cols = lax.broadcasted_iota(jnp.int32, scores.shape, 1)
    keep = cols <= rows
    scores = jnp.where(keep, scores, -1e+30)
    top = lax.optimization_barrier(jnp.max(scores, axis=1, keepdims=True))
    expw = jnp.where(keep, jnp.exp(scores - top), 0.0)
    denom = lax.optimization_barrier(jnp.sum(expw, axis=1, keepdims=True))
    summed = jnp.dot(expw.astype(jnp.bfloat16), v_head, preferred_element_type=jnp.float32)
    return (summed / denom).astype(jnp.bfloat16)

def expert_rows(normed, w_gate, w_up, w_down):
    gate_part = jnp.dot(normed, w_gate, preferred_element_type=jnp.float32)
    up_part = jnp.dot(normed, w_up, preferred_element_type=jnp.float32)
    act = (jax.nn.silu(gate_part) * up_part).astype(jnp.bfloat16)
    width = FFW // N_CTX

    def add_block(total, index):
        piece = lax.dynamic_slice_in_dim(act, index * width, width, 1)
        rows_down = lax.dynamic_slice_in_dim(w_down, index * width, width, 0)
        term = jnp.dot(piece, rows_down, preferred_element_type=jnp.float32).astype(jnp.bfloat16)
        return (total + lax.optimization_barrier(term).astype(jnp.float32), None)
    total, _ = lax.scan(add_block, jnp.zeros((TOKENS, D), jnp.float32), jnp.arange(N_CTX, dtype=jnp.int32))
    return total.astype(jnp.bfloat16)

def reference(queries, keys, values, residual, ln_gain, out_weight, gate_weight, up_weight, down_weight, expert_ids, gate_scores):
    group = QH // KVH
    q_heads = queries.reshape(TOKENS, QH, HD).transpose(1, 0, 2)
    k_heads = jnp.repeat(keys.reshape(TOKENS, KVH, HD).transpose(1, 0, 2), group, axis=0)
    v_heads = jnp.repeat(values.reshape(TOKENS, KVH, HD).transpose(1, 0, 2), group, axis=0)
    heads = lax.map(lambda item: head_attention(item[0], item[1], item[2]), (q_heads, k_heads, v_heads))
    attended = heads.transpose(1, 0, 2).reshape(TOKENS, QH * HD)
    projected = jnp.dot(attended, out_weight, preferred_element_type=jnp.float32)
    hidden = residual.astype(jnp.float32) + projected
    mean = lax.optimization_barrier(jnp.sum(hidden, axis=1, keepdims=True)) / D
    second = lax.optimization_barrier(jnp.sum(hidden * hidden, axis=1, keepdims=True)) / D
    normed = ((hidden - mean) * lax.rsqrt(second - mean * mean + EPS) * ln_gain[None, :]).astype(jnp.bfloat16)
    share = gate_scores / lax.optimization_barrier(jnp.sum(gate_scores, axis=1, keepdims=True))

    def one_expert(total, item):
        index, w_gate, w_up, w_down = item
        out_rows = lax.optimization_barrier(expert_rows(normed, w_gate, w_up, w_down)).astype(jnp.float32)
        coefficient = lax.optimization_barrier(jnp.sum(jnp.where(expert_ids == index, share, 0.0), axis=1))
        return (total + coefficient[:, None] * out_rows, None)
    items = (jnp.arange(EXPERTS, dtype=jnp.int32), gate_weight, up_weight, down_weight)
    moe, _ = lax.scan(one_expert, jnp.zeros((TOKENS, D), jnp.float32), items)
    return (hidden + moe).astype(jnp.bfloat16)
```

```python
import functools

import jax
import jax.numpy as jnp
from jax import lax
from jax.experimental import pallas as pl
from jax.experimental.pallas import tpu as pltpu
from jax.sharding import PartitionSpec as P

D = 6144
HD = 128
EXPERTS = 8
TOPK = 4
CAP = 80
AUX = 16
TOK = 128
SLICE = 768
SHARDS = 16
UNITS = 336
MAIN = 256
REST = UNITS - MAIN
EPS = 1e-05
F32 = jnp.float32
BF16 = jnp.bfloat16
MIB = 1 << 20


def place(index):
    return index // 4, (index // 2) % 2, index % 2


def route(dy, dz, dc):
    pairs = []
    for index in range(SHARDS):
        y, z, c = place(index)
        pairs.append((index, (((y + dy) % 4) * 2 + (z + dz) % 2) * 2 + (c + dc) % 2))
    return pairs


def send(block, dy=0, dz=0, dc=0):
    return lax.ppermute(block, "ctx", route(dy, dz, dc))


def call(kernel, out_shape, limit, flops, moved, **kwargs):
    return pl.pallas_call(
        kernel,
        out_shape=out_shape,
        compiler_params=pltpu.CompilerParams(vmem_limit_bytes=limit * MIB),
        cost_estimate=pl.CostEstimate(flops=flops, bytes_accessed=moved, transcendentals=0),
        **kwargs,
    )


def shape(dims, dtype=BF16):
    return jax.ShapeDtypeStruct(dims, dtype)


def pieces(value):
    high = value.astype(BF16).astype(F32)
    left = value - high
    mid = left.astype(BF16).astype(F32)
    return high, mid, left - mid


def routing_kernel(ids_ref, scores_ref, placing_ref, high_ref, low_ref):
    ids = ids_ref[...]
    scores = scores_ref[...]
    total = scores[:, 0:1] + scores[:, 1:2] + scores[:, 2:3] + scores[:, 3:4]
    lanes = lax.broadcasted_iota(jnp.int32, (TOK, TOK), 1)
    rows = lax.broadcasted_iota(jnp.int32, (TOK, TOK), 0)
    named = [(lanes == ids[:, k : k + 1]).astype(F32) for k in range(TOPK)]
    member = named[0] + named[1] + named[2] + named[3]
    lower = (lanes < rows).astype(BF16)
    slots = jnp.dot(lower, member.astype(BF16), preferred_element_type=F32)
    wide = lax.broadcasted_iota(jnp.int32, (TOK, EXPERTS * TOK), 1)
    columns = lax.broadcasted_iota(jnp.int32, (TOK, EXPERTS * CAP), 1)
    placed = jnp.zeros((TOK, EXPERTS * TOK), F32)
    shares = jnp.zeros((TOK, EXPERTS * CAP), F32)
    for k in range(TOPK):
        slot = jnp.sum(named[k] * slots, axis=1, keepdims=True).astype(jnp.int32)
        expert = ids[:, k : k + 1]
        placed = placed + (wide == expert * TOK + slot).astype(F32)
        share = scores[:, k : k + 1] / total
        shares = shares + jnp.where(columns == expert * CAP + slot, share, 0.0)
    for e in range(EXPERTS):
        placing_ref[e] = placed[:, e * TOK : (e + 1) * TOK].T.astype(BF16)
    high = shares.astype(BF16)
    high_ref[...] = high
    low_ref[...] = (shares - high.astype(F32)).astype(BF16)


def routing(expert_ids, gate_scores):
    return call(
        routing_kernel,
        (
            shape((EXPERTS, TOK, TOK)),
            shape((TOK, EXPERTS * CAP)),
            shape((TOK, EXPERTS * CAP)),
        ),
        16,
        10**7,
        10**6,
    )(expert_ids, gate_scores)


def attention_kernel(starts_ref, queries_ref, paired_ref, weight_ref, term_ref, held, ready):
    copy = pltpu.make_async_copy(weight_ref, held, ready)
    copy.start()
    keys = paired_ref[:, 0].reshape(SHARDS * TOK, HD)
    values = paired_ref[:, 1].reshape(SHARDS * TOK, HD)
    rows = lax.broadcasted_iota(jnp.int32, (TOK, TOK), 0)
    lanes = lax.broadcasted_iota(jnp.int32, (TOK, TOK), 1)
    ahead = rows - lanes + starts_ref[SHARDS]
    keep = jnp.concatenate([ahead >= starts_ref[b] for b in range(SHARDS)], axis=1)
    heads = []
    for h in range(queries_ref.shape[1] // HD):
        query = queries_ref[:, h * HD : (h + 1) * HD]
        scores = lax.dot_general(
            query, keys, (((1,), (1,)), ((), ())), preferred_element_type=F32
        ) * (HD**-0.5)
        scores = jnp.where(keep, scores, -1e30)
        top = jnp.max(scores, axis=1, keepdims=True)
        expw = jnp.exp(scores - top)
        denom = jnp.sum(expw, axis=1, keepdims=True)
        summed = jnp.dot(expw.astype(BF16), values, preferred_element_type=F32)
        heads.append((summed / denom).astype(BF16))
    attended = jnp.concatenate(heads, axis=1)
    copy.wait()
    for j in range(EXPERTS):
        term_ref[j] = jnp.dot(
            attended, held[:, j * SLICE : (j + 1) * SLICE], preferred_element_type=F32
        ).astype(BF16)


def attention(starts, queries, paired, out_weight):
    return call(
        attention_kernel,
        shape((EXPERTS, TOK, SLICE)),
        48,
        2 * 10**9,
        13 * 10**6,
        in_specs=[
            pl.BlockSpec(memory_space=pltpu.SMEM),
            pl.BlockSpec(memory_space=pltpu.VMEM),
            pl.BlockSpec(memory_space=pltpu.VMEM),
            pl.BlockSpec(memory_space=pl.ANY),
        ],
        out_specs=pl.BlockSpec(memory_space=pltpu.VMEM),
        scratch_shapes=[pltpu.VMEM((SLICE, D), BF16), pltpu.SemaphoreType.DMA],
    )(starts, queries, paired, out_weight)


def dispatch_kernel(terms_ref, residual_ref, gain_ref, placing_ref, hidden_ref, out_ref):
    hidden = residual_ref[...].astype(F32)
    for j in range(EXPERTS):
        hidden = hidden + terms_ref[j].astype(F32)
    hidden_ref[...] = hidden
    mean = jnp.sum(hidden, axis=1, keepdims=True) * (1.0 / SLICE)
    apart = (hidden - mean).astype(BF16)
    lanes = lax.broadcasted_iota(jnp.int32, (TOK, TOK), 1)
    high, mid, low = pieces(mean)
    spread = jnp.where(lanes == 0, high, jnp.where(lanes == 1, mid, jnp.where(lanes == 2, low, 0.0)))
    means = spread.T[:AUX].astype(BF16)
    rows = lax.broadcasted_iota(jnp.int32, (AUX, SLICE), 0)
    high, mid, low = pieces(gain_ref[...])
    gains = jnp.where(rows == 3, high, jnp.where(rows == 4, mid, jnp.where(rows == 5, low, 0.0)))
    for e in range(EXPERTS):
        placing = placing_ref[e]
        out_ref[e, :CAP] = jnp.dot(placing[:CAP], apart, preferred_element_type=F32).astype(BF16)
        sent = lax.dot_general(means, placing, (((1,), (1,)), ((), ())), preferred_element_type=F32)
        out_ref[e, CAP:] = jnp.concatenate(
            [sent + gains[:, :TOK], gains[:, TOK:]], axis=1
        ).astype(BF16)


def dispatch(terms, residual, gain, placing):
    return call(
        dispatch_kernel,
        (shape((TOK, SLICE), F32), shape((EXPERTS, CAP + AUX, SLICE))),
        24,
        2 * 10**8,
        5 * 10**6,
    )(terms, residual, gain, placing)


def norm_kernel(arrived_ref, out_ref):
    rows = lax.broadcasted_iota(jnp.int32, (CAP, TOK), 0)
    lanes = lax.broadcasted_iota(jnp.int32, (CAP, TOK), 1)
    diagonal = (rows == lanes).astype(BF16)
    means = []
    total = jnp.zeros((CAP, 1), F32)
    for j in range(EXPERTS):
        turned = lax.dot_general(
            diagonal, arrived_ref[j, CAP:, :TOK], (((1,), (1,)), ((), ())), preferred_element_type=F32
        )
        means.append(turned[:, 0:1] + turned[:, 1:2] + turned[:, 2:3])
        total = total + SLICE * means[j]
        total = total + jnp.sum(arrived_ref[j, :CAP].astype(F32), axis=1, keepdims=True)
    mean = total / D
    spread = jnp.zeros((CAP, 1), F32)
    for j in range(EXPERTS):
        apart = arrived_ref[j, :CAP].astype(F32) + (means[j] - mean)
        spread = spread + jnp.sum(apart * apart, axis=1, keepdims=True)
    scale = lax.rsqrt(spread / D + EPS)
    for j in range(EXPERTS):
        aux = arrived_ref[j, CAP:].astype(F32)
        gain = aux[3:4] + aux[4:5] + aux[5:6]
        apart = arrived_ref[j, :CAP].astype(F32) + (means[j] - mean)
        out_ref[j] = (apart * scale * gain).astype(BF16)


def norm(arrived):
    return call(norm_kernel, shape((EXPERTS, CAP, SLICE)), 16, 10**7, 2 * 10**6)(arrived)


STEP = 2
STEPS = EXPERTS // STEP


def expert_kernel(parts, *refs):
    count = len(parts)
    xs, refs = refs[:count], refs[count:]
    gate_own, gate_other, up_own, up_other, down_own, down_other = refs[:6]
    outs = refs[6 : 6 + count]
    rows_ref, gate_sum, up_sum, act_ref, gate_rest, up_rest, down_rest = refs[6 + count :]
    step = pl.program_id(0)

    @pl.when(step == 0)
    def _():
        gate_sum[...] = jnp.zeros_like(gate_sum)
        up_sum[...] = jnp.zeros_like(up_sum)
        gate_rest[...] = jnp.zeros_like(gate_rest)
        up_rest[...] = jnp.zeros_like(up_rest)
        down_rest[...] = jnp.zeros_like(down_rest)

    @pl.when(step < STEPS)
    def _():
        for (shard, start, steps), x in zip(parts, xs):

            @pl.when((step >= start) & (step < start + steps))
            def _():
                for k in range(STEP):
                    rows_ref[shard * CAP : (shard + 1) * CAP, k * SLICE : (k + 1) * SLICE] = x[k]

        rows = rows_ref[...]
        for own, other, rest, total in (
            (gate_own, gate_other, gate_rest, gate_sum),
            (up_own, up_other, up_rest, up_sum),
        ):
            rest[:, :REST] = own[0, :, MAIN:]
            rest[:, 128 : 128 + REST] = other[0, :, MAIN:]
            total[:, :MAIN] += jnp.dot(rows, own[0, :, :MAIN], preferred_element_type=F32)
            total[:, MAIN : 2 * MAIN] += jnp.dot(
                rows, other[0, :, :MAIN], preferred_element_type=F32
            )
            total[:, 2 * MAIN :] += jnp.dot(rows, rest[...], preferred_element_type=F32)

    @pl.when(step == STEPS)
    def _():
        gate = gate_sum[...]
        act_ref[...] = (gate / (1.0 + jnp.exp(-gate)) * up_sum[...]).astype(BF16)

    @pl.when(step >= STEPS)
    def _():
        down_rest[:REST] = down_own[0, MAIN:]
        down_rest[128 : 128 + REST] = down_other[0, MAIN:]
        for k in range(STEP):
            cols = slice(k * SLICE, (k + 1) * SLICE)
            result = jnp.dot(act_ref[:, :MAIN], down_own[0, :MAIN, cols], preferred_element_type=F32)
            result += jnp.dot(
                act_ref[:, MAIN : 2 * MAIN], down_other[0, :MAIN, cols], preferred_element_type=F32
            )
            result += jnp.dot(
                act_ref[:, 2 * MAIN :], down_rest[:, cols], preferred_element_type=F32
            )
            result = result.astype(BF16)
            for (shard, start, steps), out in zip(parts, outs):

                @pl.when((step >= STEPS + start) & (step < STEPS + start + steps))
                def _():
                    out[k] = result[shard * CAP : (shard + 1) * CAP]


def expert(shards, weights):
    parts, arrays = [], []
    for number, split in enumerate(shards):
        start = 0
        for array in split:
            steps = array.shape[0] // STEP
            parts.append((number, start, steps))
            arrays.append(array)
            start += steps
    total = CAP * len(shards)
    width = STEP * SLICE

    def rows_spec(part, late):
        _, start, steps = part
        return pl.BlockSpec(
            (STEP, CAP, SLICE),
            lambda i: (jnp.clip(i - start - late, 0, steps - 1), 0, 0),
        )

    across = pl.BlockSpec((1, width, UNITS), lambda i: (0, jnp.minimum(i, STEPS - 1), 0))
    along = pl.BlockSpec((1, UNITS, width), lambda i: (0, 0, jnp.maximum(i - STEPS, 0)))
    outs = call(
        functools.partial(expert_kernel, parts),
        tuple(shape(array.shape) for array in arrays),
        44,
        total * D * 2 * UNITS * 6,
        27 * 10**6,
        grid=(2 * STEPS,),
        in_specs=[rows_spec(part, 0) for part in parts] + [across] * 4 + [along] * 2,
        out_specs=tuple(rows_spec(part, STEPS) for part in parts),
        scratch_shapes=[
            pltpu.VMEM((total, width), BF16),
            pltpu.VMEM((total, 3 * MAIN), F32),
            pltpu.VMEM((total, 3 * MAIN), F32),
            pltpu.VMEM((total, 3 * MAIN), BF16),
            pltpu.VMEM((width, MAIN), BF16),
            pltpu.VMEM((width, MAIN), BF16),
            pltpu.VMEM((MAIN, width), BF16),
        ],
    )(*arrays, *weights)
    results, taken = [], 0
    for split in shards:
        results.append(list(outs[taken : taken + len(split)]))
        taken += len(split)
    return results


def add(*values):
    total = values[0].astype(F32)
    for value in values[1:]:
        total = total + value.astype(F32)
    return total.astype(BF16)


def combine_kernel(hidden_ref, high_ref, low_ref, outputs_ref, mixed_ref):
    outputs = outputs_ref[...].reshape(EXPERTS * CAP, SLICE)
    moe = jnp.dot(high_ref[...], outputs, preferred_element_type=F32)
    moe += jnp.dot(low_ref[...], outputs, preferred_element_type=F32)
    mixed_ref[...] = (hidden_ref[...] + moe).astype(BF16)


def combine(hidden, high, low, outputs):
    return call(combine_kernel, shape((TOK, SLICE)), 16, 3 * 10**8, 2 * 10**6)(
        hidden, high, low, outputs
    )


def body(
    queries,
    keys,
    values,
    residual,
    ln_gain,
    out_weight,
    gate_weight,
    up_weight,
    down_weight,
    expert_ids,
    gate_scores,
):
    ctx = lax.axis_index("ctx")
    own = jnp.stack((keys, values))[None]
    near = jnp.concatenate([own, send(own, dz=1)])
    near = jnp.concatenate([near, send(near, dy=1), send(near, dy=-1), send(near, dy=2)])
    paired = jnp.concatenate([near, send(near, dc=1)])
    y, z, c = ctx // 4, (ctx // 2) % 2, ctx % 2
    starts = [
        ((((y - dy) % 4) * 2 + (z + dz) % 2) * 2 + (c + dc) % 2) * TOK
        for dc in (0, 1)
        for dy in (0, 1, -1, 2)
        for dz in (0, 1)
    ]
    starts = jnp.stack(starts + [ctx * TOK]).astype(jnp.int32)
    placing, high, low = routing(expert_ids, gate_scores)
    weights = []
    for weight in (gate_weight, up_weight, down_weight):
        weights += [weight, send(weight, dc=1)]

    term = attention(starts, queries, paired, out_weight)
    terms = lax.all_to_all(term, "exp", 0, 0, tiled=True)
    hidden, outgoing = dispatch(terms, residual, ln_gain[None], placing)
    arrived = lax.all_to_all(outgoing, "exp", 0, 0, tiled=True)
    mine = norm(arrived)

    half = EXPERTS // 2
    back, ahead, across = send(mine, dy=1), send(mine, dy=-1), send(mine, dz=1)
    across_back, across_ahead = send(across, dy=1), send(across, dy=-1)
    far = [send(back[:half], dy=1), send(ahead[half:], dy=-1)]
    across_far = [send(across_back[:half], dy=1), send(across_ahead[half:], dy=-1)]
    first = expert([[mine], [across], [back], [ahead]], weights)
    second = expert([[across_back], [across_ahead], far, across_far], weights)
    part = [first[0][0], first[2][0], first[3][0], second[2]]
    across_part = [first[1][0], second[0][0], second[1][0], second[3]]

    def ring(part):
        mine, back, ahead, far = part
        low_half, high_half = send(far[0], dy=1), send(far[1], dy=-1)
        ahead = jnp.concatenate([add(ahead[:half], low_half), ahead[half:]])
        back = jnp.concatenate([back[:half], add(back[half:], high_half)])
        return mine, send(ahead, dy=1), send(back, dy=-1)

    across_sum = send(add(*ring(across_part)), dz=1)
    result = add(across_sum, *ring(part))
    outputs = lax.all_to_all(result, "exp", 0, 0, tiled=True)
    return combine(hidden, high, low, outputs)


def solution(mesh):
    return jax.shard_map(
        body,
        mesh=mesh,
        in_specs=(
            P("ctx", "exp"),
            P("ctx", "exp"),
            P("ctx", "exp"),
            P("ctx", "exp"),
            P("exp"),
            P("exp", None),
            P("exp", None, "ctx"),
            P("exp", None, "ctx"),
            P("exp", "ctx", None),
            P("ctx", None),
            P("ctx", None),
        ),
        out_specs=P("ctx", "exp"),
        check_vma=False,
    )
```

```python
import functools

import jax
import jax.numpy as jnp
from jax import lax
from jax.experimental import pallas as pl
from jax.experimental.pallas import tpu as pltpu
from jax.sharding import PartitionSpec as P

D = 6144
HD = 128
EXPERTS = 8
TOPK = 4
CAP = 80
AUX = 16
TOK = 128
SLICE = 768
SHARDS = 16
UNITS = 336
EPS = 1e-05
F32 = jnp.float32
BF16 = jnp.bfloat16
MIB = 1 << 20


def place(index):
    return index // 4, (index // 2) % 2, index % 2


def route(dy, dz, dc):
    pairs = []
    for index in range(SHARDS):
        y, z, c = place(index)
        pairs.append((index, (((y + dy) % 4) * 2 + (z + dz) % 2) * 2 + (c + dc) % 2))
    return pairs


def send(block, dy=0, dz=0, dc=0):
    return lax.ppermute(block, "ctx", route(dy, dz, dc))


def call(kernel, out_shape, limit, flops, moved, **kwargs):
    return pl.pallas_call(
        kernel,
        out_shape=out_shape,
        compiler_params=pltpu.CompilerParams(vmem_limit_bytes=limit * MIB),
        cost_estimate=pl.CostEstimate(flops=flops, bytes_accessed=moved, transcendentals=0),
        **kwargs,
    )


def shape(dims, dtype=BF16):
    return jax.ShapeDtypeStruct(dims, dtype)


def pieces(value):
    high = value.astype(BF16).astype(F32)
    left = value - high
    mid = left.astype(BF16).astype(F32)
    return high, mid, left - mid


def routing_kernel(ids_ref, scores_ref, placing_ref, high_ref, low_ref):
    ids = ids_ref[...]
    scores = scores_ref[...]
    total = scores[:, 0:1] + scores[:, 1:2] + scores[:, 2:3] + scores[:, 3:4]
    lanes = lax.broadcasted_iota(jnp.int32, (TOK, TOK), 1)
    rows = lax.broadcasted_iota(jnp.int32, (TOK, TOK), 0)
    named = [(lanes == ids[:, k : k + 1]).astype(F32) for k in range(TOPK)]
    member = named[0] + named[1] + named[2] + named[3]
    lower = (lanes < rows).astype(BF16)
    slots = jnp.dot(lower, member.astype(BF16), preferred_element_type=F32)
    wide = lax.broadcasted_iota(jnp.int32, (TOK, EXPERTS * TOK), 1)
    columns = lax.broadcasted_iota(jnp.int32, (TOK, EXPERTS * CAP), 1)
    placed = jnp.zeros((TOK, EXPERTS * TOK), F32)
    shares = jnp.zeros((TOK, EXPERTS * CAP), F32)
    for k in range(TOPK):
        slot = jnp.sum(named[k] * slots, axis=1, keepdims=True).astype(jnp.int32)
        expert = ids[:, k : k + 1]
        placed = placed + (wide == expert * TOK + slot).astype(F32)
        share = scores[:, k : k + 1] / total
        shares = shares + jnp.where(columns == expert * CAP + slot, share, 0.0)
    for e in range(EXPERTS):
        placing_ref[e] = placed[:, e * TOK : (e + 1) * TOK].T.astype(BF16)
    high = shares.astype(BF16)
    high_ref[...] = high
    low_ref[...] = (shares - high.astype(F32)).astype(BF16)


def routing(expert_ids, gate_scores):
    return call(
        routing_kernel,
        (
            shape((EXPERTS, TOK, TOK)),
            shape((TOK, EXPERTS * CAP)),
            shape((TOK, EXPERTS * CAP)),
        ),
        16,
        10**7,
        10**6,
    )(expert_ids, gate_scores)


def attention_kernel(starts_ref, queries_ref, paired_ref, weight_ref, term_ref, held, ready):
    copy = pltpu.make_async_copy(weight_ref, held, ready)
    copy.start()
    keys = paired_ref[:, 0].reshape(SHARDS * TOK, HD)
    values = paired_ref[:, 1].reshape(SHARDS * TOK, HD)
    rows = lax.broadcasted_iota(jnp.int32, (TOK, TOK), 0)
    lanes = lax.broadcasted_iota(jnp.int32, (TOK, TOK), 1)
    ahead = rows - lanes + starts_ref[SHARDS]
    keep = jnp.concatenate([ahead >= starts_ref[b] for b in range(SHARDS)], axis=1)
    heads = []
    for h in range(queries_ref.shape[1] // HD):
        query = queries_ref[:, h * HD : (h + 1) * HD]
        scores = lax.dot_general(
            query, keys, (((1,), (1,)), ((), ())), preferred_element_type=F32
        ) * (HD**-0.5)
        scores = jnp.where(keep, scores, -1e30)
        top = jnp.max(scores, axis=1, keepdims=True)
        expw = jnp.exp(scores - top)
        denom = jnp.sum(expw, axis=1, keepdims=True)
        summed = jnp.dot(expw.astype(BF16), values, preferred_element_type=F32)
        heads.append((summed / denom).astype(BF16))
    attended = jnp.concatenate(heads, axis=1)
    copy.wait()
    for j in range(EXPERTS):
        term_ref[j] = jnp.dot(
            attended, held[:, j * SLICE : (j + 1) * SLICE], preferred_element_type=F32
        ).astype(BF16)


def attention(starts, queries, paired, out_weight):
    return call(
        attention_kernel,
        shape((EXPERTS, TOK, SLICE)),
        48,
        2 * 10**9,
        13 * 10**6,
        in_specs=[
            pl.BlockSpec(memory_space=pltpu.SMEM),
            pl.BlockSpec(memory_space=pltpu.VMEM),
            pl.BlockSpec(memory_space=pltpu.VMEM),
            pl.BlockSpec(memory_space=pl.ANY),
        ],
        out_specs=pl.BlockSpec(memory_space=pltpu.VMEM),
        scratch_shapes=[pltpu.VMEM((SLICE, D), BF16), pltpu.SemaphoreType.DMA],
    )(starts, queries, paired, out_weight)


def dispatch_kernel(terms_ref, residual_ref, gain_ref, placing_ref, *refs):
    hidden_ref, out_ref = refs[-2:]
    hidden = residual_ref[...].astype(F32)
    for j in range(EXPERTS):
        hidden = hidden + terms_ref[j].astype(F32)
    hidden_ref[...] = hidden
    mean = jnp.sum(hidden, axis=1, keepdims=True) * (1.0 / SLICE)
    apart = (hidden - mean).astype(BF16)
    lanes = lax.broadcasted_iota(jnp.int32, (TOK, TOK), 1)
    high, mid, low = pieces(mean)
    spread = jnp.where(lanes == 0, high, jnp.where(lanes == 1, mid, jnp.where(lanes == 2, low, 0.0)))
    means = spread.T[:AUX].astype(BF16)
    rows = lax.broadcasted_iota(jnp.int32, (AUX, SLICE), 0)
    high, mid, low = pieces(gain_ref[...])
    gains = jnp.where(rows == 3, high, jnp.where(rows == 4, mid, jnp.where(rows == 5, low, 0.0)))
    for e in range(EXPERTS):
        placing = placing_ref[e]
        out_ref[e, :CAP] = jnp.dot(placing[:CAP], apart, preferred_element_type=F32).astype(BF16)
        sent = lax.dot_general(means, placing, (((1,), (1,)), ((), ())), preferred_element_type=F32)
        out_ref[e, CAP:] = jnp.concatenate(
            [sent + gains[:, :TOK], gains[:, TOK:]], axis=1
        ).astype(BF16)


def dispatch(terms, residual, gain, placing, after):
    whole = pl.BlockSpec(memory_space=pltpu.VMEM)
    return call(
        dispatch_kernel,
        (shape((TOK, SLICE), F32), shape((EXPERTS, CAP + AUX, SLICE))),
        24,
        2 * 10**8,
        5 * 10**6,
        in_specs=[whole] * 4 + [pl.BlockSpec(memory_space=pl.ANY)] * len(after),
    )(terms, residual, gain, placing, *after)


def norm_kernel(arrived_ref, out_ref):
    rows = lax.broadcasted_iota(jnp.int32, (CAP, TOK), 0)
    lanes = lax.broadcasted_iota(jnp.int32, (CAP, TOK), 1)
    diagonal = (rows == lanes).astype(BF16)
    means = []
    total = jnp.zeros((CAP, 1), F32)
    for j in range(EXPERTS):
        turned = lax.dot_general(
            diagonal, arrived_ref[j, CAP:, :TOK], (((1,), (1,)), ((), ())), preferred_element_type=F32
        )
        means.append(turned[:, 0:1] + turned[:, 1:2] + turned[:, 2:3])
        total = total + SLICE * means[j]
        total = total + jnp.sum(arrived_ref[j, :CAP].astype(F32), axis=1, keepdims=True)
    mean = total / D
    spread = jnp.zeros((CAP, 1), F32)
    for j in range(EXPERTS):
        apart = arrived_ref[j, :CAP].astype(F32) + (means[j] - mean)
        spread = spread + jnp.sum(apart * apart, axis=1, keepdims=True)
    scale = lax.rsqrt(spread / D + EPS)
    for j in range(EXPERTS):
        aux = arrived_ref[j, CAP:].astype(F32)
        gain = aux[3:4] + aux[4:5] + aux[5:6]
        apart = arrived_ref[j, :CAP].astype(F32) + (means[j] - mean)
        out_ref[j] = (apart * scale * gain).astype(BF16)


def norm(arrived):
    return call(norm_kernel, shape((EXPERTS, CAP, SLICE)), 16, 10**7, 2 * 10**6)(arrived)


STEP = 2
STEPS = EXPERTS // STEP
WIDTH = STEP * SLICE
HELD = 2 * UNITS


def expert_kernel(pieces_in, pieces_out, n_in, *refs):
    xs, refs = refs[:n_in], refs[n_in:]
    weights, outs = refs[:6], refs[6:-8]
    rows_ref, gate_ref, up_ref, down_ref, gate_sum, up_sum, act_ref, ready = refs[-8:]

    def copies(step):
        found = []
        for number, (held, late) in enumerate(((gate_ref, 0), (up_ref, 0), (down_ref, STEPS))):
            if not 0 <= step - late < STEPS:
                continue
            columns = pl.ds((step - late) * WIDTH, WIDTH)
            for core in range(2):
                found.append(
                    pltpu.make_async_copy(
                        weights[2 * number + core].at[:, columns],
                        held.at[pl.ds(core * UNITS, UNITS), columns],
                        ready.at[number * 2 + core, step - late],
                    )
                )
        return found

    def start(step):
        for copy in copies(step):
            copy.start()

    start(0)
    start(1)
    for step in range(2 * STEPS):
        if step < STEPS:
            for shard, split in enumerate(pieces_in):
                block = 0
                for number, first, count in split:
                    for k in range(first, first + count):
                        if block // STEP == step:
                            rows_ref[
                                shard * CAP : (shard + 1) * CAP, block * SLICE : (block + 1) * SLICE
                            ] = xs[number][k]
                        block += 1
        for copy in copies(step):
            copy.wait()
        if step + 2 < 2 * STEPS:
            start(step + 2)
        if step < STEPS:
            columns = slice(step * WIDTH, (step + 1) * WIDTH)
            rows = rows_ref[:, columns]
            for held, total in ((gate_ref, gate_sum), (up_ref, up_sum)):
                term = lax.dot_general(
                    rows, held[:, columns], (((1,), (1,)), ((), ())), preferred_element_type=F32
                )
                if step == 0:
                    total[...] = term
                else:
                    total[...] += term
        if step == STEPS - 1:
            gate = gate_sum[...]
            act_ref[...] = (gate / (1.0 + jnp.exp(-gate)) * up_sum[...]).astype(BF16)
        if step >= STEPS:
            for now in range((step - STEPS) * STEP, (step - STEPS + 1) * STEP):
                result = jnp.dot(
                    act_ref[...],
                    down_ref[:, now * SLICE : (now + 1) * SLICE],
                    preferred_element_type=F32,
                ).astype(BF16)
                for shard, split in enumerate(pieces_out):
                    block = 0
                    for number, first, count in split:
                        if block <= now < block + count:
                            outs[number][first + now - block] = result[
                                shard * CAP : (shard + 1) * CAP
                            ]
                        block += count


def expert(arrays, pieces_in, sizes, pieces_out, weights):
    total = CAP * len(pieces_in)
    whole = pl.BlockSpec(memory_space=pltpu.VMEM)
    apart = pl.BlockSpec(memory_space=pl.ANY)
    return call(
        functools.partial(expert_kernel, pieces_in, pieces_out, len(arrays)),
        tuple(shape((size, CAP, SLICE)) for size in sizes),
        44,
        total * D * 2 * UNITS * 6,
        25 * 10**6,
        in_specs=[whole] * len(arrays) + [apart] * 6,
        out_specs=(whole,) * len(sizes),
        scratch_shapes=[
            pltpu.VMEM((total, D), BF16),
            pltpu.VMEM((HELD, D), BF16),
            pltpu.VMEM((HELD, D), BF16),
            pltpu.VMEM((HELD, D), BF16),
            pltpu.VMEM((total, HELD), F32),
            pltpu.VMEM((total, HELD), F32),
            pltpu.VMEM((total, HELD), BF16),
            pltpu.SemaphoreType.DMA((6, STEPS)),
        ],
    )(*arrays, *weights)


def join_kernel(plans, *refs):
    ins, outs = refs, refs[len(refs) - len(plans) :]
    for (size, terms), out in zip(plans, outs):
        for block in range(size):
            total = None
            for number, first, into, count in terms:
                if into <= block < into + count:
                    value = ins[number][first + block - into]
                    if total is None:
                        total = value
                    else:
                        total = total.astype(F32) + value.astype(F32)
            out[block] = total.astype(BF16)


def join(plans, *arrays, after=()):
    whole = pl.BlockSpec(memory_space=pltpu.VMEM)
    return call(
        functools.partial(join_kernel, plans),
        tuple(shape((size, CAP, SLICE)) for size, _ in plans),
        16,
        10**7,
        8 * 10**6,
        in_specs=[whole] * len(arrays) + [pl.BlockSpec(memory_space=pl.ANY)] * len(after),
        out_specs=(whole,) * len(plans),
    )(*arrays, *after)


def combine_kernel(hidden_ref, high_ref, low_ref, outputs_ref, mixed_ref):
    outputs = outputs_ref[...].reshape(EXPERTS * CAP, SLICE)
    moe = jnp.dot(high_ref[...], outputs, preferred_element_type=F32)
    moe += jnp.dot(low_ref[...], outputs, preferred_element_type=F32)
    mixed_ref[...] = (hidden_ref[...] + moe).astype(BF16)


def combine(hidden, high, low, outputs):
    return call(combine_kernel, shape((TOK, SLICE)), 16, 3 * 10**8, 2 * 10**6)(
        hidden, high, low, outputs
    )


def body(
    queries,
    keys,
    values,
    residual,
    ln_gain,
    out_weight,
    gate_weight,
    up_weight,
    down_weight,
    expert_ids,
    gate_scores,
):
    ctx = lax.axis_index("ctx")
    own = jnp.stack((keys, values))[None]
    near = jnp.concatenate([own, send(own, dz=1)])
    near = jnp.concatenate([near, send(near, dy=1), send(near, dy=-1), send(near, dy=2)])
    paired = jnp.concatenate([near, send(near, dc=1)])
    y, z, c = ctx // 4, (ctx // 2) % 2, ctx % 2
    starts = [
        ((((y - dy) % 4) * 2 + (z + dz) % 2) * 2 + (c + dc) % 2) * TOK
        for dc in (0, 1)
        for dy in (0, 1, -1, 2)
        for dz in (0, 1)
    ]
    starts = jnp.stack(starts + [ctx * TOK]).astype(jnp.int32)
    placing, share_high, share_low = routing(expert_ids, gate_scores)
    weights = []
    for weight in (gate_weight[0].T, up_weight[0].T, down_weight[0]):
        weights += [weight, send(weight, dc=1)]

    term = attention(starts, queries, paired, out_weight)
    terms = lax.all_to_all(term, "exp", 0, 0, tiled=True)
    hidden, outgoing = dispatch(terms, residual, ln_gain[None], placing, weights[1::2])
    arrived = lax.all_to_all(outgoing, "exp", 0, 0, tiled=True)
    mine = norm(arrived)

    back, ahead, across = send(mine, dy=1), send(mine, dy=-1), send(mine, dz=1)
    low, high, across_a, both_b = join(
        (
            (4, ((0, 0, 0, 4),)),
            (4, ((1, 4, 0, 4),)),
            (5, ((2, 0, 0, 5),)),
            (6, ((0, 5, 0, 3), (1, 5, 3, 3))),
        ),
        back,
        ahead,
        across,
    )
    far_low, far_high = send(low, dy=1), send(high, dy=-1)
    across_back, across_ahead = send(across_a, dy=1), send(across_a, dy=-1)
    across_b = send(both_b, dz=1)
    mine, across, back, ahead = expert(
        [mine, across, back, ahead],
        [[(k, 0, 8)] for k in range(4)],
        (8,) * 4,
        [[(k, 0, 8)] for k in range(4)],
        weights,
    )
    low, high, far_b = join(
        (
            (3, ((0, 0, 0, 3),)),
            (2, ((1, 3, 0, 2),)),
            (3, ((3, 1, 0, 3),)),
        ),
        across_back,
        across_ahead,
        far_low,
        far_high,
        across_b,
        after=(mine,),
    )
    across_far = [send(low, dy=1), send(high, dy=-1), send(far_b, dz=1)]
    far, across_back, across_ahead, across_b, far_low, far_high, far_b = expert(
        [far_low, far_high, across_back, across_ahead, across_b] + across_far,
        [
            [(0, 0, 4), (1, 0, 4)],
            [(2, 0, 5), (4, 0, 3)],
            [(3, 0, 5), (4, 3, 3)],
            [(5, 0, 3), (6, 0, 2), (7, 0, 3)],
        ],
        (8, 5, 5, 6, 3, 2, 3),
        [
            [(0, 0, 8)],
            [(1, 0, 5), (3, 0, 3)],
            [(2, 0, 5), (3, 3, 3)],
            [(4, 0, 3), (5, 0, 2), (6, 0, 3)],
        ],
        weights,
    )
    across_ahead, across_back, low, high = join(
        (
            (5, ((0, 0, 0, 5), (3, 0, 0, 3))),
            (5, ((1, 0, 0, 5), (4, 0, 3, 2))),
            (4, ((2, 0, 0, 4),)),
            (4, ((2, 4, 0, 4), (5, 0, 1, 3))),
        ),
        across_ahead,
        across_back,
        far,
        send(far_low, dy=1),
        send(far_high, dy=-1),
        send(far_b, dz=1),
    )
    across, ahead, back = join(
        (
            (8, ((0, 0, 0, 8), (3, 0, 0, 5), (4, 0, 0, 5))),
            (8, ((1, 0, 0, 8), (5, 0, 0, 4), (7, 3, 5, 3))),
            (8, ((2, 0, 0, 8), (6, 0, 4, 4), (7, 0, 5, 3))),
        ),
        across,
        ahead,
        back,
        send(across_ahead, dy=1),
        send(across_back, dy=-1),
        send(low, dy=1),
        send(high, dy=-1),
        send(across_b, dz=1),
    )
    (result,) = join(
        ((8, tuple((number, 0, 0, 8) for number in range(4))),),
        mine,
        send(ahead, dy=1),
        send(back, dy=-1),
        send(across, dz=1),
    )
    outputs = lax.all_to_all(result, "exp", 0, 0, tiled=True)
    return combine(hidden, share_high, share_low, outputs)


def solution(mesh):
    return jax.shard_map(
        body,
        mesh=mesh,
        in_specs=(
            P("ctx", "exp"),
            P("ctx", "exp"),
            P("ctx", "exp"),
            P("ctx", "exp"),
            P("exp"),
            P("exp", None),
            P("exp", None, "ctx"),
            P("exp", None, "ctx"),
            P("exp", "ctx", None),
            P("ctx", None),
            P("ctx", None),
        ),
        out_specs=P("ctx", "exp"),
        check_vma=False,
    )
```

```python
import functools

import jax
import jax.numpy as jnp
from jax import lax
from jax.experimental import pallas as pl
from jax.experimental.pallas import tpu as pltpu
from jax.sharding import PartitionSpec as P

D = 6144
HD = 128
EXPERTS = 8
TOPK = 4
CAP = 80
AUX = 16
TOK = 128
SLICE = 768
SHARDS = 16
UNITS = 336
EPS = 1e-05
F32 = jnp.float32
BF16 = jnp.bfloat16
MIB = 1 << 20


def place(index):
    return index // 4, (index // 2) % 2, index % 2


def route(dy, dz, dc):
    pairs = []
    for index in range(SHARDS):
        y, z, c = place(index)
        pairs.append((index, (((y + dy) % 4) * 2 + (z + dz) % 2) * 2 + (c + dc) % 2))
    return pairs


def send(block, dy=0, dz=0, dc=0):
    return lax.ppermute(block, "ctx", route(dy, dz, dc))


def call(kernel, out_shape, limit, flops, moved, **kwargs):
    return pl.pallas_call(
        kernel,
        out_shape=out_shape,
        compiler_params=pltpu.CompilerParams(vmem_limit_bytes=limit * MIB),
        cost_estimate=pl.CostEstimate(flops=flops, bytes_accessed=moved, transcendentals=0),
        **kwargs,
    )


def shape(dims, dtype=BF16):
    return jax.ShapeDtypeStruct(dims, dtype)


def pieces(value):
    high = value.astype(BF16).astype(F32)
    left = value - high
    mid = left.astype(BF16).astype(F32)
    return high, mid, left - mid


def routing_kernel(ids_ref, scores_ref, placing_ref, high_ref, low_ref):
    ids = ids_ref[...]
    scores = scores_ref[...]
    total = scores[:, 0:1] + scores[:, 1:2] + scores[:, 2:3] + scores[:, 3:4]
    lanes = lax.broadcasted_iota(jnp.int32, (TOK, TOK), 1)
    rows = lax.broadcasted_iota(jnp.int32, (TOK, TOK), 0)
    named = [(lanes == ids[:, k : k + 1]).astype(F32) for k in range(TOPK)]
    member = named[0] + named[1] + named[2] + named[3]
    lower = (lanes < rows).astype(BF16)
    slots = jnp.dot(lower, member.astype(BF16), preferred_element_type=F32)
    wide = lax.broadcasted_iota(jnp.int32, (TOK, EXPERTS * TOK), 1)
    columns = lax.broadcasted_iota(jnp.int32, (TOK, EXPERTS * CAP), 1)
    placed = jnp.zeros((TOK, EXPERTS * TOK), F32)
    shares = jnp.zeros((TOK, EXPERTS * CAP), F32)
    for k in range(TOPK):
        slot = jnp.sum(named[k] * slots, axis=1, keepdims=True).astype(jnp.int32)
        expert = ids[:, k : k + 1]
        placed = placed + (wide == expert * TOK + slot).astype(F32)
        share = scores[:, k : k + 1] / total
        shares = shares + jnp.where(columns == expert * CAP + slot, share, 0.0)
    for e in range(EXPERTS):
        placing_ref[e] = placed[:, e * TOK : (e + 1) * TOK].T.astype(BF16)
    high = shares.astype(BF16)
    high_ref[...] = high
    low_ref[...] = (shares - high.astype(F32)).astype(BF16)


def routing(expert_ids, gate_scores):
    return call(
        routing_kernel,
        (
            shape((EXPERTS, TOK, TOK)),
            shape((TOK, EXPERTS * CAP)),
            shape((TOK, EXPERTS * CAP)),
        ),
        6,
        10**7,
        10**6,
    )(expert_ids, gate_scores)


def attention_kernel(starts_ref, queries_ref, paired_ref, weight_ref, term_ref, held, ready):
    copy = pltpu.make_async_copy(weight_ref, held, ready)
    copy.start()
    keys = paired_ref[:, 0].reshape(SHARDS * TOK, HD)
    values = paired_ref[:, 1].reshape(SHARDS * TOK, HD)
    rows = lax.broadcasted_iota(jnp.int32, (TOK, TOK), 0)
    lanes = lax.broadcasted_iota(jnp.int32, (TOK, TOK), 1)
    ahead = rows - lanes + starts_ref[SHARDS]
    keep = jnp.concatenate([ahead >= starts_ref[b] for b in range(SHARDS)], axis=1)
    heads = []
    for h in range(queries_ref.shape[1] // HD):
        query = queries_ref[:, h * HD : (h + 1) * HD]
        scores = lax.dot_general(
            query, keys, (((1,), (1,)), ((), ())), preferred_element_type=F32
        ) * (HD**-0.5)
        scores = jnp.where(keep, scores, -1e30)
        top = jnp.max(scores, axis=1, keepdims=True)
        expw = jnp.exp(scores - top)
        denom = jnp.sum(expw, axis=1, keepdims=True)
        summed = jnp.dot(expw.astype(BF16), values, preferred_element_type=F32)
        heads.append((summed / denom).astype(BF16))
    attended = jnp.concatenate(heads, axis=1)
    copy.wait()
    for j in range(EXPERTS):
        term_ref[j] = jnp.dot(
            attended, held[:, j * SLICE : (j + 1) * SLICE], preferred_element_type=F32
        ).astype(BF16)


def attention(starts, queries, paired, out_weight):
    return call(
        attention_kernel,
        shape((EXPERTS, TOK, SLICE)),
        20,
        2 * 10**9,
        13 * 10**6,
        in_specs=[
            pl.BlockSpec(memory_space=pltpu.SMEM),
            pl.BlockSpec(memory_space=pltpu.VMEM),
            pl.BlockSpec(memory_space=pltpu.VMEM),
            pl.BlockSpec(memory_space=pl.ANY),
        ],
        out_specs=pl.BlockSpec(memory_space=pltpu.VMEM),
        scratch_shapes=[pltpu.VMEM((SLICE, D), BF16), pltpu.SemaphoreType.DMA],
    )(starts, queries, paired, out_weight)


def dispatch_kernel(terms_ref, residual_ref, gain_ref, placing_ref, *refs):
    hidden_ref, out_ref = refs[-2:]
    hidden = residual_ref[...].astype(F32)
    for j in range(EXPERTS):
        hidden = hidden + terms_ref[j].astype(F32)
    hidden_ref[...] = hidden
    mean = jnp.sum(hidden, axis=1, keepdims=True) * (1.0 / SLICE)
    apart = (hidden - mean).astype(BF16)
    lanes = lax.broadcasted_iota(jnp.int32, (TOK, TOK), 1)
    high, mid, low = pieces(mean)
    spread = jnp.where(lanes == 0, high, jnp.where(lanes == 1, mid, jnp.where(lanes == 2, low, 0.0)))
    means = spread.T[:AUX].astype(BF16)
    rows = lax.broadcasted_iota(jnp.int32, (AUX, SLICE), 0)
    high, mid, low = pieces(gain_ref[...])
    gains = jnp.where(rows == 3, high, jnp.where(rows == 4, mid, jnp.where(rows == 5, low, 0.0)))
    for e in range(EXPERTS):
        placing = placing_ref[e]
        out_ref[e, :CAP] = jnp.dot(placing[:CAP], apart, preferred_element_type=F32).astype(BF16)
        sent = lax.dot_general(means, placing, (((1,), (1,)), ((), ())), preferred_element_type=F32)
        out_ref[e, CAP:] = jnp.concatenate(
            [sent + gains[:, :TOK], gains[:, TOK:]], axis=1
        ).astype(BF16)


def dispatch(terms, residual, gain, placing, after):
    whole = pl.BlockSpec(memory_space=pltpu.VMEM)
    return call(
        dispatch_kernel,
        (shape((TOK, SLICE), F32), shape((EXPERTS, CAP + AUX, SLICE))),
        4,
        2 * 10**8,
        5 * 10**6,
        in_specs=[whole] * 4 + [pl.BlockSpec(memory_space=pl.ANY)] * len(after),
    )(terms, residual, gain, placing, *after)


def norm_kernel(arrived_ref, out_ref):
    rows = lax.broadcasted_iota(jnp.int32, (CAP, TOK), 0)
    lanes = lax.broadcasted_iota(jnp.int32, (CAP, TOK), 1)
    diagonal = (rows == lanes).astype(BF16)
    means = []
    total = jnp.zeros((CAP, 1), F32)
    for j in range(EXPERTS):
        turned = lax.dot_general(
            diagonal, arrived_ref[j, CAP:, :TOK], (((1,), (1,)), ((), ())), preferred_element_type=F32
        )
        means.append(turned[:, 0:1] + turned[:, 1:2] + turned[:, 2:3])
        total = total + SLICE * means[j]
        total = total + jnp.sum(arrived_ref[j, :CAP].astype(F32), axis=1, keepdims=True)
    mean = total / D
    spread = jnp.zeros((CAP, 1), F32)
    for j in range(EXPERTS):
        apart = arrived_ref[j, :CAP].astype(F32) + (means[j] - mean)
        spread = spread + jnp.sum(apart * apart, axis=1, keepdims=True)
    scale = lax.rsqrt(spread / D + EPS)
    for j in range(EXPERTS):
        aux = arrived_ref[j, CAP:].astype(F32)
        gain = aux[3:4] + aux[4:5] + aux[5:6]
        apart = arrived_ref[j, :CAP].astype(F32) + (means[j] - mean)
        out_ref[j] = (apart * scale * gain).astype(BF16)


def norm(arrived):
    return call(norm_kernel, shape((EXPERTS, CAP, SLICE)), 4, 10**7, 2 * 10**6)(arrived)


HELD = 2 * UNITS


def hold_kernel(*refs):
    weights, held, ready = refs[:6], refs[-4:-1], refs[-1]
    copies = [
        pltpu.make_async_copy(
            weights[2 * number + core],
            held[number].at[pl.ds(core * UNITS, UNITS)],
            ready.at[2 * number + core],
        )
        for number in range(3)
        for core in range(2)
    ]
    for copy in copies:
        copy.start()
    for copy in copies:
        copy.wait()


def hold(weights, after):
    apart = pl.BlockSpec(memory_space=pl.ANY)
    return call(
        hold_kernel,
        tuple(pltpu.VMEM((HELD, D), BF16) for _ in range(3)),
        1,
        10**6,
        25 * 10**6,
        in_specs=[apart] * (6 + len(after)),
        out_specs=(pl.BlockSpec(memory_space=pltpu.VMEM),) * 3,
        scratch_shapes=[pltpu.SemaphoreType.DMA((6,))],
    )(*weights, *after)


def expert_kernel(pieces_in, pieces_out, n_in, *refs):
    xs, refs = refs[:n_in], refs[n_in:]
    gate_ref, up_ref, down_ref = refs[:3]
    outs, rows_ref = refs[3:-1], refs[-1]
    for shard, split in enumerate(pieces_in):
        block = 0
        for number, first, count in split:
            for k in range(first, first + count):
                rows_ref[
                    shard * CAP : (shard + 1) * CAP, block * SLICE : (block + 1) * SLICE
                ] = xs[number][k]
                block += 1
    turned = (((1,), (1,)), ((), ()))
    rows = rows_ref[...]
    gate = lax.dot_general(rows, gate_ref[...], turned, preferred_element_type=F32)
    up = lax.dot_general(rows, up_ref[...], turned, preferred_element_type=F32)
    act = (gate / (1.0 + jnp.exp(-gate)) * up).astype(BF16)
    for now in range(EXPERTS):
        result = jnp.dot(
            act, down_ref[:, now * SLICE : (now + 1) * SLICE], preferred_element_type=F32
        ).astype(BF16)
        for shard, split in enumerate(pieces_out):
            block = 0
            for number, first, count in split:
                if block <= now < block + count:
                    outs[number][first + now - block] = result[shard * CAP : (shard + 1) * CAP]
                block += count


def expert(arrays, pieces_in, sizes, pieces_out, held):
    total = CAP * len(pieces_in)
    whole = pl.BlockSpec(memory_space=pltpu.VMEM)
    return call(
        functools.partial(expert_kernel, pieces_in, pieces_out, len(arrays)),
        tuple(shape((size, CAP, SLICE)) for size in sizes),
        10,
        total * D * 2 * UNITS * 6,
        25 * 10**6,
        in_specs=[whole] * (len(arrays) + 3),
        out_specs=(whole,) * len(sizes),
        scratch_shapes=[pltpu.VMEM((total, D), BF16)],
    )(*arrays, *held)


def join_kernel(plans, *refs):
    ins, outs = refs, refs[len(refs) - len(plans) :]
    for (size, terms), out in zip(plans, outs):
        for block in range(size):
            total = None
            for number, first, into, count in terms:
                if into <= block < into + count:
                    value = ins[number][first + block - into]
                    if total is None:
                        total = value
                    else:
                        total = total.astype(F32) + value.astype(F32)
            out[block] = total.astype(BF16)


def join(plans, *arrays, after=()):
    whole = pl.BlockSpec(memory_space=pltpu.VMEM)
    return call(
        functools.partial(join_kernel, plans),
        tuple(shape((size, CAP, SLICE)) for size, _ in plans),
        2,
        10**7,
        8 * 10**6,
        in_specs=[whole] * len(arrays) + [pl.BlockSpec(memory_space=pl.ANY)] * len(after),
        out_specs=(whole,) * len(plans),
    )(*arrays, *after)


def combine_kernel(hidden_ref, high_ref, low_ref, outputs_ref, mixed_ref):
    outputs = outputs_ref[...].reshape(EXPERTS * CAP, SLICE)
    moe = jnp.dot(high_ref[...], outputs, preferred_element_type=F32)
    moe += jnp.dot(low_ref[...], outputs, preferred_element_type=F32)
    mixed_ref[...] = (hidden_ref[...] + moe).astype(BF16)


def combine(hidden, high, low, outputs):
    return call(combine_kernel, shape((TOK, SLICE)), 4, 3 * 10**8, 2 * 10**6)(
        hidden, high, low, outputs
    )


def body(
    queries,
    keys,
    values,
    residual,
    ln_gain,
    out_weight,
    gate_weight,
    up_weight,
    down_weight,
    expert_ids,
    gate_scores,
):
    ctx = lax.axis_index("ctx")
    own = jnp.stack((keys, values))[None]
    near = jnp.concatenate([own, send(own, dz=1)])
    near = jnp.concatenate([near, send(near, dy=1), send(near, dy=-1), send(near, dy=2)])
    paired = jnp.concatenate([near, send(near, dc=1)])
    y, z, c = ctx // 4, (ctx // 2) % 2, ctx % 2
    starts = [
        ((((y - dy) % 4) * 2 + (z + dz) % 2) * 2 + (c + dc) % 2) * TOK
        for dc in (0, 1)
        for dy in (0, 1, -1, 2)
        for dz in (0, 1)
    ]
    starts = jnp.stack(starts + [ctx * TOK]).astype(jnp.int32)
    placing, share_high, share_low = routing(expert_ids, gate_scores)
    weights = []
    for weight in (gate_weight[0].T, up_weight[0].T, down_weight[0]):
        weights += [weight, send(weight, dc=1)]

    term = attention(starts, queries, paired, out_weight)
    terms = lax.all_to_all(term, "exp", 0, 0, tiled=True)
    hidden, outgoing = dispatch(terms, residual, ln_gain[None], placing, weights[1::2])
    arrived = lax.all_to_all(outgoing, "exp", 0, 0, tiled=True)
    mine = norm(arrived)

    back, ahead, across = send(mine, dy=1), send(mine, dy=-1), send(mine, dz=1)
    held = hold(weights, (mine,))
    up, down, over = join(
        (
            (9, ((0, 0, 0, 4), (2, 0, 4, 5))),
            (9, ((1, 4, 0, 4), (2, 0, 4, 5))),
            (6, ((0, 5, 0, 3), (1, 5, 3, 3))),
        ),
        back,
        ahead,
        across,
        after=(held[0],),
    )
    low, high, both = send(up, dy=1), send(down, dy=-1), send(over, dz=1)
    mine, across, back, ahead = expert(
        [mine, across, back, ahead],
        [[(k, 0, 8)] for k in range(4)],
        (8,) * 4,
        [[(k, 0, 8)] for k in range(4)],
        held,
    )
    up, down, over = join(
        (
            (3, ((0, 4, 0, 3),)),
            (2, ((1, 7, 0, 2),)),
            (3, ((1, 1, 0, 3),)),
        ),
        low,
        high,
        both,
        after=(mine,),
    )
    across_far = [send(up, dy=1), send(down, dy=-1), send(over, dz=1)]
    far, across_back, across_ahead, over = expert(
        [low, high, both],
        [
            [(0, 0, 4), (1, 0, 4)],
            [(0, 4, 5), (2, 0, 3)],
            [(1, 4, 5), (2, 3, 3)],
        ],
        (8, 5, 5, 6),
        [
            [(0, 0, 8)],
            [(1, 0, 5), (3, 0, 3)],
            [(2, 0, 5), (3, 3, 3)],
        ],
        held,
    )
    far_low, far_high, far_over = expert(
        across_far,
        [[(0, 0, 3), (1, 0, 2), (2, 0, 3)]],
        (3, 2, 3),
        [[(0, 0, 3), (1, 0, 2), (2, 0, 3)]],
        held,
    )
    up, down = join(
        (
            (9, ((2, 0, 0, 4), (0, 0, 4, 5), (3, 0, 4, 3))),
            (9, ((2, 4, 0, 4), (5, 0, 1, 3), (1, 0, 4, 5), (4, 0, 7, 2))),
        ),
        across_ahead,
        across_back,
        far,
        send(far_low, dy=1),
        send(far_high, dy=-1),
        send(far_over, dz=1),
    )
    across, ahead, back = join(
        (
            (8, ((0, 0, 0, 8), (3, 4, 0, 5), (4, 4, 0, 5))),
            (8, ((1, 0, 0, 8), (3, 0, 0, 4), (5, 3, 5, 3))),
            (8, ((2, 0, 0, 8), (4, 0, 4, 4), (5, 0, 5, 3))),
        ),
        across,
        ahead,
        back,
        send(up, dy=1),
        send(down, dy=-1),
        send(over, dz=1),
    )
    (result,) = join(
        ((8, tuple((number, 0, 0, 8) for number in range(4))),),
        mine,
        send(ahead, dy=1),
        send(back, dy=-1),
        send(across, dz=1),
    )
    outputs = lax.all_to_all(result, "exp", 0, 0, tiled=True)
    return combine(hidden, share_high, share_low, outputs)


def solution(mesh):
    return jax.shard_map(
        body,
        mesh=mesh,
        in_specs=(
            P("ctx", "exp"),
            P("ctx", "exp"),
            P("ctx", "exp"),
            P("ctx", "exp"),
            P("exp"),
            P("exp", None),
            P("exp", None, "ctx"),
            P("exp", None, "ctx"),
            P("exp", "ctx", None),
            P("ctx", None),
            P("ctx", None),
        ),
        out_specs=P("ctx", "exp"),
        check_vma=False,
    )
```

```python
import functools

import jax
import jax.numpy as jnp
from jax import lax
from jax.experimental import pallas as pl
from jax.experimental.pallas import tpu as pltpu
from jax.sharding import PartitionSpec as P

D = 6144
HD = 128
EXPERTS = 8
TOPK = 4
CAP = 80
AUX = 16
TOK = 128
SLICE = 768
SHARDS = 16
NEAR = 8
META = 16
UNITS = 336
CUT = 512
TAIL = SLICE - CUT
DEPTH = 384
EPS = 1e-05
F32 = jnp.float32
BF16 = jnp.bfloat16
MIB = 1 << 20


def place(index):
    return index // 4, (index // 2) % 2, index % 2


def route(dy, dz, dc):
    pairs = []
    for index in range(SHARDS):
        y, z, c = place(index)
        pairs.append((index, (((y + dy) % 4) * 2 + (z + dz) % 2) * 2 + (c + dc) % 2))
    return pairs


def send(block, dy=0, dz=0, dc=0):
    return lax.ppermute(block, "ctx", route(dy, dz, dc))


def turn(block, dx=0, dz=0):
    pairs = [(j, (j // 4 + dz) % 2 * 4 + (j + dx) % 4) for j in range(EXPERTS)]
    return lax.ppermute(block, "exp", pairs)


def call(kernel, out_shape, limit, flops, moved, **kwargs):
    return pl.pallas_call(
        kernel,
        out_shape=out_shape,
        compiler_params=pltpu.CompilerParams(vmem_limit_bytes=limit * MIB),
        cost_estimate=pl.CostEstimate(flops=flops, bytes_accessed=moved, transcendentals=0),
        **kwargs,
    )


def shape(dims, dtype=BF16):
    return jax.ShapeDtypeStruct(dims, dtype)


def pieces(value):
    high = value.astype(BF16).astype(F32)
    left = value - high
    mid = left.astype(BF16).astype(F32)
    return high, mid, left - mid


def routing_kernel(ids_ref, scores_ref, placing_ref, high_ref, low_ref):
    ids = ids_ref[...]
    scores = scores_ref[...]
    total = scores[:, 0:1] + scores[:, 1:2] + scores[:, 2:3] + scores[:, 3:4]
    lanes = lax.broadcasted_iota(jnp.int32, (TOK, TOK), 1)
    rows = lax.broadcasted_iota(jnp.int32, (TOK, TOK), 0)
    named = [(lanes == ids[:, k : k + 1]).astype(F32) for k in range(TOPK)]
    member = named[0] + named[1] + named[2] + named[3]
    lower = (lanes < rows).astype(BF16)
    slots = jnp.dot(lower, member.astype(BF16), preferred_element_type=F32)
    wide = lax.broadcasted_iota(jnp.int32, (TOK, EXPERTS * TOK), 1)
    columns = lax.broadcasted_iota(jnp.int32, (TOK, EXPERTS * CAP), 1)
    placed = jnp.zeros((TOK, EXPERTS * TOK), F32)
    shares = jnp.zeros((TOK, EXPERTS * CAP), F32)
    for k in range(TOPK):
        slot = jnp.sum(named[k] * slots, axis=1, keepdims=True).astype(jnp.int32)
        expert = ids[:, k : k + 1]
        placed = placed + (wide == expert * TOK + slot).astype(F32)
        share = scores[:, k : k + 1] / total
        shares = shares + jnp.where(columns == expert * CAP + slot, share, 0.0)
    for e in range(EXPERTS):
        placing_ref[e] = placed[:, e * TOK : (e + 1) * TOK].T.astype(BF16)
    high = shares.astype(BF16)
    high_ref[...] = high
    low_ref[...] = (shares - high.astype(F32)).astype(BF16)


def routing(expert_ids, gate_scores):
    return call(
        routing_kernel,
        (
            shape((EXPERTS, TOK, TOK)),
            shape((TOK, EXPERTS * CAP)),
            shape((TOK, EXPERTS * CAP)),
        ),
        6,
        10**7,
        10**6,
    )(expert_ids, gate_scores)


def shares_kernel(spot_ref, paired_ref, shares_ref):
    eights = lax.broadcasted_iota(jnp.int32, (EXPERTS, TOK), 0)
    slots = lax.broadcasted_iota(jnp.int32, (CAP, TOK), 0).astype(F32)
    rows = lax.broadcasted_iota(jnp.int32, (TOK, TOK), 0)
    lanes = lax.broadcasted_iota(jnp.int32, (TOK, TOK), 1)
    upper = (rows < lanes).astype(BF16)
    for shard in range(NEAR):
        meta = paired_ref[shard, 2 * TOK :].astype(F32)
        scores = meta[4:8] + meta[8:12] + meta[12:16]
        total = scores[0:1] + scores[1:2] + scores[2:3] + scores[3:4]
        member = jnp.zeros((EXPERTS, TOK), F32)
        share = jnp.zeros((EXPERTS, TOK), F32)
        for k in range(TOPK):
            named = (meta[k : k + 1].astype(jnp.int32) == eights).astype(F32)
            member = member + named
            share = share + named * (scores[k : k + 1] / total)
        taken = jnp.dot(member.astype(BF16), upper, preferred_element_type=F32)
        taken = jnp.where(member > 0.5, taken, -1.0)
        parts = []
        for back in range(4):
            mine = eights == spot_ref[1] * 4 + lax.rem(spot_ref[0] - back + 4, 4)
            slot = jnp.sum(jnp.where(mine, taken, 0.0), axis=0, keepdims=True)
            part = jnp.sum(jnp.where(mine, share, 0.0), axis=0, keepdims=True)
            parts.append(jnp.where(slots == slot, part, 0.0))
        parts.append(jnp.zeros((DEPTH - 4 * CAP, TOK), F32))
        shares_ref[shard] = jnp.concatenate(parts, axis=0).T.astype(BF16)


def shares_of(spot, paired):
    return call(
        shares_kernel,
        shape((NEAR, TOK, DEPTH)),
        6,
        10**7,
        2 * 10**6,
        in_specs=[
            pl.BlockSpec(memory_space=pltpu.SMEM),
            pl.BlockSpec(memory_space=pltpu.VMEM),
        ],
    )(spot, paired)


def attention_kernel(starts_ref, queries_ref, paired_ref, weight_ref, term_ref, held, ready):
    copies = []
    for j in range(EXPERTS):
        columns = pl.ds(j * SLICE, SLICE)
        copies.append(
            pltpu.make_async_copy(weight_ref.at[:, columns], held.at[:, columns], ready.at[j])
        )
        copies[j].start()
    keys = paired_ref[:, :TOK].reshape(SHARDS * TOK, HD)
    values = paired_ref[:, TOK : 2 * TOK].reshape(SHARDS * TOK, HD)
    rows = lax.broadcasted_iota(jnp.int32, (TOK, TOK), 0)
    lanes = lax.broadcasted_iota(jnp.int32, (TOK, TOK), 1)
    ahead = rows - lanes + starts_ref[SHARDS]
    keep = jnp.concatenate([ahead >= starts_ref[b] for b in range(SHARDS)], axis=1)
    heads = []
    for h in range(queries_ref.shape[1] // HD):
        query = queries_ref[:, h * HD : (h + 1) * HD]
        scores = lax.dot_general(
            query, keys, (((1,), (1,)), ((), ())), preferred_element_type=F32
        ) * (HD**-0.5)
        scores = jnp.where(keep, scores, -1e30)
        top = jnp.max(scores, axis=1, keepdims=True)
        expw = jnp.exp(scores - top)
        denom = jnp.sum(expw, axis=1, keepdims=True)
        summed = jnp.dot(expw.astype(BF16), values, preferred_element_type=F32)
        heads.append((summed / denom).astype(BF16))
    attended = jnp.concatenate(heads, axis=1)
    for j in range(EXPERTS):
        copies[j].wait()
        term_ref[j] = jnp.dot(
            attended, held[:, j * SLICE : (j + 1) * SLICE], preferred_element_type=F32
        ).astype(BF16)


def attention(starts, queries, paired, out_weight):
    return call(
        attention_kernel,
        shape((EXPERTS, TOK, SLICE)),
        48,
        2 * 10**9,
        13 * 10**6,
        in_specs=[
            pl.BlockSpec(memory_space=pltpu.SMEM),
            pl.BlockSpec(memory_space=pltpu.VMEM),
            pl.BlockSpec(memory_space=pltpu.VMEM),
            pl.BlockSpec(memory_space=pl.ANY),
        ],
        out_specs=pl.BlockSpec(memory_space=pltpu.VMEM),
        scratch_shapes=[pltpu.VMEM((SLICE, D), BF16), pltpu.SemaphoreType.DMA((EXPERTS,))],
    )(starts, queries, paired, out_weight)


def dispatch_kernel(terms_ref, residual_ref, gain_ref, placing_ref, hidden_ref, out_ref):
    hidden = residual_ref[...].astype(F32)
    for j in range(EXPERTS):
        hidden = hidden + terms_ref[j].astype(F32)
    hidden_ref[...] = hidden
    mean = jnp.sum(hidden, axis=1, keepdims=True) * (1.0 / SLICE)
    apart = (hidden - mean).astype(BF16)
    lanes = lax.broadcasted_iota(jnp.int32, (TOK, TOK), 1)
    high, mid, low = pieces(mean)
    spread = jnp.where(lanes == 0, high, jnp.where(lanes == 1, mid, jnp.where(lanes == 2, low, 0.0)))
    means = spread.T[:AUX].astype(BF16)
    rows = lax.broadcasted_iota(jnp.int32, (AUX, SLICE), 0)
    high, mid, low = pieces(gain_ref[...])
    gains = jnp.where(rows == 3, high, jnp.where(rows == 4, mid, jnp.where(rows == 5, low, 0.0)))
    for e in range(EXPERTS):
        placing = placing_ref[e]
        out_ref[e, :CAP] = jnp.dot(placing[:CAP], apart, preferred_element_type=F32).astype(BF16)
        sent = lax.dot_general(means, placing, (((1,), (1,)), ((), ())), preferred_element_type=F32)
        out_ref[e, CAP:] = jnp.concatenate(
            [sent + gains[:, :TOK], gains[:, TOK:]], axis=1
        ).astype(BF16)


def dispatch(terms, residual, gain, placing):
    return call(
        dispatch_kernel,
        (shape((TOK, SLICE), F32), shape((EXPERTS, CAP + AUX, SLICE))),
        4,
        2 * 10**8,
        5 * 10**6,
    )(terms, residual, gain, placing)


def norm_kernel(arrived_ref, *refs):
    out_ref = refs[-1]
    rows = lax.broadcasted_iota(jnp.int32, (CAP, TOK), 0)
    lanes = lax.broadcasted_iota(jnp.int32, (CAP, TOK), 1)
    diagonal = (rows == lanes).astype(BF16)
    means = []
    total = jnp.zeros((CAP, 1), F32)
    for j in range(EXPERTS):
        turned = lax.dot_general(
            diagonal, arrived_ref[j, CAP:, :TOK], (((1,), (1,)), ((), ())), preferred_element_type=F32
        )
        means.append(turned[:, 0:1] + turned[:, 1:2] + turned[:, 2:3])
        total = total + SLICE * means[j]
        total = total + jnp.sum(arrived_ref[j, :CAP].astype(F32), axis=1, keepdims=True)
    mean = total / D
    spread = jnp.zeros((CAP, 1), F32)
    for j in range(EXPERTS):
        apart = arrived_ref[j, :CAP].astype(F32) + (means[j] - mean)
        spread = spread + jnp.sum(apart * apart, axis=1, keepdims=True)
    scale = lax.rsqrt(spread / D + EPS)
    for j in range(EXPERTS):
        aux = arrived_ref[j, CAP:].astype(F32)
        gain = aux[3:4] + aux[4:5] + aux[5:6]
        apart = arrived_ref[j, :CAP].astype(F32) + (means[j] - mean)
        out_ref[j] = (apart * scale * gain).astype(BF16)


def norm(arrived, after):
    return call(
        norm_kernel,
        shape((EXPERTS, CAP, SLICE)),
        4,
        10**7,
        2 * 10**6,
        in_specs=[pl.BlockSpec(memory_space=pltpu.VMEM)]
        + [pl.BlockSpec(memory_space=pl.ANY)] * len(after),
    )(arrived, *after)


HELD = 2 * UNITS


def hold_kernel(*refs):
    weights, held, ready = refs[:6], refs[-4:-1], refs[-1]
    copies = [
        pltpu.make_async_copy(
            weights[2 * number + core],
            held[number].at[pl.ds(core * UNITS, UNITS)],
            ready.at[2 * number + core],
        )
        for number in range(3)
        for core in range(2)
    ]
    for copy in copies:
        copy.start()
    for copy in copies:
        copy.wait()


def hold(weights, after):
    apart = pl.BlockSpec(memory_space=pl.ANY)
    return call(
        hold_kernel,
        tuple(pltpu.VMEM((HELD, D), BF16) for _ in range(3)),
        1,
        10**6,
        25 * 10**6,
        in_specs=[apart] * (6 + len(after)),
        out_specs=(pl.BlockSpec(memory_space=pltpu.VMEM),) * 3,
        scratch_shapes=[pltpu.SemaphoreType.DMA((6,))],
    )(*weights, *after)


def expert_kernel(pieces_in, pieces_out, n_in, n_out, spot_ref, *refs):
    xs, refs = refs[:n_in], refs[n_in:]
    gate_ref, up_ref, down_ref = refs[:3]
    refs = refs[len(refs) - n_out - 5 :]
    outs, tails, rows_ref = refs[:n_out], refs[n_out:-1], refs[-1]
    for shard, split in enumerate(pieces_in):
        block = 0
        for number, first, count in split:
            for k in range(first, first + count):
                rows_ref[
                    shard * CAP : (shard + 1) * CAP, block * SLICE : (block + 1) * SLICE
                ] = xs[number][k]
                block += 1
    turned = (((1,), (1,)), ((), ()))
    rows = rows_ref[...]
    gate = lax.dot_general(rows, gate_ref[...], turned, preferred_element_type=F32)
    up = lax.dot_general(rows, up_ref[...], turned, preferred_element_type=F32)
    act = (gate / (1.0 + jnp.exp(-gate)) * up).astype(BF16)
    for dx in range(4):
        for z in range(2):
            first = (z * 4 + lax.rem(spot_ref[0] + dx, 4)) * SLICE + CUT
            result = jnp.dot(
                act, down_ref[:, pl.ds(pl.multiple_of(first, 128), TAIL)], preferred_element_type=F32
            ).astype(BF16)
            for shard in range(len(pieces_in)):
                tails[dx][shard, z] = result[shard * CAP : (shard + 1) * CAP]
    for now in range(EXPERTS):
        result = jnp.dot(
            act, down_ref[:, now * SLICE : now * SLICE + CUT], preferred_element_type=F32
        ).astype(BF16)
        for shard, split in enumerate(pieces_out):
            block = 0
            for number, first, count in split:
                if block <= now < block + count:
                    outs[number][first + now - block] = result[shard * CAP : (shard + 1) * CAP]
                block += count


def expert(spot, arrays, pieces_in, sizes, pieces_out, held, after=()):
    total = CAP * len(pieces_in)
    whole = pl.BlockSpec(memory_space=pltpu.VMEM)
    outs = call(
        functools.partial(expert_kernel, pieces_in, pieces_out, len(arrays), len(sizes)),
        tuple(shape((size, CAP, CUT)) for size in sizes)
        + (shape((len(pieces_in), 2, CAP, TAIL)),) * 4,
        10,
        total * D * 2 * UNITS * 6,
        25 * 10**6,
        in_specs=[pl.BlockSpec(memory_space=pltpu.SMEM)]
        + [whole] * (len(arrays) + 3)
        + [pl.BlockSpec(memory_space=pl.ANY)] * len(after),
        out_specs=(whole,) * (len(sizes) + 4),
        scratch_shapes=[pltpu.VMEM((total, D), BF16)],
    )(spot, *arrays, *held, *after)
    return outs[:-4], outs[-4:]


def blend_kernel(shards, spot_ref, shares_ref, *refs):
    tails, (own_ref, other_ref, rows_ref) = refs[:4], refs[-3:]
    rows_ref[4 * CAP :] = jnp.zeros((DEPTH - 4 * CAP, TAIL), BF16)
    for number, shard in enumerate(shards):
        for other in range(2):
            z = spot_ref[1] if other == 0 else 1 - spot_ref[1]
            for dx in range(4):
                rows_ref[dx * CAP : (dx + 1) * CAP] = tails[dx][number, z]
            total = jnp.dot(shares_ref[shard], rows_ref[...], preferred_element_type=F32)
            if other == 0:
                own_ref[number] = total
            else:
                other_ref[number] = total.astype(BF16)


def blend(spot, shares, shards, tails, after=()):
    tails = [tails[0]] + [turn(tails[dx], dx=dx) for dx in range(1, 4)]
    whole = pl.BlockSpec(memory_space=pltpu.VMEM)
    own, other = call(
        functools.partial(blend_kernel, shards),
        (shape((len(shards), TOK, TAIL), F32), shape((len(shards), TOK, TAIL))),
        6,
        len(shards) * 10**8,
        10**6,
        in_specs=[pl.BlockSpec(memory_space=pltpu.SMEM)]
        + [whole] * 5
        + [pl.BlockSpec(memory_space=pl.ANY)] * len(after),
        scratch_shapes=[pltpu.VMEM((DEPTH, TAIL), BF16)],
    )(spot, shares, *tails, *after)
    return own, turn(other, dz=1)


def sums_kernel(plans, *refs):
    outs = refs[len(refs) - len(plans) :]
    for terms, out in zip(plans, outs):
        for block, term in enumerate(terms):
            total = refs[term[0][0]][term[0][1]].astype(F32)
            for number, index in term[1:]:
                total = total + refs[number][index].astype(F32)
            out[block] = total.astype(out.dtype)


def sums(plans, dtypes, *arrays):
    whole = pl.BlockSpec(memory_space=pltpu.VMEM)
    return call(
        functools.partial(sums_kernel, plans),
        tuple(shape((len(plan), TOK, TAIL), dtype) for plan, dtype in zip(plans, dtypes)),
        4,
        10**6,
        10**6,
        in_specs=[whole] * len(arrays),
    )(*arrays)


def join_kernel(plans, *refs):
    ins, outs = refs, refs[len(refs) - len(plans) :]
    for (size, terms), out in zip(plans, outs):
        for block in range(size):
            total = None
            for number, first, into, count in terms:
                if into <= block < into + count:
                    value = ins[number][first + block - into]
                    if total is None:
                        total = value
                    else:
                        total = total.astype(F32) + value.astype(F32)
            out[block] = total.astype(BF16)


def join(plans, *arrays, after=()):
    whole = pl.BlockSpec(memory_space=pltpu.VMEM)
    return call(
        functools.partial(join_kernel, plans),
        tuple(shape((size, CAP, arrays[0].shape[2])) for size, _ in plans),
        2,
        10**7,
        8 * 10**6,
        in_specs=[whole] * len(arrays) + [pl.BlockSpec(memory_space=pl.ANY)] * len(after),
        out_specs=(whole,) * len(plans),
    )(*arrays, *after)


def combine_kernel(hidden_ref, high_ref, low_ref, outputs_ref, *refs):
    tails, mixed_ref = refs[:-1], refs[-1]
    outputs = outputs_ref[...].reshape(EXPERTS * CAP, CUT)
    moe = jnp.dot(high_ref[...], outputs, preferred_element_type=F32)
    moe += jnp.dot(low_ref[...], outputs, preferred_element_type=F32)
    mixed_ref[:, :CUT] = (hidden_ref[:, :CUT] + moe).astype(BF16)
    total = hidden_ref[:, CUT:]
    for tail in tails:
        total = total + tail[0].astype(F32)
    mixed_ref[:, CUT:] = total.astype(BF16)


def combine(hidden, high, low, outputs, tails):
    return call(combine_kernel, shape((TOK, SLICE)), 4, 3 * 10**8, 2 * 10**6)(
        hidden, high, low, outputs, *tails
    )


def body(
    queries,
    keys,
    values,
    residual,
    ln_gain,
    out_weight,
    gate_weight,
    up_weight,
    down_weight,
    expert_ids,
    gate_scores,
):
    ctx = lax.axis_index("ctx")
    scores = jnp.concatenate(pieces(gate_scores.T))
    meta = jnp.concatenate([expert_ids.T.astype(F32), scores]).astype(BF16)
    own = jnp.concatenate([keys, values, meta])[None]
    near = jnp.concatenate([own, send(own, dz=1)])
    near = jnp.concatenate([near, send(near, dy=1), send(near, dy=-1), send(near, dy=2)])
    paired = jnp.concatenate([near, send(near, dc=1)])
    y, z, c = ctx // 4, (ctx // 2) % 2, ctx % 2
    starts = [
        ((((y - dy) % 4) * 2 + (z + dz) % 2) * 2 + (c + dc) % 2) * TOK
        for dc in (0, 1)
        for dy in (0, 1, -1, 2)
        for dz in (0, 1)
    ]
    starts = jnp.stack(starts + [ctx * TOK]).astype(jnp.int32)
    placing, share_high, share_low = routing(expert_ids, gate_scores)
    exp = lax.axis_index("exp")
    spot = jnp.stack([exp % 4, exp // 4]).astype(jnp.int32)
    shares = shares_of(spot, paired)
    weights = []
    for weight in (gate_weight[0].T, up_weight[0].T, down_weight[0]):
        weights += [weight, send(weight, dc=1)]

    term = attention(starts, queries, paired, out_weight)
    terms = lax.all_to_all(term, "exp", 0, 0, tiled=True)
    hidden, outgoing = dispatch(terms, residual, ln_gain[None], placing)
    arrived = lax.all_to_all(outgoing, "exp", 0, 0, tiled=True)
    mine = norm(arrived, weights[1::2])

    back, ahead, across = send(mine, dy=1), send(mine, dy=-1), send(mine, dz=1)
    held = hold(weights, (mine,))
    up, down, over = join(
        (
            (9, ((0, 0, 0, 4), (2, 0, 4, 5))),
            (9, ((1, 4, 0, 4), (2, 0, 4, 5))),
            (6, ((0, 5, 0, 3), (1, 5, 3, 3))),
        ),
        back,
        ahead,
        across,
        after=(held[0],),
    )
    low, high, both = send(up, dy=1), send(down, dy=-1), send(over, dz=1)
    (mine, across, back, ahead), tails = expert(
        spot,
        [mine, across, back, ahead],
        [[(k, 0, 8)] for k in range(4)],
        (8,) * 4,
        [[(k, 0, 8)] for k in range(4)],
        held,
    )
    first_own, first_other = blend(spot, shares, (0, 1, 2, 4), tails)
    up, down, over = join(
        (
            (3, ((0, 4, 0, 3),)),
            (2, ((1, 7, 0, 2),)),
            (3, ((1, 1, 0, 3),)),
        ),
        low,
        high,
        both,
        after=(mine,),
    )
    across_far = [send(up, dy=1), send(down, dy=-1), send(over, dz=1)]
    (far, across_back, across_ahead, over), tails = expert(
        spot,
        [low, high, both],
        [
            [(0, 0, 4), (1, 0, 4)],
            [(0, 4, 5), (2, 0, 3)],
            [(1, 4, 5), (2, 3, 3)],
        ],
        (8, 5, 5, 6),
        [
            [(0, 0, 8)],
            [(1, 0, 5), (3, 0, 3)],
            [(2, 0, 5), (3, 3, 3)],
        ],
        held,
    )
    second_own, second_other = blend(spot, shares, (6, 3, 5), tails)
    (far_low, far_high, far_over), tails = expert(
        spot,
        across_far,
        [[(0, 0, 3), (1, 0, 2), (2, 0, 3)]],
        (3, 2, 3),
        [[(0, 0, 3), (1, 0, 2), (2, 0, 3)]],
        held,
        (far, first_own),
    )
    third_own, third_other = blend(spot, shares, (7,), tails)
    up, down = join(
        (
            (9, ((2, 0, 0, 4), (0, 0, 4, 5), (3, 0, 4, 3))),
            (9, ((2, 4, 0, 4), (5, 0, 1, 3), (1, 0, 4, 5), (4, 0, 7, 2))),
        ),
        across_ahead,
        across_back,
        far,
        send(far_low, dy=1),
        send(far_high, dy=-1),
        send(far_over, dz=1),
        after=(second_own, first_other),
    )
    own_plane = tuple(((k, n), (k + 1, n)) for k, n in ((0, 0), (0, 2), (0, 3), (2, 0)))
    other_plane = tuple(((k, n), (k + 1, n)) for k, n in ((0, 1), (2, 1), (2, 2), (4, 0)))
    here, there = sums(
        (own_plane, other_plane),
        (F32, BF16),
        first_own,
        first_other,
        second_own,
        second_other,
        third_own,
        third_other,
    )
    across, ahead, back = join(
        (
            (8, ((0, 0, 0, 8), (3, 4, 0, 5), (4, 4, 0, 5))),
            (8, ((1, 0, 0, 8), (3, 0, 0, 4), (5, 3, 5, 3))),
            (8, ((2, 0, 0, 8), (4, 0, 4, 4), (5, 0, 5, 3))),
        ),
        across,
        ahead,
        back,
        send(up, dy=1),
        send(down, dy=-1),
        send(over, dz=1),
        after=(there,),
    )
    there = send(there, dz=1)
    tail, tail_back, tail_ahead, tail_far = sums(
        tuple((((0, k), (1, k)),) for k in range(4)), (F32, BF16, BF16, BF16), here, there
    )
    tails = [tail, send(tail_back, dy=-1), send(tail_ahead, dy=1), send(tail_far, dy=2)]
    (result,) = join(
        ((8, tuple((number, 0, 0, 8) for number in range(4))),),
        mine,
        send(ahead, dy=1),
        send(back, dy=-1),
        send(across, dz=1),
    )
    outputs = lax.all_to_all(result, "exp", 0, 0, tiled=True)
    return combine(hidden, share_high, share_low, outputs, tails)


def solution(mesh):
    return jax.shard_map(
        body,
        mesh=mesh,
        in_specs=(
            P("ctx", "exp"),
            P("ctx", "exp"),
            P("ctx", "exp"),
            P("ctx", "exp"),
            P("exp"),
            P("exp", None),
            P("exp", None, "ctx"),
            P("exp", None, "ctx"),
            P("exp", "ctx", None),
            P("ctx", None),
            P("ctx", None),
        ),
        out_specs=P("ctx", "exp"),
        check_vma=False,
    )
```

```python
import functools

import jax
import jax.numpy as jnp
from jax import lax
from jax.experimental import pallas as pl
from jax.experimental.pallas import tpu as pltpu
from jax.sharding import PartitionSpec as P

D = 6144
HD = 128
EXPERTS = 8
TOPK = 4
CAP = 80
AUX = 16
TOK = 128
SLICE = 768
SHARDS = 16
UNITS = 336
EPS = 1e-05
F32 = jnp.float32
BF16 = jnp.bfloat16
MIB = 1 << 20


def place(index):
    return index // 4, (index // 2) % 2, index % 2


def route(dy, dz, dc):
    pairs = []
    for index in range(SHARDS):
        y, z, c = place(index)
        pairs.append((index, (((y + dy) % 4) * 2 + (z + dz) % 2) * 2 + (c + dc) % 2))
    return pairs


def send(block, dy=0, dz=0, dc=0):
    return lax.ppermute(block, "ctx", route(dy, dz, dc))


def call(kernel, out_shape, limit, flops, moved, **kwargs):
    return pl.pallas_call(
        kernel,
        out_shape=out_shape,
        compiler_params=pltpu.CompilerParams(vmem_limit_bytes=limit * MIB),
        cost_estimate=pl.CostEstimate(flops=flops, bytes_accessed=moved, transcendentals=0),
        **kwargs,
    )


def shape(dims, dtype=BF16):
    return jax.ShapeDtypeStruct(dims, dtype)


def pieces(value):
    high = value.astype(BF16).astype(F32)
    left = value - high
    mid = left.astype(BF16).astype(F32)
    return high, mid, left - mid


def routing_kernel(ids_ref, scores_ref, placing_ref, high_ref, low_ref):
    ids = ids_ref[...]
    scores = scores_ref[...]
    total = scores[:, 0:1] + scores[:, 1:2] + scores[:, 2:3] + scores[:, 3:4]
    lanes = lax.broadcasted_iota(jnp.int32, (TOK, TOK), 1)
    rows = lax.broadcasted_iota(jnp.int32, (TOK, TOK), 0)
    named = [(lanes == ids[:, k : k + 1]).astype(F32) for k in range(TOPK)]
    member = named[0] + named[1] + named[2] + named[3]
    lower = (lanes < rows).astype(BF16)
    slots = jnp.dot(lower, member.astype(BF16), preferred_element_type=F32)
    wide = lax.broadcasted_iota(jnp.int32, (TOK, EXPERTS * TOK), 1)
    columns = lax.broadcasted_iota(jnp.int32, (TOK, EXPERTS * CAP), 1)
    placed = jnp.zeros((TOK, EXPERTS * TOK), F32)
    shares = jnp.zeros((TOK, EXPERTS * CAP), F32)
    for k in range(TOPK):
        slot = jnp.sum(named[k] * slots, axis=1, keepdims=True).astype(jnp.int32)
        expert = ids[:, k : k + 1]
        placed = placed + (wide == expert * TOK + slot).astype(F32)
        share = scores[:, k : k + 1] / total
        shares = shares + jnp.where(columns == expert * CAP + slot, share, 0.0)
    for e in range(EXPERTS):
        placing_ref[e] = placed[:, e * TOK : (e + 1) * TOK].T.astype(BF16)
    high = shares.astype(BF16)
    high_ref[...] = high
    low_ref[...] = (shares - high.astype(F32)).astype(BF16)


def routing(expert_ids, gate_scores):
    return call(
        routing_kernel,
        (
            shape((EXPERTS, TOK, TOK)),
            shape((TOK, EXPERTS * CAP)),
            shape((TOK, EXPERTS * CAP)),
        ),
        6,
        10**7,
        10**6,
    )(expert_ids, gate_scores)


def attention_kernel(starts_ref, queries_ref, paired_ref, weight_ref, *refs):
    term_ref, held, scores_ref, expw_ref, ready = refs[-5:]
    copies = []
    for j in range(EXPERTS):
        columns = pl.ds(j * SLICE, SLICE)
        copies.append(
            pltpu.make_async_copy(weight_ref.at[:, columns], held.at[:, columns], ready.at[j])
        )
        copies[j].start()
    keys = paired_ref[:, 0].reshape(SHARDS * TOK, HD)
    values = paired_ref[:, 1].reshape(SHARDS * TOK, HD)
    rows = lax.broadcasted_iota(jnp.int32, (TOK, TOK), 0)
    lanes = lax.broadcasted_iota(jnp.int32, (TOK, TOK), 1)
    ahead = rows - lanes + starts_ref[SHARDS]
    keep = jnp.concatenate([ahead >= starts_ref[b] for b in range(SHARDS)], axis=1)
    count = queries_ref.shape[1] // HD
    stacked = jnp.concatenate(
        [queries_ref[:, h * HD : (h + 1) * HD] for h in range(count)], axis=0
    )
    scores_ref[...] = lax.dot_general(
        stacked, keys, (((1,), (1,)), ((), ())), preferred_element_type=F32
    )
    denoms = []
    for h in range(count):
        part = slice(h * TOK, (h + 1) * TOK)
        scores = jnp.where(keep, scores_ref[part] * (HD**-0.5), -1e30)
        expw = jnp.exp(scores - jnp.max(scores, axis=1, keepdims=True))
        denoms.append(jnp.sum(expw, axis=1, keepdims=True))
        expw_ref[part] = expw.astype(BF16)
    summed = jnp.dot(expw_ref[...], values, preferred_element_type=F32)
    attended = jnp.concatenate(
        [(summed[h * TOK : (h + 1) * TOK] / denoms[h]).astype(BF16) for h in range(count)], axis=1
    )
    for j in range(EXPERTS):
        copies[j].wait()
        term_ref[j] = jnp.dot(
            attended, held[:, j * SLICE : (j + 1) * SLICE], preferred_element_type=F32
        ).astype(BF16)


def attention(starts, queries, paired, out_weight):
    return call(
        attention_kernel,
        shape((EXPERTS, TOK, SLICE)),
        48,
        2 * 10**9,
        13 * 10**6,
        in_specs=[
            pl.BlockSpec(memory_space=pltpu.SMEM),
            pl.BlockSpec(memory_space=pltpu.VMEM),
            pl.BlockSpec(memory_space=pltpu.VMEM),
            pl.BlockSpec(memory_space=pl.ANY),
        ],
        out_specs=pl.BlockSpec(memory_space=pltpu.VMEM),
        scratch_shapes=[
            pltpu.VMEM((SLICE, D), BF16),
            pltpu.VMEM((SLICE, SHARDS * TOK), F32),
            pltpu.VMEM((SLICE, SHARDS * TOK), BF16),
            pltpu.SemaphoreType.DMA((EXPERTS,)),
        ],
    )(starts, queries, paired, out_weight)


def dispatch_kernel(terms_ref, residual_ref, gain_ref, placing_ref, hidden_ref, out_ref):
    hidden = residual_ref[...].astype(F32)
    for j in range(EXPERTS):
        hidden = hidden + terms_ref[j].astype(F32)
    hidden_ref[...] = hidden
    mean = jnp.sum(hidden, axis=1, keepdims=True) * (1.0 / SLICE)
    apart = (hidden - mean).astype(BF16)
    lanes = lax.broadcasted_iota(jnp.int32, (TOK, TOK), 1)
    high, mid, low = pieces(mean)
    spread = jnp.where(lanes == 0, high, jnp.where(lanes == 1, mid, jnp.where(lanes == 2, low, 0.0)))
    means = spread.T[:AUX].astype(BF16)
    rows = lax.broadcasted_iota(jnp.int32, (AUX, SLICE), 0)
    high, mid, low = pieces(gain_ref[...])
    gains = jnp.where(rows == 3, high, jnp.where(rows == 4, mid, jnp.where(rows == 5, low, 0.0)))
    for e in range(EXPERTS):
        placing = placing_ref[e]
        out_ref[e, :CAP] = jnp.dot(placing[:CAP], apart, preferred_element_type=F32).astype(BF16)
        sent = lax.dot_general(means, placing, (((1,), (1,)), ((), ())), preferred_element_type=F32)
        out_ref[e, CAP:] = jnp.concatenate(
            [sent + gains[:, :TOK], gains[:, TOK:]], axis=1
        ).astype(BF16)


def dispatch(terms, residual, gain, placing):
    return call(
        dispatch_kernel,
        (shape((TOK, SLICE), F32), shape((EXPERTS, CAP + AUX, SLICE))),
        4,
        2 * 10**8,
        5 * 10**6,
    )(terms, residual, gain, placing)


def norm_kernel(arrived_ref, *refs):
    out_ref = refs[-1]
    rows = lax.broadcasted_iota(jnp.int32, (CAP, TOK), 0)
    lanes = lax.broadcasted_iota(jnp.int32, (CAP, TOK), 1)
    diagonal = (rows == lanes).astype(BF16)
    means = []
    total = jnp.zeros((CAP, 1), F32)
    for j in range(EXPERTS):
        turned = lax.dot_general(
            diagonal, arrived_ref[j, CAP:, :TOK], (((1,), (1,)), ((), ())), preferred_element_type=F32
        )
        means.append(turned[:, 0:1] + turned[:, 1:2] + turned[:, 2:3])
        total = total + SLICE * means[j]
        total = total + jnp.sum(arrived_ref[j, :CAP].astype(F32), axis=1, keepdims=True)
    mean = total / D
    spread = jnp.zeros((CAP, 1), F32)
    for j in range(EXPERTS):
        apart = arrived_ref[j, :CAP].astype(F32) + (means[j] - mean)
        spread = spread + jnp.sum(apart * apart, axis=1, keepdims=True)
    scale = lax.rsqrt(spread / D + EPS)
    for j in range(EXPERTS):
        aux = arrived_ref[j, CAP:].astype(F32)
        gain = aux[3:4] + aux[4:5] + aux[5:6]
        apart = arrived_ref[j, :CAP].astype(F32) + (means[j] - mean)
        out_ref[j] = (apart * scale * gain).astype(BF16)


def norm(arrived, after):
    return call(
        norm_kernel,
        shape((EXPERTS, CAP, SLICE)),
        4,
        10**7,
        2 * 10**6,
        in_specs=[pl.BlockSpec(memory_space=pltpu.VMEM)]
        + [pl.BlockSpec(memory_space=pl.ANY)] * len(after),
    )(arrived, *after)


HELD = 2 * UNITS


def hold_kernel(*refs):
    weights, held, ready = refs[:6], refs[-4:-1], refs[-1]
    copies = [
        pltpu.make_async_copy(
            weights[2 * number + core],
            held[number].at[pl.ds(core * UNITS, UNITS)],
            ready.at[2 * number + core],
        )
        for number in range(3)
        for core in range(2)
    ]
    for copy in copies:
        copy.start()
    for copy in copies:
        copy.wait()


def hold(weights, after):
    apart = pl.BlockSpec(memory_space=pl.ANY)
    return call(
        hold_kernel,
        tuple(pltpu.VMEM((HELD, D), BF16) for _ in range(3)),
        1,
        10**6,
        25 * 10**6,
        in_specs=[apart] * (6 + len(after)),
        out_specs=(pl.BlockSpec(memory_space=pltpu.VMEM),) * 3,
        scratch_shapes=[pltpu.SemaphoreType.DMA((6,))],
    )(*weights, *after)


def expert_kernel(pieces_in, pieces_out, n_in, n_out, *refs):
    xs, refs = refs[:n_in], refs[n_in:]
    gate_ref, up_ref, down_ref = refs[:3]
    outs, rows_ref = refs[len(refs) - n_out - 1 : -1], refs[-1]
    for shard, split in enumerate(pieces_in):
        block = 0
        for number, first, count in split:
            for k in range(first, first + count):
                rows_ref[
                    shard * CAP : (shard + 1) * CAP, block * SLICE : (block + 1) * SLICE
                ] = xs[number][k]
                block += 1
    turned = (((1,), (1,)), ((), ()))
    rows = rows_ref[...]
    gate = lax.dot_general(rows, gate_ref[...], turned, preferred_element_type=F32)
    up = lax.dot_general(rows, up_ref[...], turned, preferred_element_type=F32)
    act = (gate / (1.0 + jnp.exp(-gate)) * up).astype(BF16)
    for now in range(EXPERTS):
        result = jnp.dot(
            act, down_ref[:, now * SLICE : (now + 1) * SLICE], preferred_element_type=F32
        ).astype(BF16)
        for shard, split in enumerate(pieces_out):
            block = 0
            for number, first, count in split:
                if block <= now < block + count:
                    outs[number][first + now - block] = result[shard * CAP : (shard + 1) * CAP]
                block += count


def expert(arrays, pieces_in, sizes, pieces_out, held, after=()):
    total = CAP * len(pieces_in)
    whole = pl.BlockSpec(memory_space=pltpu.VMEM)
    return call(
        functools.partial(expert_kernel, pieces_in, pieces_out, len(arrays), len(sizes)),
        tuple(shape((size, CAP, SLICE)) for size in sizes),
        10,
        total * D * 2 * UNITS * 6,
        25 * 10**6,
        in_specs=[whole] * (len(arrays) + 3) + [pl.BlockSpec(memory_space=pl.ANY)] * len(after),
        out_specs=(whole,) * len(sizes),
        scratch_shapes=[pltpu.VMEM((total, D), BF16)],
    )(*arrays, *held, *after)


def join_kernel(plans, *refs):
    ins, outs = refs, refs[len(refs) - len(plans) :]
    for (size, terms), out in zip(plans, outs):
        for block in range(size):
            total = None
            for number, first, into, count in terms:
                if into <= block < into + count:
                    value = ins[number][first + block - into]
                    if total is None:
                        total = value
                    else:
                        total = total.astype(F32) + value.astype(F32)
            out[block] = total.astype(BF16)


def join(plans, *arrays, after=()):
    whole = pl.BlockSpec(memory_space=pltpu.VMEM)
    return call(
        functools.partial(join_kernel, plans),
        tuple(shape((size, CAP, SLICE)) for size, _ in plans),
        2,
        10**7,
        8 * 10**6,
        in_specs=[whole] * len(arrays) + [pl.BlockSpec(memory_space=pl.ANY)] * len(after),
        out_specs=(whole,) * len(plans),
    )(*arrays, *after)


def combine_kernel(hidden_ref, high_ref, low_ref, outputs_ref, mixed_ref):
    outputs = outputs_ref[...].reshape(EXPERTS * CAP, SLICE)
    moe = jnp.dot(high_ref[...], outputs, preferred_element_type=F32)
    moe += jnp.dot(low_ref[...], outputs, preferred_element_type=F32)
    mixed_ref[...] = (hidden_ref[...] + moe).astype(BF16)


def combine(hidden, high, low, outputs):
    return call(combine_kernel, shape((TOK, SLICE)), 4, 3 * 10**8, 2 * 10**6)(
        hidden, high, low, outputs
    )


def body(
    queries,
    keys,
    values,
    residual,
    ln_gain,
    out_weight,
    gate_weight,
    up_weight,
    down_weight,
    expert_ids,
    gate_scores,
):
    ctx = lax.axis_index("ctx")
    own = jnp.stack((keys, values))[None]
    near = jnp.concatenate([own, send(own, dz=1)])
    near = jnp.concatenate([near, send(near, dy=1), send(near, dy=-1), send(near, dy=2)])
    paired = jnp.concatenate([near, send(near, dc=1)])
    y, z, c = ctx // 4, (ctx // 2) % 2, ctx % 2
    starts = [
        ((((y - dy) % 4) * 2 + (z + dz) % 2) * 2 + (c + dc) % 2) * TOK
        for dc in (0, 1)
        for dy in (0, 1, -1, 2)
        for dz in (0, 1)
    ]
    starts = jnp.stack(starts + [ctx * TOK]).astype(jnp.int32)
    placing, share_high, share_low = routing(expert_ids, gate_scores)
    weights = []
    for weight in (gate_weight[0].T, up_weight[0].T, down_weight[0]):
        weights += [weight, send(weight, dc=1)]

    term = attention(starts, queries, paired, out_weight)
    terms = lax.all_to_all(term, "exp", 0, 0, tiled=True)
    hidden, outgoing = dispatch(terms, residual, ln_gain[None], placing)
    arrived = lax.all_to_all(outgoing, "exp", 0, 0, tiled=True)
    mine = norm(arrived, weights[1:4:2])

    back, ahead, across = send(mine, dy=1), send(mine, dy=-1), send(mine, dz=1)
    held = hold(weights, (mine,))
    up, down, over = join(
        (
            (9, ((0, 0, 0, 4), (2, 0, 4, 3), (2, 4, 7, 2))),
            (9, ((1, 4, 0, 4), (2, 0, 4, 3), (2, 4, 7, 2))),
            (6, ((0, 3, 0, 1), (0, 6, 1, 2), (1, 3, 3, 1), (1, 6, 4, 2))),
        ),
        back,
        ahead,
        across,
        after=(held[0],),
    )
    low, high, both = send(up, dy=1), send(down, dy=-1), send(over, dz=1)
    mine, across, back, ahead = expert(
        [mine, across, back, ahead],
        [[(k, 0, 8)] for k in range(4)],
        (8,) * 4,
        [[(k, 0, 8)] for k in range(4)],
        held,
    )
    up, down, over = join(
        (
            (3, ((0, 4, 0, 3),)),
            (2, ((1, 7, 0, 2),)),
            (3, ((0, 3, 0, 1), (1, 2, 1, 2))),
        ),
        low,
        high,
        both,
        after=(mine,),
    )
    across_far = [send(up, dy=1), send(down, dy=-1), send(over, dz=1)]
    far_low, far_high, far_rest, across_back, across_ahead, over = expert(
        [low, high, both],
        [
            [(0, 0, 4), (1, 0, 4)],
            [(0, 4, 3), (2, 0, 1), (0, 7, 2), (2, 1, 2)],
            [(1, 4, 3), (2, 3, 1), (1, 7, 2), (2, 4, 2)],
        ],
        (3, 2, 3, 5, 5, 6),
        [
            [(0, 0, 3), (2, 0, 1), (1, 0, 2), (2, 1, 2)],
            [(3, 0, 3), (5, 0, 1), (3, 3, 2), (5, 1, 2)],
            [(4, 0, 3), (5, 3, 1), (4, 3, 2), (5, 4, 2)],
        ],
        held,
    )
    low, high, over = send(far_low, dy=1), send(far_high, dy=-1), send(over, dz=1)
    last_low, last_high, last_over = expert(
        across_far,
        [[(0, 0, 3), (2, 0, 1), (1, 0, 2), (2, 1, 2)]],
        (3, 2, 3),
        [[(0, 0, 3), (2, 0, 1), (1, 0, 2), (2, 1, 2)]],
        held,
        (far_low,),
    )
    up, down = join(
        (
            (6, ((0, 0, 0, 5), (3, 0, 0, 3), (2, 0, 5, 1), (5, 0, 5, 1))),
            (7, ((1, 0, 0, 5), (4, 0, 3, 2), (2, 1, 5, 2), (5, 1, 5, 2))),
        ),
        across_ahead,
        across_back,
        far_rest,
        send(last_low, dy=1),
        send(last_high, dy=-1),
        send(last_over, dz=1),
        after=(low, high, over),
    )
    up, down = send(up, dy=1), send(down, dy=-1)
    across, ahead, back = join(
        (
            (
                8,
                ((0, 0, 0, 8), (3, 0, 0, 3), (3, 3, 4, 2), (4, 0, 0, 3), (4, 3, 4, 2)),
            ),
            (8, ((1, 0, 0, 8), (5, 0, 0, 3), (3, 5, 3, 1), (7, 3, 3, 1), (7, 4, 6, 2))),
            (8, ((2, 0, 0, 8), (6, 0, 4, 2), (4, 5, 6, 2), (7, 0, 3, 1), (7, 1, 6, 2))),
        ),
        across,
        ahead,
        back,
        up,
        down,
        low,
        high,
        over,
    )
    (result,) = join(
        ((8, tuple((number, 0, 0, 8) for number in range(4))),),
        mine,
        send(ahead, dy=1),
        send(back, dy=-1),
        send(across, dz=1),
    )
    outputs = lax.all_to_all(result, "exp", 0, 0, tiled=True)
    return combine(hidden, share_high, share_low, outputs)


def solution(mesh):
    return jax.shard_map(
        body,
        mesh=mesh,
        in_specs=(
            P("ctx", "exp"),
            P("ctx", "exp"),
            P("ctx", "exp"),
            P("ctx", "exp"),
            P("exp"),
            P("exp", None),
            P("exp", None, "ctx"),
            P("exp", None, "ctx"),
            P("exp", "ctx", None),
            P("ctx", None),
            P("ctx", None),
        ),
        out_specs=P("ctx", "exp"),
        check_vma=False,
    )
```

```python
import functools

import jax
import jax.numpy as jnp
from jax import lax
from jax.experimental import pallas as pl
from jax.experimental.pallas import tpu as pltpu
from jax.sharding import PartitionSpec as P

D = 6144
HD = 128
EXPERTS = 8
TOPK = 4
CAP = 80
AUX = 16
TOK = 128
SLICE = 768
SHARDS = 16
UNITS = 336
EPS = 1e-05
LOG2E = 1.4426950408889634
F32 = jnp.float32
BF16 = jnp.bfloat16
MIB = 1 << 20


def place(index):
    return index // 4, (index // 2) % 2, index % 2


def route(dy, dz, dc):
    pairs = []
    for index in range(SHARDS):
        y, z, c = place(index)
        pairs.append((index, (((y + dy) % 4) * 2 + (z + dz) % 2) * 2 + (c + dc) % 2))
    return pairs


def send(block, dy=0, dz=0, dc=0):
    return lax.ppermute(block, "ctx", route(dy, dz, dc))


def turn(block, dx=0, dz=0):
    pairs = [(j, (j // 4 + dz) % 2 * 4 + (j + dx) % 4) for j in range(EXPERTS)]
    return lax.ppermute(block, "exp", pairs)


WAYS = ((0, 0), (2, 1), (2, 0), (1, 1), (3, 1), (1, 0), (3, 0), (0, 1))


def exchange(blocks):
    return [blocks[0]] + [turn(block, *way) for block, way in zip(blocks[1:], WAYS[1:])]


def number_at(spot_ref, way, sign):
    x, z = spot_ref[0] + sign * way[0] + 4, spot_ref[1] + way[1]
    return lax.rem(z, 2) * 4 + lax.rem(x, 4)


def call(kernel, out_shape, limit, flops, moved, **kwargs):
    return pl.pallas_call(
        kernel,
        out_shape=out_shape,
        compiler_params=pltpu.CompilerParams(vmem_limit_bytes=limit * MIB),
        cost_estimate=pl.CostEstimate(flops=flops, bytes_accessed=moved, transcendentals=0),
        **kwargs,
    )


def shape(dims, dtype=BF16):
    return jax.ShapeDtypeStruct(dims, dtype)


def pieces(value):
    high = value.astype(BF16).astype(F32)
    left = value - high
    mid = left.astype(BF16).astype(F32)
    return high, mid, left - mid


def routing_kernel(ids_ref, scores_ref, placing_ref, high_ref, low_ref):
    ids = ids_ref[...]
    scores = scores_ref[...]
    total = scores[:, 0:1] + scores[:, 1:2] + scores[:, 2:3] + scores[:, 3:4]
    lanes = lax.broadcasted_iota(jnp.int32, (TOK, TOK), 1)
    rows = lax.broadcasted_iota(jnp.int32, (TOK, TOK), 0)
    named = [(lanes == ids[:, k : k + 1]).astype(F32) for k in range(TOPK)]
    member = named[0] + named[1] + named[2] + named[3]
    lower = (lanes < rows).astype(BF16)
    slots = jnp.dot(lower, member.astype(BF16), preferred_element_type=F32)
    wide = lax.broadcasted_iota(jnp.int32, (TOK, EXPERTS * TOK), 1)
    columns = lax.broadcasted_iota(jnp.int32, (TOK, EXPERTS * CAP), 1)
    placed = jnp.zeros((TOK, EXPERTS * TOK), F32)
    shares = jnp.zeros((TOK, EXPERTS * CAP), F32)
    for k in range(TOPK):
        slot = jnp.sum(named[k] * slots, axis=1, keepdims=True).astype(jnp.int32)
        expert = ids[:, k : k + 1]
        placed = placed + (wide == expert * TOK + slot).astype(F32)
        share = scores[:, k : k + 1] / total
        shares = shares + jnp.where(columns == expert * CAP + slot, share, 0.0)
    for e in range(EXPERTS):
        placing_ref[e] = placed[:, e * TOK : (e + 1) * TOK].T.astype(BF16)
    high = shares.astype(BF16)
    high_ref[...] = high
    low_ref[...] = (shares - high.astype(F32)).astype(BF16)


def routing(expert_ids, gate_scores):
    return call(
        routing_kernel,
        (
            shape((EXPERTS, TOK, TOK)),
            shape((TOK, EXPERTS * CAP)),
            shape((TOK, EXPERTS * CAP)),
        ),
        6,
        10**7,
        10**6,
    )(expert_ids, gate_scores)


def keep_kernel(weight_ref, *refs):
    held_ref, ready = refs[-2:]
    rows = SLICE // 4
    copies = [
        pltpu.make_async_copy(
            weight_ref.at[pl.ds(k * rows, rows)], held_ref.at[pl.ds(k * rows, rows)], ready.at[k]
        )
        for k in range(4)
    ]
    for copy in copies:
        copy.start()
    for copy in copies:
        copy.wait()


def keep(weight, after):
    return call(
        keep_kernel,
        pltpu.VMEM((SLICE, D), BF16),
        1,
        10**6,
        10**7,
        in_specs=[pl.BlockSpec(memory_space=pl.ANY)] * (1 + len(after)),
        out_specs=pl.BlockSpec(memory_space=pltpu.VMEM),
        scratch_shapes=[pltpu.SemaphoreType.DMA((4,))],
    )(weight, *after)


def attention_kernel(starts_ref, spot_ref, queries_ref, paired_ref, weight_ref, *refs):
    terms = refs[-len(WAYS) :]
    keys = paired_ref[:, 0].reshape(SHARDS * TOK, HD)
    values = paired_ref[:, 1].reshape(SHARDS * TOK, HD)
    rows = lax.broadcasted_iota(jnp.int32, (TOK, TOK), 0)
    lanes = lax.broadcasted_iota(jnp.int32, (TOK, TOK), 1)
    ahead = rows - lanes + starts_ref[SHARDS]
    keep = jnp.concatenate([ahead >= starts_ref[b] for b in range(SHARDS)], axis=1)
    heads = []
    for h in range(queries_ref.shape[1] // HD):
        query = queries_ref[:, h * HD : (h + 1) * HD]
        scores = lax.dot_general(
            query, keys, (((1,), (1,)), ((), ())), preferred_element_type=F32
        )
        scores = jnp.where(keep, scores, -1e30)
        top = jnp.max(scores, axis=1, keepdims=True)
        expw = jnp.exp2((scores - top) * (HD**-0.5 * LOG2E))
        denom = jnp.sum(expw, axis=1, keepdims=True)
        summed = jnp.dot(expw.astype(BF16), values, preferred_element_type=F32)
        heads.append((summed / denom).astype(BF16))
    attended = jnp.concatenate(heads, axis=1)
    for term, way in zip(terms, WAYS):
        first = pl.multiple_of(number_at(spot_ref, way, 1) * SLICE, 128)
        term[...] = jnp.dot(
            attended, weight_ref[:, pl.ds(first, SLICE)], preferred_element_type=F32
        ).astype(BF16)


def attention(starts, spot, queries, paired, held, after):
    whole = pl.BlockSpec(memory_space=pltpu.VMEM)
    return call(
        attention_kernel,
        (shape((TOK, SLICE)),) * len(WAYS),
        20,
        2 * 10**9,
        13 * 10**6,
        in_specs=[pl.BlockSpec(memory_space=pltpu.SMEM)] * 2
        + [whole] * 3
        + [pl.BlockSpec(memory_space=pl.ANY)] * len(after),
        out_specs=(whole,) * len(WAYS),
    )(starts, spot, queries, paired, held, *after)


def dispatch_kernel(spot_ref, residual_ref, gain_ref, placing_ref, *refs):
    terms, hidden_ref, outs = refs[: len(WAYS)], refs[len(WAYS)], refs[len(WAYS) + 1 :]
    hidden = residual_ref[...].astype(F32)
    for term in terms:
        hidden = hidden + term[...].astype(F32)
    hidden_ref[...] = hidden
    mean = jnp.sum(hidden, axis=1, keepdims=True) * (1.0 / SLICE)
    apart = (hidden - mean).astype(BF16)
    lanes = lax.broadcasted_iota(jnp.int32, (TOK, TOK), 1)
    high, mid, low = pieces(mean)
    spread = jnp.where(lanes == 0, high, jnp.where(lanes == 1, mid, jnp.where(lanes == 2, low, 0.0)))
    means = spread.T[:AUX].astype(BF16)
    rows = lax.broadcasted_iota(jnp.int32, (AUX, SLICE), 0)
    high, mid, low = pieces(gain_ref[...])
    gains = jnp.where(rows == 3, high, jnp.where(rows == 4, mid, jnp.where(rows == 5, low, 0.0)))
    for out, way in zip(outs, WAYS):
        placing = placing_ref[number_at(spot_ref, way, 1)]
        out[:CAP] = jnp.dot(placing[:CAP], apart, preferred_element_type=F32).astype(BF16)
        sent = lax.dot_general(means, placing, (((1,), (1,)), ((), ())), preferred_element_type=F32)
        out[CAP:] = jnp.concatenate([sent + gains[:, :TOK], gains[:, TOK:]], axis=1).astype(BF16)


def dispatch(spot, terms, residual, gain, placing):
    whole = pl.BlockSpec(memory_space=pltpu.VMEM)
    outs = call(
        dispatch_kernel,
        (shape((TOK, SLICE), F32),) + (shape((CAP + AUX, SLICE)),) * len(WAYS),
        4,
        2 * 10**8,
        5 * 10**6,
        in_specs=[pl.BlockSpec(memory_space=pltpu.SMEM)] + [whole] * (3 + len(WAYS)),
    )(spot, residual, gain, placing, *terms)
    return outs[0], outs[1:]


def norm_kernel(spot_ref, *refs):
    arrived, out_ref = refs[: len(WAYS)], refs[-1]
    rows = lax.broadcasted_iota(jnp.int32, (CAP, TOK), 0)
    lanes = lax.broadcasted_iota(jnp.int32, (CAP, TOK), 1)
    diagonal = (rows == lanes).astype(BF16)
    means = []
    total = jnp.zeros((CAP, 1), F32)
    for block in arrived:
        turned = lax.dot_general(
            diagonal, block[CAP:, :TOK], (((1,), (1,)), ((), ())), preferred_element_type=F32
        )
        means.append(turned[:, 0:1] + turned[:, 1:2] + turned[:, 2:3])
        total = total + SLICE * means[-1]
        total = total + jnp.sum(block[:CAP].astype(F32), axis=1, keepdims=True)
    mean = total / D
    spread = jnp.zeros((CAP, 1), F32)
    for block, own in zip(arrived, means):
        apart = block[:CAP].astype(F32) + (own - mean)
        spread = spread + jnp.sum(apart * apart, axis=1, keepdims=True)
    scale = lax.rsqrt(spread / D + EPS)
    for block, own, way in zip(arrived, means, WAYS):
        aux = block[CAP:].astype(F32)
        gain = aux[3:4] + aux[4:5] + aux[5:6]
        apart = block[:CAP].astype(F32) + (own - mean)
        out_ref[number_at(spot_ref, way, -1)] = (apart * scale * gain).astype(BF16)


def norm(spot, arrived):
    return call(
        norm_kernel,
        shape((EXPERTS, CAP, SLICE)),
        4,
        10**7,
        2 * 10**6,
        in_specs=[pl.BlockSpec(memory_space=pltpu.SMEM)]
        + [pl.BlockSpec(memory_space=pltpu.VMEM)] * len(WAYS),
    )(spot, *arrived)


HELD = 2 * UNITS


def hold_kernel(*refs):
    weights, held, ready = refs[:6], refs[-4:-1], refs[-1]
    copies = [
        pltpu.make_async_copy(
            weights[2 * number + core],
            held[number].at[pl.ds(core * UNITS, UNITS)],
            ready.at[2 * number + core],
        )
        for number in range(3)
        for core in range(2)
    ]
    for copy in copies:
        copy.start()
    for copy in copies:
        copy.wait()


def hold(weights, after):
    apart = pl.BlockSpec(memory_space=pl.ANY)
    return call(
        hold_kernel,
        tuple(pltpu.VMEM((HELD, D), BF16) for _ in range(3)),
        1,
        10**6,
        25 * 10**6,
        in_specs=[apart] * (6 + len(after)),
        out_specs=(pl.BlockSpec(memory_space=pltpu.VMEM),) * 3,
        scratch_shapes=[pltpu.SemaphoreType.DMA((6,))],
    )(*weights, *after)


def expert_kernel(pieces_in, pieces_out, n_in, n_out, *refs):
    xs, refs = refs[:n_in], refs[n_in:]
    gate_ref, up_ref, down_ref = refs[:3]
    outs, rows_ref = refs[len(refs) - n_out - 1 : -1], refs[-1]
    for shard, split in enumerate(pieces_in):
        block = 0
        for number, first, count in split:
            for k in range(first, first + count):
                rows_ref[
                    shard * CAP : (shard + 1) * CAP, block * SLICE : (block + 1) * SLICE
                ] = xs[number][k]
                block += 1
    turned = (((1,), (1,)), ((), ()))
    rows = rows_ref[...]
    gate = lax.dot_general(rows, gate_ref[...], turned, preferred_element_type=F32)
    up = lax.dot_general(rows, up_ref[...], turned, preferred_element_type=F32)
    act = (gate / (1.0 + jnp.exp(-gate)) * up).astype(BF16)
    for now in range(EXPERTS):
        result = jnp.dot(
            act, down_ref[:, now * SLICE : (now + 1) * SLICE], preferred_element_type=F32
        ).astype(BF16)
        for shard, split in enumerate(pieces_out):
            block = 0
            for number, first, count in split:
                if block <= now < block + count:
                    outs[number][first + now - block] = result[shard * CAP : (shard + 1) * CAP]
                block += count


def expert(arrays, pieces_in, sizes, pieces_out, held, after=()):
    total = CAP * len(pieces_in)
    whole = pl.BlockSpec(memory_space=pltpu.VMEM)
    return call(
        functools.partial(expert_kernel, pieces_in, pieces_out, len(arrays), len(sizes)),
        tuple(shape((size, CAP, SLICE)) for size in sizes),
        10,
        total * D * 2 * UNITS * 6,
        25 * 10**6,
        in_specs=[whole] * (len(arrays) + 3) + [pl.BlockSpec(memory_space=pl.ANY)] * len(after),
        out_specs=(whole,) * len(sizes),
        scratch_shapes=[pltpu.VMEM((total, D), BF16)],
    )(*arrays, *held, *after)


def join_kernel(plans, *refs):
    ins, outs = refs, refs[len(refs) - len(plans) :]
    for (size, terms), out in zip(plans, outs):
        for block in range(size):
            total = None
            for number, first, into, count in terms:
                if into <= block < into + count:
                    value = ins[number][first + block - into]
                    if total is None:
                        total = value
                    else:
                        total = total.astype(F32) + value.astype(F32)
            out[block] = total.astype(BF16)


def join(plans, *arrays, after=()):
    whole = pl.BlockSpec(memory_space=pltpu.VMEM)
    return call(
        functools.partial(join_kernel, plans),
        tuple(shape((size, CAP, SLICE)) for size, _ in plans),
        2,
        10**7,
        8 * 10**6,
        in_specs=[whole] * len(arrays) + [pl.BlockSpec(memory_space=pl.ANY)] * len(after),
        out_specs=(whole,) * len(plans),
    )(*arrays, *after)


def combine_kernel(hidden_ref, high_ref, low_ref, outputs_ref, mixed_ref):
    outputs = outputs_ref[...].reshape(EXPERTS * CAP, SLICE)
    moe = jnp.dot(high_ref[...], outputs, preferred_element_type=F32)
    moe += jnp.dot(low_ref[...], outputs, preferred_element_type=F32)
    mixed_ref[...] = (hidden_ref[...] + moe).astype(BF16)


def combine(hidden, high, low, outputs):
    return call(combine_kernel, shape((TOK, SLICE)), 4, 3 * 10**8, 2 * 10**6)(
        hidden, high, low, outputs
    )


def body(
    queries,
    keys,
    values,
    residual,
    ln_gain,
    out_weight,
    gate_weight,
    up_weight,
    down_weight,
    expert_ids,
    gate_scores,
):
    ctx = lax.axis_index("ctx")
    own = jnp.stack((keys, values))[None]
    first = jnp.concatenate([own, send(own, dz=1)])
    near = first
    near = jnp.concatenate([near, send(near, dy=1), send(near, dy=-1), send(near, dy=2)])
    paired = jnp.concatenate([near, send(near, dc=1)])
    y, z, c = ctx // 4, (ctx // 2) % 2, ctx % 2
    starts = [
        ((((y - dy) % 4) * 2 + (z + dz) % 2) * 2 + (c + dc) % 2) * TOK
        for dc in (0, 1)
        for dy in (0, 1, -1, 2)
        for dz in (0, 1)
    ]
    starts = jnp.stack(starts + [ctx * TOK]).astype(jnp.int32)
    placing, share_high, share_low = routing(expert_ids, gate_scores)
    weights = []
    for weight in (gate_weight[0].T, up_weight[0].T, down_weight[0]):
        weights += [weight, send(weight, dc=1)]

    exp = lax.axis_index("exp")
    spot = jnp.stack([exp % 4, exp // 4]).astype(jnp.int32)
    kept = keep(out_weight, (first,))
    terms = attention(starts, spot, queries, paired, kept, weights[1::2])
    hidden, outgoing = dispatch(spot, exchange(terms), residual, ln_gain[None], placing)
    mine = norm(spot, exchange(outgoing))

    back, ahead, across = send(mine, dy=1), send(mine, dy=-1), send(mine, dz=1)
    held = hold(weights, (mine,))
    up, down, over = join(
        (
            (9, ((0, 0, 0, 4), (2, 0, 4, 3), (2, 4, 7, 2))),
            (9, ((1, 4, 0, 4), (2, 0, 4, 3), (2, 4, 7, 2))),
            (6, ((0, 3, 0, 1), (0, 6, 1, 2), (1, 3, 3, 1), (1, 6, 4, 2))),
        ),
        back,
        ahead,
        across,
        after=(held[0],),
    )
    low, high, both = send(up, dy=1), send(down, dy=-1), send(over, dz=1)
    mine, across, back, ahead = expert(
        [mine, across, back, ahead],
        [[(k, 0, 8)] for k in range(4)],
        (8,) * 4,
        [[(k, 0, 8)] for k in range(4)],
        held,
    )
    up, down, over = join(
        (
            (3, ((0, 4, 0, 3),)),
            (2, ((1, 7, 0, 2),)),
            (3, ((0, 3, 0, 1), (1, 2, 1, 2))),
        ),
        low,
        high,
        both,
        after=(mine,),
    )
    across_far = [send(up, dy=1), send(down, dy=-1), send(over, dz=1)]
    far_low, far_high, far_rest, across_back, across_ahead, over = expert(
        [low, high, both],
        [
            [(0, 0, 4), (1, 0, 4)],
            [(0, 4, 3), (2, 0, 1), (0, 7, 2), (2, 1, 2)],
            [(1, 4, 3), (2, 3, 1), (1, 7, 2), (2, 4, 2)],
        ],
        (3, 2, 3, 5, 5, 6),
        [
            [(0, 0, 3), (2, 0, 1), (1, 0, 2), (2, 1, 2)],
            [(3, 0, 3), (5, 0, 1), (3, 3, 2), (5, 1, 2)],
            [(4, 0, 3), (5, 3, 1), (4, 3, 2), (5, 4, 2)],
        ],
        held,
    )
    low, high, over = send(far_low, dy=1), send(far_high, dy=-1), send(over, dz=1)
    last_low, last_high, last_over = expert(
        across_far,
        [[(0, 0, 3), (2, 0, 1), (1, 0, 2), (2, 1, 2)]],
        (3, 2, 3),
        [[(0, 0, 3), (2, 0, 1), (1, 0, 2), (2, 1, 2)]],
        held,
        (far_low,),
    )
    up, down = join(
        (
            (6, ((0, 0, 0, 5), (3, 0, 0, 3), (2, 0, 5, 1), (5, 0, 5, 1))),
            (7, ((1, 0, 0, 5), (4, 0, 3, 2), (2, 1, 5, 2), (5, 1, 5, 2))),
        ),
        across_ahead,
        across_back,
        far_rest,
        send(last_low, dy=1),
        send(last_high, dy=-1),
        send(last_over, dz=1),
        after=(low, high, over),
    )
    up, down = send(up, dy=1), send(down, dy=-1)
    across, ahead, back = join(
        (
            (
                8,
                ((0, 0, 0, 8), (3, 0, 0, 3), (3, 3, 4, 2), (4, 0, 0, 3), (4, 3, 4, 2)),
            ),
            (8, ((1, 0, 0, 8), (5, 0, 0, 3), (3, 5, 3, 1), (7, 3, 3, 1), (7, 4, 6, 2))),
            (8, ((2, 0, 0, 8), (6, 0, 4, 2), (4, 5, 6, 2), (7, 0, 3, 1), (7, 1, 6, 2))),
        ),
        across,
        ahead,
        back,
        up,
        down,
        low,
        high,
        over,
    )
    (result,) = join(
        ((8, tuple((number, 0, 0, 8) for number in range(4))),),
        mine,
        send(ahead, dy=1),
        send(back, dy=-1),
        send(across, dz=1),
    )
    outputs = lax.all_to_all(result, "exp", 0, 0, tiled=True)
    return combine(hidden, share_high, share_low, outputs)


def solution(mesh):
    return jax.shard_map(
        body,
        mesh=mesh,
        in_specs=(
            P("ctx", "exp"),
            P("ctx", "exp"),
            P("ctx", "exp"),
            P("ctx", "exp"),
            P("exp"),
            P("exp", None),
            P("exp", None, "ctx"),
            P("exp", None, "ctx"),
            P("exp", "ctx", None),
            P("ctx", None),
            P("ctx", None),
        ),
        out_specs=P("ctx", "exp"),
        check_vma=False,
    )
```

```python
import functools

import jax
import jax.numpy as jnp
from jax import lax
from jax.experimental import pallas as pl
from jax.experimental.pallas import tpu as pltpu
from jax.sharding import PartitionSpec as P

D = 6144
HD = 128
EXPERTS = 8
TOPK = 4
CAP = 80
AUX = 16
TOK = 128
SLICE = 768
SHARDS = 16
UNITS = 336
EPS = 1e-05
LOG2E = 1.4426950408889634
F32 = jnp.float32
BF16 = jnp.bfloat16
MIB = 1 << 20


def place(index):
    return index // 4, (index // 2) % 2, index % 2


def route(dy, dz, dc):
    pairs = []
    for index in range(SHARDS):
        y, z, c = place(index)
        pairs.append((index, (((y + dy) % 4) * 2 + (z + dz) % 2) * 2 + (c + dc) % 2))
    return pairs


def send(block, dy=0, dz=0, dc=0):
    return lax.ppermute(block, "ctx", route(dy, dz, dc))


def turn(block, dx=0, dz=0):
    pairs = [(j, (j // 4 + dz) % 2 * 4 + (j + dx) % 4) for j in range(EXPERTS)]
    return lax.ppermute(block, "exp", pairs)


WAYS = ((0, 0), (2, 1), (2, 0), (1, 1), (3, 1), (1, 0), (3, 0), (0, 1))


def exchange(blocks):
    return [blocks[0]] + [turn(block, *way) for block, way in zip(blocks[1:], WAYS[1:])]


def number_at(spot_ref, way, sign):
    x, z = spot_ref[0] + sign * way[0] + 4, spot_ref[1] + way[1]
    return lax.rem(z, 2) * 4 + lax.rem(x, 4)


def call(kernel, out_shape, limit, flops, moved, **kwargs):
    return pl.pallas_call(
        kernel,
        out_shape=out_shape,
        compiler_params=pltpu.CompilerParams(vmem_limit_bytes=limit * MIB),
        cost_estimate=pl.CostEstimate(flops=flops, bytes_accessed=moved, transcendentals=0),
        **kwargs,
    )


def shape(dims, dtype=BF16):
    return jax.ShapeDtypeStruct(dims, dtype)


def pieces(value):
    high = value.astype(BF16).astype(F32)
    left = value - high
    mid = left.astype(BF16).astype(F32)
    return high, mid, left - mid


def routing_kernel(ids_ref, scores_ref, placing_ref, high_ref, low_ref):
    ids = ids_ref[...]
    scores = scores_ref[...]
    total = scores[:, 0:1] + scores[:, 1:2] + scores[:, 2:3] + scores[:, 3:4]
    lanes = lax.broadcasted_iota(jnp.int32, (TOK, TOK), 1)
    rows = lax.broadcasted_iota(jnp.int32, (TOK, TOK), 0)
    named = [(lanes == ids[:, k : k + 1]).astype(F32) for k in range(TOPK)]
    member = named[0] + named[1] + named[2] + named[3]
    lower = (lanes < rows).astype(BF16)
    slots = jnp.dot(lower, member.astype(BF16), preferred_element_type=F32)
    wide = lax.broadcasted_iota(jnp.int32, (TOK, EXPERTS * TOK), 1)
    columns = lax.broadcasted_iota(jnp.int32, (TOK, EXPERTS * CAP), 1)
    placed = jnp.zeros((TOK, EXPERTS * TOK), F32)
    shares = jnp.zeros((TOK, EXPERTS * CAP), F32)
    for k in range(TOPK):
        slot = jnp.sum(named[k] * slots, axis=1, keepdims=True).astype(jnp.int32)
        expert = ids[:, k : k + 1]
        placed = placed + (wide == expert * TOK + slot).astype(F32)
        share = scores[:, k : k + 1] / total
        shares = shares + jnp.where(columns == expert * CAP + slot, share, 0.0)
    for e in range(EXPERTS):
        placing_ref[e] = placed[:, e * TOK : (e + 1) * TOK].T.astype(BF16)
    high = shares.astype(BF16)
    high_ref[...] = high
    low_ref[...] = (shares - high.astype(F32)).astype(BF16)


def routing(expert_ids, gate_scores):
    return call(
        routing_kernel,
        (
            shape((EXPERTS, TOK, TOK)),
            shape((TOK, EXPERTS * CAP)),
            shape((TOK, EXPERTS * CAP)),
        ),
        6,
        10**7,
        10**6,
    )(expert_ids, gate_scores)


def keep_kernel(weight_ref, *refs):
    held_ref, ready = refs[-2:]
    rows = SLICE // 4
    copies = [
        pltpu.make_async_copy(
            weight_ref.at[pl.ds(k * rows, rows)], held_ref.at[pl.ds(k * rows, rows)], ready.at[k]
        )
        for k in range(4)
    ]
    for copy in copies:
        copy.start()
    for copy in copies:
        copy.wait()


def keep(weight, after):
    return call(
        keep_kernel,
        pltpu.VMEM((SLICE, D), BF16),
        48,
        10**6,
        10**7,
        in_specs=[pl.BlockSpec(memory_space=pl.ANY)] * (1 + len(after)),
        out_specs=pl.BlockSpec(memory_space=pltpu.VMEM),
        scratch_shapes=[pltpu.SemaphoreType.DMA((4,))],
    )(weight, *after)


def stack_kernel(*refs):
    out_ref = refs[-1]
    for k in range(4):
        out_ref[2 * k : 2 * k + 2] = refs[k][...]


def stack(parts, after):
    whole = pl.BlockSpec(memory_space=pltpu.VMEM)
    return call(
        stack_kernel,
        shape((8, 2, TOK, HD)),
        2,
        10**5,
        10**6,
        in_specs=[whole] * 4 + [pl.BlockSpec(memory_space=pl.ANY)] * len(after),
        out_specs=whole,
    )(*parts, *after)


def attention_kernel(starts_ref, spot_ref, queries_ref, paired_ref, weight_ref, *refs):
    terms = refs[-len(WAYS) :]
    keys = paired_ref[:, 0].reshape(SHARDS * TOK, HD)
    values = paired_ref[:, 1].reshape(SHARDS * TOK, HD)
    rows = lax.broadcasted_iota(jnp.int32, (TOK, TOK), 0)
    lanes = lax.broadcasted_iota(jnp.int32, (TOK, TOK), 1)
    ahead = rows - lanes + starts_ref[SHARDS]
    keep = jnp.concatenate([ahead >= starts_ref[b] for b in range(SHARDS)], axis=1)
    heads = []
    for h in range(queries_ref.shape[1] // HD):
        query = queries_ref[:, h * HD : (h + 1) * HD]
        scores = lax.dot_general(
            query, keys, (((1,), (1,)), ((), ())), preferred_element_type=F32
        )
        scores = jnp.where(keep, scores, -1e30)
        top = jnp.max(scores, axis=1, keepdims=True)
        expw = jnp.exp2((scores - top) * (HD**-0.5 * LOG2E))
        denom = jnp.sum(expw, axis=1, keepdims=True)
        summed = jnp.dot(expw.astype(BF16), values, preferred_element_type=F32)
        heads.append((summed / denom).astype(BF16))
    attended = jnp.concatenate(heads, axis=1)
    for term, way in zip(terms, WAYS):
        first = pl.multiple_of(number_at(spot_ref, way, 1) * SLICE, 128)
        term[...] = jnp.dot(
            attended, weight_ref[:, pl.ds(first, SLICE)], preferred_element_type=F32
        ).astype(BF16)


def attention(starts, spot, queries, paired, held, after):
    whole = pl.BlockSpec(memory_space=pltpu.VMEM)
    return call(
        attention_kernel,
        (shape((TOK, SLICE)),) * len(WAYS),
        20,
        2 * 10**9,
        13 * 10**6,
        in_specs=[pl.BlockSpec(memory_space=pltpu.SMEM)] * 2
        + [whole] * 3
        + [pl.BlockSpec(memory_space=pl.ANY)] * len(after),
        out_specs=(whole,) * len(WAYS),
    )(starts, spot, queries, paired, held, *after)


def dispatch_kernel(residual_ref, gain_ref, placing_ref, *refs):
    terms, (hidden_ref, out_ref) = refs[: len(WAYS)], refs[len(WAYS) :]
    hidden = residual_ref[...].astype(F32)
    for term in terms:
        hidden = hidden + term[...].astype(F32)
    hidden_ref[...] = hidden
    mean = jnp.sum(hidden, axis=1, keepdims=True) * (1.0 / SLICE)
    apart = (hidden - mean).astype(BF16)
    lanes = lax.broadcasted_iota(jnp.int32, (TOK, TOK), 1)
    high, mid, low = pieces(mean)
    spread = jnp.where(lanes == 0, high, jnp.where(lanes == 1, mid, jnp.where(lanes == 2, low, 0.0)))
    means = spread.T[:AUX].astype(BF16)
    rows = lax.broadcasted_iota(jnp.int32, (AUX, SLICE), 0)
    high, mid, low = pieces(gain_ref[...])
    gains = jnp.where(rows == 3, high, jnp.where(rows == 4, mid, jnp.where(rows == 5, low, 0.0)))
    for e in range(EXPERTS):
        placing = placing_ref[e]
        out_ref[e, :CAP] = jnp.dot(placing[:CAP], apart, preferred_element_type=F32).astype(BF16)
        sent = lax.dot_general(means, placing, (((1,), (1,)), ((), ())), preferred_element_type=F32)
        out_ref[e, CAP:] = jnp.concatenate(
            [sent + gains[:, :TOK], gains[:, TOK:]], axis=1
        ).astype(BF16)


def dispatch(terms, residual, gain, placing):
    return call(
        dispatch_kernel,
        (shape((TOK, SLICE), F32), shape((EXPERTS, CAP + AUX, SLICE))),
        4,
        2 * 10**8,
        5 * 10**6,
    )(residual, gain, placing, *terms)


def norm_kernel(arrived_ref, out_ref):
    rows = lax.broadcasted_iota(jnp.int32, (CAP, TOK), 0)
    lanes = lax.broadcasted_iota(jnp.int32, (CAP, TOK), 1)
    diagonal = (rows == lanes).astype(BF16)
    means = []
    total = jnp.zeros((CAP, 1), F32)
    for j in range(EXPERTS):
        turned = lax.dot_general(
            diagonal, arrived_ref[j, CAP:, :TOK], (((1,), (1,)), ((), ())), preferred_element_type=F32
        )
        means.append(turned[:, 0:1] + turned[:, 1:2] + turned[:, 2:3])
        total = total + SLICE * means[j]
        total = total + jnp.sum(arrived_ref[j, :CAP].astype(F32), axis=1, keepdims=True)
    mean = total / D
    spread = jnp.zeros((CAP, 1), F32)
    for j in range(EXPERTS):
        apart = arrived_ref[j, :CAP].astype(F32) + (means[j] - mean)
        spread = spread + jnp.sum(apart * apart, axis=1, keepdims=True)
    scale = lax.rsqrt(spread / D + EPS)
    for j in range(EXPERTS):
        aux = arrived_ref[j, CAP:].astype(F32)
        gain = aux[3:4] + aux[4:5] + aux[5:6]
        apart = arrived_ref[j, :CAP].astype(F32) + (means[j] - mean)
        out_ref[j] = (apart * scale * gain).astype(BF16)


def norm(arrived):
    return call(norm_kernel, shape((EXPERTS, CAP, SLICE)), 4, 10**7, 2 * 10**6)(arrived)


HELD = 2 * UNITS


def hold_kernel(*refs):
    weights, held, ready = refs[:6], refs[-4:-1], refs[-1]
    copies = [
        pltpu.make_async_copy(
            weights[2 * number + core],
            held[number].at[pl.ds(core * UNITS, UNITS)],
            ready.at[2 * number + core],
        )
        for number in range(3)
        for core in range(2)
    ]
    for copy in copies:
        copy.start()
    for copy in copies:
        copy.wait()


def hold(weights, after):
    apart = pl.BlockSpec(memory_space=pl.ANY)
    return call(
        hold_kernel,
        tuple(pltpu.VMEM((HELD, D), BF16) for _ in range(3)),
        1,
        10**6,
        25 * 10**6,
        in_specs=[apart] * (6 + len(after)),
        out_specs=(pl.BlockSpec(memory_space=pltpu.VMEM),) * 3,
        scratch_shapes=[pltpu.SemaphoreType.DMA((6,))],
    )(*weights, *after)


def expert_kernel(pieces_in, pieces_out, n_in, n_out, *refs):
    xs, refs = refs[:n_in], refs[n_in:]
    gate_ref, up_ref, down_ref = refs[:3]
    outs, rows_ref = refs[len(refs) - n_out - 1 : -1], refs[-1]
    for shard, split in enumerate(pieces_in):
        block = 0
        for number, first, count in split:
            for k in range(first, first + count):
                rows_ref[
                    shard * CAP : (shard + 1) * CAP, block * SLICE : (block + 1) * SLICE
                ] = xs[number][k]
                block += 1
    turned = (((1,), (1,)), ((), ()))
    rows = rows_ref[...]
    gate = lax.dot_general(rows, gate_ref[...], turned, preferred_element_type=F32)
    up = lax.dot_general(rows, up_ref[...], turned, preferred_element_type=F32)
    act = (gate / (1.0 + jnp.exp(-gate)) * up).astype(BF16)
    for now in range(EXPERTS):
        result = jnp.dot(
            act, down_ref[:, now * SLICE : (now + 1) * SLICE], preferred_element_type=F32
        ).astype(BF16)
        for shard, split in enumerate(pieces_out):
            block = 0
            for number, first, count in split:
                if block <= now < block + count:
                    outs[number][first + now - block] = result[shard * CAP : (shard + 1) * CAP]
                block += count


def expert(arrays, pieces_in, sizes, pieces_out, held, after=()):
    total = CAP * len(pieces_in)
    whole = pl.BlockSpec(memory_space=pltpu.VMEM)
    return call(
        functools.partial(expert_kernel, pieces_in, pieces_out, len(arrays), len(sizes)),
        tuple(shape((size, CAP, SLICE)) for size in sizes),
        10,
        total * D * 2 * UNITS * 6,
        25 * 10**6,
        in_specs=[whole] * (len(arrays) + 3) + [pl.BlockSpec(memory_space=pl.ANY)] * len(after),
        out_specs=(whole,) * len(sizes),
        scratch_shapes=[pltpu.VMEM((total, D), BF16)],
    )(*arrays, *held, *after)


def join_kernel(plans, *refs):
    ins, outs = refs, refs[len(refs) - len(plans) :]
    for (size, terms), out in zip(plans, outs):
        for block in range(size):
            total = None
            for number, first, into, count in terms:
                if into <= block < into + count:
                    value = ins[number][first + block - into]
                    if total is None:
                        total = value
                    else:
                        total = total.astype(F32) + value.astype(F32)
            out[block] = total.astype(BF16)


def join(plans, *arrays, after=()):
    whole = pl.BlockSpec(memory_space=pltpu.VMEM)
    return call(
        functools.partial(join_kernel, plans),
        tuple(shape((size, CAP, SLICE)) for size, _ in plans),
        2,
        10**7,
        8 * 10**6,
        in_specs=[whole] * len(arrays) + [pl.BlockSpec(memory_space=pl.ANY)] * len(after),
        out_specs=(whole,) * len(plans),
    )(*arrays, *after)


def combine_kernel(hidden_ref, high_ref, low_ref, outputs_ref, mixed_ref):
    outputs = outputs_ref[...].reshape(EXPERTS * CAP, SLICE)
    moe = jnp.dot(high_ref[...], outputs, preferred_element_type=F32)
    moe += jnp.dot(low_ref[...], outputs, preferred_element_type=F32)
    mixed_ref[...] = (hidden_ref[...] + moe).astype(BF16)


def combine(hidden, high, low, outputs):
    return call(combine_kernel, shape((TOK, SLICE)), 4, 3 * 10**8, 2 * 10**6)(
        hidden, high, low, outputs
    )


def body(
    queries,
    keys,
    values,
    residual,
    ln_gain,
    out_weight,
    gate_weight,
    up_weight,
    down_weight,
    expert_ids,
    gate_scores,
):
    ctx = lax.axis_index("ctx")
    own = jnp.stack((keys, values))[None]
    first = jnp.concatenate([own, send(own, dz=1)])
    kept = keep(out_weight, (first,))
    near = stack([first, send(first, dy=1), send(first, dy=-1), send(first, dy=2)], (kept,))
    paired = jnp.concatenate([near, send(near, dc=1)])
    y, z, c = ctx // 4, (ctx // 2) % 2, ctx % 2
    starts = [
        ((((y - dy) % 4) * 2 + (z + dz) % 2) * 2 + (c + dc) % 2) * TOK
        for dc in (0, 1)
        for dy in (0, 1, -1, 2)
        for dz in (0, 1)
    ]
    starts = jnp.stack(starts + [ctx * TOK]).astype(jnp.int32)
    placing, share_high, share_low = routing(expert_ids, gate_scores)
    weights = []
    for weight in (gate_weight[0].T, up_weight[0].T, down_weight[0]):
        weights += [weight, send(weight, dc=1)]

    exp = lax.axis_index("exp")
    spot = jnp.stack([exp % 4, exp // 4]).astype(jnp.int32)
    terms = attention(starts, spot, queries, paired, kept, weights[1::2])
    hidden, outgoing = dispatch(exchange(terms), residual, ln_gain[None], placing)
    mine = norm(lax.all_to_all(outgoing, "exp", 0, 0, tiled=True))

    across, back, ahead = send(mine, dz=1), send(mine, dy=1), send(mine, dy=-1)
    held = hold(weights, (mine,))
    up, down, over = join(
        (
            (9, ((0, 0, 0, 4), (2, 0, 4, 3), (2, 4, 7, 2))),
            (9, ((1, 4, 0, 4), (2, 0, 4, 3), (2, 4, 7, 2))),
            (6, ((0, 3, 0, 1), (0, 6, 1, 2), (1, 3, 3, 1), (1, 6, 4, 2))),
        ),
        back,
        ahead,
        across,
        after=(held[0],),
    )
    low, high, both = send(up, dy=1), send(down, dy=-1), send(over, dz=1)
    mine, across, back, ahead = expert(
        [mine, across, back, ahead],
        [[(k, 0, 8)] for k in range(4)],
        (8,) * 4,
        [[(k, 0, 8)] for k in range(4)],
        held,
    )
    up, down, over = join(
        (
            (3, ((0, 4, 0, 3),)),
            (2, ((1, 7, 0, 2),)),
            (3, ((0, 3, 0, 1), (1, 2, 1, 2))),
        ),
        low,
        high,
        both,
        after=(mine,),
    )
    across_far = [send(up, dy=1), send(down, dy=-1), send(over, dz=1)]
    far_low, far_high, far_rest, across_back, across_ahead, over = expert(
        [low, high, both],
        [
            [(0, 0, 4), (1, 0, 4)],
            [(0, 4, 3), (2, 0, 1), (0, 7, 2), (2, 1, 2)],
            [(1, 4, 3), (2, 3, 1), (1, 7, 2), (2, 4, 2)],
        ],
        (3, 2, 3, 5, 5, 6),
        [
            [(0, 0, 3), (2, 0, 1), (1, 0, 2), (2, 1, 2)],
            [(3, 0, 3), (5, 0, 1), (3, 3, 2), (5, 1, 2)],
            [(4, 0, 3), (5, 3, 1), (4, 3, 2), (5, 4, 2)],
        ],
        held,
    )
    low, high, over = send(far_low, dy=1), send(far_high, dy=-1), send(over, dz=1)
    last_low, last_high, last_over = expert(
        across_far,
        [[(0, 0, 3), (2, 0, 1), (1, 0, 2), (2, 1, 2)]],
        (3, 2, 3),
        [[(0, 0, 3), (2, 0, 1), (1, 0, 2), (2, 1, 2)]],
        held,
        (far_low,),
    )
    up, down = join(
        (
            (6, ((0, 0, 0, 5), (3, 0, 0, 3), (2, 0, 5, 1), (5, 0, 5, 1))),
            (7, ((1, 0, 0, 5), (4, 0, 3, 2), (2, 1, 5, 2), (5, 1, 5, 2))),
        ),
        across_ahead,
        across_back,
        far_rest,
        send(last_low, dy=1),
        send(last_high, dy=-1),
        send(last_over, dz=1),
        after=(low, high, over),
    )
    up, down = send(up, dy=1), send(down, dy=-1)
    across, ahead, back = join(
        (
            (
                8,
                ((0, 0, 0, 8), (3, 0, 0, 3), (3, 3, 4, 2), (4, 0, 0, 3), (4, 3, 4, 2)),
            ),
            (8, ((1, 0, 0, 8), (5, 0, 0, 3), (3, 5, 3, 1), (7, 3, 3, 1), (7, 4, 6, 2))),
            (8, ((2, 0, 0, 8), (6, 0, 4, 2), (4, 5, 6, 2), (7, 0, 3, 1), (7, 1, 6, 2))),
        ),
        across,
        ahead,
        back,
        up,
        down,
        low,
        high,
        over,
    )
    (result,) = join(
        ((8, tuple((number, 0, 0, 8) for number in range(4))),),
        mine,
        send(across, dz=1),
        send(ahead, dy=1),
        send(back, dy=-1),
    )
    outputs = lax.all_to_all(result, "exp", 0, 0, tiled=True)
    return combine(hidden, share_high, share_low, outputs)


def solution(mesh):
    return jax.shard_map(
        body,
        mesh=mesh,
        in_specs=(
            P("ctx", "exp"),
            P("ctx", "exp"),
            P("ctx", "exp"),
            P("ctx", "exp"),
            P("exp"),
            P("exp", None),
            P("exp", None, "ctx"),
            P("exp", None, "ctx"),
            P("exp", "ctx", None),
            P("ctx", None),
            P("ctx", None),
        ),
        out_specs=P("ctx", "exp"),
        check_vma=False,
    )
```

```python
import functools

import jax
import jax.numpy as jnp
from jax import lax
from jax.experimental import pallas as pl
from jax.experimental.pallas import tpu as pltpu
from jax.sharding import PartitionSpec as P

D = 6144
HD = 128
EXPERTS = 8
TOPK = 4
CAP = 80
AUX = 16
TOK = 128
SLICE = 768
SHARDS = 16
UNITS = 336
EPS = 1e-05
LOG2E = 1.4426950408889634
F32 = jnp.float32
BF16 = jnp.bfloat16
MIB = 1 << 20


def place(index):
    return index // 4, (index // 2) % 2, index % 2


def route(dy, dz, dc):
    pairs = []
    for index in range(SHARDS):
        y, z, c = place(index)
        pairs.append((index, (((y + dy) % 4) * 2 + (z + dz) % 2) * 2 + (c + dc) % 2))
    return pairs


def send(block, dy=0, dz=0, dc=0):
    return lax.ppermute(block, "ctx", route(dy, dz, dc))


def turn(block, dx=0, dz=0):
    pairs = [(j, (j // 4 + dz) % 2 * 4 + (j + dx) % 4) for j in range(EXPERTS)]
    return lax.ppermute(block, "exp", pairs)


WAYS = ((0, 0), (2, 1), (2, 0), (1, 1), (3, 1), (1, 0), (3, 0), (0, 1))


def exchange(blocks):
    return [blocks[0]] + [turn(block, *way) for block, way in zip(blocks[1:], WAYS[1:])]


def number_at(spot_ref, way, sign):
    x, z = spot_ref[0] + sign * way[0] + 4, spot_ref[1] + way[1]
    return lax.rem(z, 2) * 4 + lax.rem(x, 4)


def call(kernel, out_shape, limit, flops, moved, **kwargs):
    return pl.pallas_call(
        kernel,
        out_shape=out_shape,
        compiler_params=pltpu.CompilerParams(vmem_limit_bytes=limit * MIB),
        cost_estimate=pl.CostEstimate(flops=flops, bytes_accessed=moved, transcendentals=0),
        **kwargs,
    )


def shape(dims, dtype=BF16):
    return jax.ShapeDtypeStruct(dims, dtype)


def pieces(value):
    high = value.astype(BF16).astype(F32)
    left = value - high
    mid = left.astype(BF16).astype(F32)
    return high, mid, left - mid


def routing_kernel(ids_ref, scores_ref, placing_ref, high_ref, low_ref):
    ids = ids_ref[...]
    scores = scores_ref[...]
    total = scores[:, 0:1] + scores[:, 1:2] + scores[:, 2:3] + scores[:, 3:4]
    lanes = lax.broadcasted_iota(jnp.int32, (TOK, TOK), 1)
    rows = lax.broadcasted_iota(jnp.int32, (TOK, TOK), 0)
    named = [(lanes == ids[:, k : k + 1]).astype(F32) for k in range(TOPK)]
    member = named[0] + named[1] + named[2] + named[3]
    lower = (lanes < rows).astype(BF16)
    slots = jnp.dot(lower, member.astype(BF16), preferred_element_type=F32)
    wide = lax.broadcasted_iota(jnp.int32, (TOK, EXPERTS * TOK), 1)
    columns = lax.broadcasted_iota(jnp.int32, (TOK, EXPERTS * CAP), 1)
    placed = jnp.zeros((TOK, EXPERTS * TOK), F32)
    shares = jnp.zeros((TOK, EXPERTS * CAP), F32)
    for k in range(TOPK):
        slot = jnp.sum(named[k] * slots, axis=1, keepdims=True).astype(jnp.int32)
        expert = ids[:, k : k + 1]
        placed = placed + (wide == expert * TOK + slot).astype(F32)
        share = scores[:, k : k + 1] / total
        shares = shares + jnp.where(columns == expert * CAP + slot, share, 0.0)
    for e in range(EXPERTS):
        placing_ref[e] = placed[:, e * TOK : (e + 1) * TOK].T.astype(BF16)
    high = shares.astype(BF16)
    high_ref[...] = high
    low_ref[...] = (shares - high.astype(F32)).astype(BF16)


def routing(expert_ids, gate_scores):
    return call(
        routing_kernel,
        (
            shape((EXPERTS, TOK, TOK)),
            shape((TOK, EXPERTS * CAP)),
            shape((TOK, EXPERTS * CAP)),
        ),
        6,
        10**7,
        10**6,
    )(expert_ids, gate_scores)


def attention_kernel(starts_ref, spot_ref, queries_ref, paired_ref, weight_ref, *refs):
    terms, (held, ready) = refs[-2 - len(WAYS) : -2], refs[-2:]
    rows = SLICE // 4
    copies = [
        pltpu.make_async_copy(
            weight_ref.at[pl.ds(k * rows, rows)], held.at[pl.ds(k * rows, rows)], ready.at[k]
        )
        for k in range(4)
    ]
    for copy in copies:
        copy.start()
    keys = paired_ref[:, 0].reshape(SHARDS * TOK, HD)
    values = paired_ref[:, 1].reshape(SHARDS * TOK, HD)
    rows = lax.broadcasted_iota(jnp.int32, (TOK, TOK), 0)
    lanes = lax.broadcasted_iota(jnp.int32, (TOK, TOK), 1)
    ahead = rows - lanes + starts_ref[SHARDS]
    keep = jnp.concatenate([ahead >= starts_ref[b] for b in range(SHARDS)], axis=1)
    heads = []
    for h in range(queries_ref.shape[1] // HD):
        query = queries_ref[:, h * HD : (h + 1) * HD]
        scores = lax.dot_general(
            query, keys, (((1,), (1,)), ((), ())), preferred_element_type=F32
        )
        scores = jnp.where(keep, scores, -1e30)
        top = jnp.max(scores, axis=1, keepdims=True)
        expw = jnp.exp2((scores - top) * (HD**-0.5 * LOG2E))
        denom = jnp.sum(expw, axis=1, keepdims=True)
        summed = jnp.dot(expw.astype(BF16), values, preferred_element_type=F32)
        heads.append((summed / denom).astype(BF16))
    attended = jnp.concatenate(heads, axis=1)
    for copy in copies:
        copy.wait()
    for term, way in zip(terms, WAYS):
        first = pl.multiple_of(number_at(spot_ref, way, 1) * SLICE, 128)
        term[...] = jnp.dot(
            attended, held[:, pl.ds(first, SLICE)], preferred_element_type=F32
        ).astype(BF16)


def attention(starts, spot, queries, paired, weight, after):
    whole = pl.BlockSpec(memory_space=pltpu.VMEM)
    return call(
        attention_kernel,
        (shape((TOK, SLICE)),) * len(WAYS),
        48,
        2 * 10**9,
        13 * 10**6,
        in_specs=[pl.BlockSpec(memory_space=pltpu.SMEM)] * 2
        + [whole] * 2
        + [pl.BlockSpec(memory_space=pl.ANY)] * (1 + len(after)),
        out_specs=(whole,) * len(WAYS),
        scratch_shapes=[pltpu.VMEM((SLICE, D), BF16), pltpu.SemaphoreType.DMA((4,))],
    )(starts, spot, queries, paired, weight, *after)


def dispatch_kernel(residual_ref, gain_ref, placing_ref, *refs):
    terms, (hidden_ref, out_ref) = refs[: len(WAYS)], refs[len(WAYS) :]
    hidden = residual_ref[...].astype(F32)
    for term in terms:
        hidden = hidden + term[...].astype(F32)
    hidden_ref[...] = hidden
    mean = jnp.sum(hidden, axis=1, keepdims=True) * (1.0 / SLICE)
    apart = (hidden - mean).astype(BF16)
    lanes = lax.broadcasted_iota(jnp.int32, (TOK, TOK), 1)
    high, mid, low = pieces(mean)
    spread = jnp.where(lanes == 0, high, jnp.where(lanes == 1, mid, jnp.where(lanes == 2, low, 0.0)))
    means = spread.T[:AUX].astype(BF16)
    rows = lax.broadcasted_iota(jnp.int32, (AUX, SLICE), 0)
    high, mid, low = pieces(gain_ref[...])
    gains = jnp.where(rows == 3, high, jnp.where(rows == 4, mid, jnp.where(rows == 5, low, 0.0)))
    for e in range(EXPERTS):
        placing = placing_ref[e]
        out_ref[e, :CAP] = jnp.dot(placing[:CAP], apart, preferred_element_type=F32).astype(BF16)
        sent = lax.dot_general(means, placing, (((1,), (1,)), ((), ())), preferred_element_type=F32)
        out_ref[e, CAP:] = jnp.concatenate(
            [sent + gains[:, :TOK], gains[:, TOK:]], axis=1
        ).astype(BF16)


def dispatch(terms, residual, gain, placing):
    return call(
        dispatch_kernel,
        (shape((TOK, SLICE), F32), shape((EXPERTS, CAP + AUX, SLICE))),
        4,
        2 * 10**8,
        5 * 10**6,
    )(residual, gain, placing, *terms)


def norm_kernel(arrived_ref, out_ref):
    rows = lax.broadcasted_iota(jnp.int32, (CAP, TOK), 0)
    lanes = lax.broadcasted_iota(jnp.int32, (CAP, TOK), 1)
    diagonal = (rows == lanes).astype(BF16)
    means = []
    total = jnp.zeros((CAP, 1), F32)
    for j in range(EXPERTS):
        turned = lax.dot_general(
            diagonal, arrived_ref[j, CAP:, :TOK], (((1,), (1,)), ((), ())), preferred_element_type=F32
        )
        means.append(turned[:, 0:1] + turned[:, 1:2] + turned[:, 2:3])
        total = total + SLICE * means[j]
        total = total + jnp.sum(arrived_ref[j, :CAP].astype(F32), axis=1, keepdims=True)
    mean = total / D
    spread = jnp.zeros((CAP, 1), F32)
    for j in range(EXPERTS):
        apart = arrived_ref[j, :CAP].astype(F32) + (means[j] - mean)
        spread = spread + jnp.sum(apart * apart, axis=1, keepdims=True)
    scale = lax.rsqrt(spread / D + EPS)
    for j in range(EXPERTS):
        aux = arrived_ref[j, CAP:].astype(F32)
        gain = aux[3:4] + aux[4:5] + aux[5:6]
        apart = arrived_ref[j, :CAP].astype(F32) + (means[j] - mean)
        out_ref[j] = (apart * scale * gain).astype(BF16)


def norm(arrived):
    return call(norm_kernel, shape((EXPERTS, CAP, SLICE)), 4, 10**7, 2 * 10**6)(arrived)


HELD = 2 * UNITS


def hold_kernel(*refs):
    weights, held, ready = refs[:6], refs[-4:-1], refs[-1]
    copies = [
        pltpu.make_async_copy(
            weights[2 * number + core],
            held[number].at[pl.ds(core * UNITS, UNITS)],
            ready.at[2 * number + core],
        )
        for number in range(3)
        for core in range(2)
    ]
    for copy in copies:
        copy.start()
    for copy in copies:
        copy.wait()


def hold(weights, after):
    apart = pl.BlockSpec(memory_space=pl.ANY)
    return call(
        hold_kernel,
        tuple(pltpu.VMEM((HELD, D), BF16) for _ in range(3)),
        1,
        10**6,
        25 * 10**6,
        in_specs=[apart] * (6 + len(after)),
        out_specs=(pl.BlockSpec(memory_space=pltpu.VMEM),) * 3,
        scratch_shapes=[pltpu.SemaphoreType.DMA((6,))],
    )(*weights, *after)


def expert_kernel(pieces_in, pieces_out, n_in, n_out, *refs):
    xs, refs = refs[:n_in], refs[n_in:]
    gate_ref, up_ref, down_ref = refs[:3]
    outs, rows_ref = refs[len(refs) - n_out - 1 : -1], refs[-1]
    for shard, split in enumerate(pieces_in):
        block = 0
        for number, first, count in split:
            for k in range(first, first + count):
                rows_ref[
                    shard * CAP : (shard + 1) * CAP, block * SLICE : (block + 1) * SLICE
                ] = xs[number][k]
                block += 1
    turned = (((1,), (1,)), ((), ()))
    rows = rows_ref[...]
    gate = lax.dot_general(rows, gate_ref[...], turned, preferred_element_type=F32)
    up = lax.dot_general(rows, up_ref[...], turned, preferred_element_type=F32)
    act = (gate / (1.0 + jnp.exp(-gate)) * up).astype(BF16)
    for now in range(EXPERTS):
        result = jnp.dot(
            act, down_ref[:, now * SLICE : (now + 1) * SLICE], preferred_element_type=F32
        ).astype(BF16)
        for shard, split in enumerate(pieces_out):
            block = 0
            for number, first, count in split:
                if block <= now < block + count:
                    outs[number][first + now - block] = result[shard * CAP : (shard + 1) * CAP]
                block += count


def expert(arrays, pieces_in, sizes, pieces_out, held, after=()):
    total = CAP * len(pieces_in)
    whole = pl.BlockSpec(memory_space=pltpu.VMEM)
    return call(
        functools.partial(expert_kernel, pieces_in, pieces_out, len(arrays), len(sizes)),
        tuple(shape((size, CAP, SLICE)) for size in sizes),
        10,
        total * D * 2 * UNITS * 6,
        25 * 10**6,
        in_specs=[whole] * (len(arrays) + 3) + [pl.BlockSpec(memory_space=pl.ANY)] * len(after),
        out_specs=(whole,) * len(sizes),
        scratch_shapes=[pltpu.VMEM((total, D), BF16)],
    )(*arrays, *held, *after)


def join_kernel(plans, *refs):
    ins, outs = refs, refs[len(refs) - len(plans) :]
    for (size, terms), out in zip(plans, outs):
        for block in range(size):
            total = None
            for number, first, into, count in terms:
                if into <= block < into + count:
                    value = ins[number][first + block - into]
                    if total is None:
                        total = value
                    else:
                        total = total.astype(F32) + value.astype(F32)
            out[block] = total.astype(BF16)


def join(plans, *arrays, after=()):
    whole = pl.BlockSpec(memory_space=pltpu.VMEM)
    return call(
        functools.partial(join_kernel, plans),
        tuple(shape((size, CAP, SLICE)) for size, _ in plans),
        2,
        10**7,
        8 * 10**6,
        in_specs=[whole] * len(arrays) + [pl.BlockSpec(memory_space=pl.ANY)] * len(after),
        out_specs=(whole,) * len(plans),
    )(*arrays, *after)


def combine_kernel(hidden_ref, high_ref, low_ref, outputs_ref, mixed_ref):
    outputs = outputs_ref[...].reshape(EXPERTS * CAP, SLICE)
    moe = jnp.dot(high_ref[...], outputs, preferred_element_type=F32)
    moe += jnp.dot(low_ref[...], outputs, preferred_element_type=F32)
    mixed_ref[...] = (hidden_ref[...] + moe).astype(BF16)


def combine(hidden, high, low, outputs):
    return call(combine_kernel, shape((TOK, SLICE)), 4, 3 * 10**8, 2 * 10**6)(
        hidden, high, low, outputs
    )


def body(
    queries,
    keys,
    values,
    residual,
    ln_gain,
    out_weight,
    gate_weight,
    up_weight,
    down_weight,
    expert_ids,
    gate_scores,
):
    ctx = lax.axis_index("ctx")
    own = jnp.stack((keys, values))[None]
    first = jnp.concatenate([own, send(own, dz=1)])
    near = jnp.concatenate([first, send(first, dy=1), send(first, dy=-1), send(first, dy=2)])
    paired = jnp.concatenate([near, send(near, dc=1)])
    y, z, c = ctx // 4, (ctx // 2) % 2, ctx % 2
    starts = [
        ((((y - dy) % 4) * 2 + (z + dz) % 2) * 2 + (c + dc) % 2) * TOK
        for dc in (0, 1)
        for dy in (0, 1, -1, 2)
        for dz in (0, 1)
    ]
    starts = jnp.stack(starts + [ctx * TOK]).astype(jnp.int32)
    placing, share_high, share_low = routing(expert_ids, gate_scores)
    weights = []
    for weight in (gate_weight[0].T, up_weight[0].T, down_weight[0]):
        weights += [weight, send(weight, dc=1)]

    exp = lax.axis_index("exp")
    spot = jnp.stack([exp % 4, exp // 4]).astype(jnp.int32)
    terms = attention(starts, spot, queries, paired, out_weight, weights[1::2])
    hidden, outgoing = dispatch(exchange(terms), residual, ln_gain[None], placing)
    mine = norm(lax.all_to_all(outgoing, "exp", 0, 0, tiled=True))

    across, back, ahead = send(mine, dz=1), send(mine, dy=1), send(mine, dy=-1)
    held = hold(weights, (mine,))
    up, down, over = join(
        (
            (9, ((0, 0, 0, 4), (2, 0, 4, 3), (2, 4, 7, 2))),
            (9, ((1, 4, 0, 4), (2, 0, 4, 3), (2, 4, 7, 2))),
            (6, ((0, 3, 0, 1), (0, 6, 1, 2), (1, 3, 3, 1), (1, 6, 4, 2))),
        ),
        back,
        ahead,
        across,
        after=(held[0],),
    )
    low, high, both = send(up, dy=1), send(down, dy=-1), send(over, dz=1)
    mine, across, back, ahead = expert(
        [mine, across, back, ahead],
        [[(k, 0, 8)] for k in range(4)],
        (8,) * 4,
        [[(k, 0, 8)] for k in range(4)],
        held,
    )
    up, down, over = join(
        (
            (3, ((0, 4, 0, 3),)),
            (2, ((1, 7, 0, 2),)),
            (3, ((0, 3, 0, 1), (1, 2, 1, 2))),
        ),
        low,
        high,
        both,
        after=(mine,),
    )
    across_far = [send(up, dy=1), send(down, dy=-1), send(over, dz=1)]
    far_low, far_high, far_rest, across_back, across_ahead, over = expert(
        [low, high, both],
        [
            [(0, 0, 4), (1, 0, 4)],
            [(0, 4, 3), (2, 0, 1), (0, 7, 2), (2, 1, 2)],
            [(1, 4, 3), (2, 3, 1), (1, 7, 2), (2, 4, 2)],
        ],
        (3, 2, 3, 5, 5, 6),
        [
            [(0, 0, 3), (2, 0, 1), (1, 0, 2), (2, 1, 2)],
            [(3, 0, 3), (5, 0, 1), (3, 3, 2), (5, 1, 2)],
            [(4, 0, 3), (5, 3, 1), (4, 3, 2), (5, 4, 2)],
        ],
        held,
    )
    low, high, over = send(far_low, dy=1), send(far_high, dy=-1), send(over, dz=1)
    last_low, last_high, last_over = expert(
        across_far,
        [[(0, 0, 3), (2, 0, 1), (1, 0, 2), (2, 1, 2)]],
        (3, 2, 3),
        [[(0, 0, 3), (2, 0, 1), (1, 0, 2), (2, 1, 2)]],
        held,
        (far_low,),
    )
    up, down = join(
        (
            (6, ((0, 0, 0, 5), (3, 0, 0, 3), (2, 0, 5, 1), (5, 0, 5, 1))),
            (7, ((1, 0, 0, 5), (4, 0, 3, 2), (2, 1, 5, 2), (5, 1, 5, 2))),
        ),
        across_ahead,
        across_back,
        far_rest,
        send(last_low, dy=1),
        send(last_high, dy=-1),
        send(last_over, dz=1),
        after=(low, high, over),
    )
    up, down = send(up, dy=1), send(down, dy=-1)
    across, ahead, back = join(
        (
            (
                8,
                ((0, 0, 0, 8), (3, 0, 0, 3), (3, 3, 4, 2), (4, 0, 0, 3), (4, 3, 4, 2)),
            ),
            (8, ((1, 0, 0, 8), (5, 0, 0, 3), (3, 5, 3, 1), (7, 3, 3, 1), (7, 4, 6, 2))),
            (8, ((2, 0, 0, 8), (6, 0, 4, 2), (4, 5, 6, 2), (7, 0, 3, 1), (7, 1, 6, 2))),
        ),
        across,
        ahead,
        back,
        up,
        down,
        low,
        high,
        over,
    )
    (result,) = join(
        ((8, tuple((number, 0, 0, 8) for number in range(4))),),
        mine,
        send(across, dz=1),
        send(ahead, dy=1),
        send(back, dy=-1),
    )
    outputs = lax.all_to_all(result, "exp", 0, 0, tiled=True)
    return combine(hidden, share_high, share_low, outputs)


def solution(mesh):
    return jax.shard_map(
        body,
        mesh=mesh,
        in_specs=(
            P("ctx", "exp"),
            P("ctx", "exp"),
            P("ctx", "exp"),
            P("ctx", "exp"),
            P("exp"),
            P("exp", None),
            P("exp", None, "ctx"),
            P("exp", None, "ctx"),
            P("exp", "ctx", None),
            P("ctx", None),
            P("ctx", None),
        ),
        out_specs=P("ctx", "exp"),
        check_vma=False,
    )
```

```python
import functools

import jax
import jax.numpy as jnp
from jax import lax
from jax.experimental import pallas as pl
from jax.experimental.pallas import tpu as pltpu
from jax.sharding import PartitionSpec as P

D = 6144
HD = 128
EXPERTS = 8
TOPK = 4
CAP = 80
AUX = 16
TOK = 128
SLICE = 768
SHARDS = 16
UNITS = 336
EPS = 1e-05
LOG2E = 1.4426950408889634
F32 = jnp.float32
BF16 = jnp.bfloat16
MIB = 1 << 20


def place(index):
    return index // 4, (index // 2) % 2, index % 2


def route(dy, dz, dc):
    pairs = []
    for index in range(SHARDS):
        y, z, c = place(index)
        pairs.append((index, (((y + dy) % 4) * 2 + (z + dz) % 2) * 2 + (c + dc) % 2))
    return pairs


def send(block, dy=0, dz=0, dc=0):
    return lax.ppermute(block, "ctx", route(dy, dz, dc))


def call(kernel, out_shape, limit, flops, moved, **kwargs):
    return pl.pallas_call(
        kernel,
        out_shape=out_shape,
        compiler_params=pltpu.CompilerParams(vmem_limit_bytes=limit * MIB),
        cost_estimate=pl.CostEstimate(flops=flops, bytes_accessed=moved, transcendentals=0),
        **kwargs,
    )


def shape(dims, dtype=BF16):
    return jax.ShapeDtypeStruct(dims, dtype)


def pieces(value):
    high = value.astype(BF16).astype(F32)
    left = value - high
    mid = left.astype(BF16).astype(F32)
    return high, mid, left - mid


def routing_kernel(ids_ref, scores_ref, placing_ref, high_ref, low_ref):
    ids = ids_ref[...]
    scores = scores_ref[...]
    total = scores[:, 0:1] + scores[:, 1:2] + scores[:, 2:3] + scores[:, 3:4]
    lanes = lax.broadcasted_iota(jnp.int32, (TOK, TOK), 1)
    rows = lax.broadcasted_iota(jnp.int32, (TOK, TOK), 0)
    named = [(lanes == ids[:, k : k + 1]).astype(F32) for k in range(TOPK)]
    member = named[0] + named[1] + named[2] + named[3]
    lower = (lanes < rows).astype(BF16)
    slots = jnp.dot(lower, member.astype(BF16), preferred_element_type=F32)
    wide = lax.broadcasted_iota(jnp.int32, (TOK, EXPERTS * TOK), 1)
    columns = lax.broadcasted_iota(jnp.int32, (TOK, EXPERTS * CAP), 1)
    placed = jnp.zeros((TOK, EXPERTS * TOK), F32)
    shares = jnp.zeros((TOK, EXPERTS * CAP), F32)
    for k in range(TOPK):
        slot = jnp.sum(named[k] * slots, axis=1, keepdims=True).astype(jnp.int32)
        expert = ids[:, k : k + 1]
        placed = placed + (wide == expert * TOK + slot).astype(F32)
        share = scores[:, k : k + 1] / total
        shares = shares + jnp.where(columns == expert * CAP + slot, share, 0.0)
    for e in range(EXPERTS):
        placing_ref[e] = placed[:, e * TOK : (e + 1) * TOK].T.astype(BF16)
    high = shares.astype(BF16)
    high_ref[...] = high
    low_ref[...] = (shares - high.astype(F32)).astype(BF16)


def routing(expert_ids, gate_scores):
    return call(
        routing_kernel,
        (
            shape((EXPERTS, TOK, TOK)),
            shape((TOK, EXPERTS * CAP)),
            shape((TOK, EXPERTS * CAP)),
        ),
        6,
        10**7,
        10**6,
    )(expert_ids, gate_scores)


def attention_kernel(starts_ref, queries_ref, paired_ref, weight_ref, terms_ref, held, ready):
    rows = SLICE // 4
    copies = [
        pltpu.make_async_copy(
            weight_ref.at[pl.ds(k * rows, rows)], held.at[pl.ds(k * rows, rows)], ready.at[k]
        )
        for k in range(4)
    ]
    for copy in copies:
        copy.start()
    keys = paired_ref[:, 0].reshape(SHARDS * TOK, HD)
    values = paired_ref[:, 1].reshape(SHARDS * TOK, HD)
    rows = lax.broadcasted_iota(jnp.int32, (TOK, TOK), 0)
    lanes = lax.broadcasted_iota(jnp.int32, (TOK, TOK), 1)
    ahead = rows - lanes + starts_ref[SHARDS]
    keep = jnp.concatenate([ahead >= starts_ref[b] for b in range(SHARDS)], axis=1)
    heads = []
    for h in range(queries_ref.shape[1] // HD):
        query = queries_ref[:, h * HD : (h + 1) * HD]
        scores = lax.dot_general(
            query, keys, (((1,), (1,)), ((), ())), preferred_element_type=F32
        )
        scores = jnp.where(keep, scores, -1e30)
        top = jnp.max(scores, axis=1, keepdims=True)
        expw = jnp.exp2((scores - top) * (HD**-0.5 * LOG2E))
        denom = jnp.sum(expw, axis=1, keepdims=True)
        summed = jnp.dot(expw.astype(BF16), values, preferred_element_type=F32)
        heads.append((summed / denom).astype(BF16))
    attended = jnp.concatenate(heads, axis=1)
    for copy in copies:
        copy.wait()
    for j in range(EXPERTS):
        terms_ref[j] = jnp.dot(
            attended, held[:, j * SLICE : (j + 1) * SLICE], preferred_element_type=F32
        ).astype(BF16)


def attention(starts, queries, paired, weight):
    whole = pl.BlockSpec(memory_space=pltpu.VMEM)
    return call(
        attention_kernel,
        shape((EXPERTS, TOK, SLICE)),
        48,
        2 * 10**9,
        13 * 10**6,
        in_specs=[pl.BlockSpec(memory_space=pltpu.SMEM), whole, whole]
        + [pl.BlockSpec(memory_space=pl.ANY)],
        out_specs=whole,
        scratch_shapes=[pltpu.VMEM((SLICE, D), BF16), pltpu.SemaphoreType.DMA((4,))],
    )(starts, queries, paired, weight)


def dispatch_kernel(terms_ref, residual_ref, gain_ref, placing_ref, hidden_ref, out_ref):
    hidden = residual_ref[...].astype(F32)
    for j in range(EXPERTS):
        hidden = hidden + terms_ref[j].astype(F32)
    hidden_ref[...] = hidden
    mean = jnp.sum(hidden, axis=1, keepdims=True) * (1.0 / SLICE)
    apart = (hidden - mean).astype(BF16)
    lanes = lax.broadcasted_iota(jnp.int32, (TOK, TOK), 1)
    high, mid, low = pieces(mean)
    spread = jnp.where(lanes == 0, high, jnp.where(lanes == 1, mid, jnp.where(lanes == 2, low, 0.0)))
    means = spread.T[:AUX].astype(BF16)
    rows = lax.broadcasted_iota(jnp.int32, (AUX, SLICE), 0)
    high, mid, low = pieces(gain_ref[...])
    gains = jnp.where(rows == 3, high, jnp.where(rows == 4, mid, jnp.where(rows == 5, low, 0.0)))
    for e in range(EXPERTS):
        placing = placing_ref[e]
        out_ref[e, :CAP] = jnp.dot(placing[:CAP], apart, preferred_element_type=F32).astype(BF16)
        sent = lax.dot_general(means, placing, (((1,), (1,)), ((), ())), preferred_element_type=F32)
        out_ref[e, CAP:] = jnp.concatenate(
            [sent + gains[:, :TOK], gains[:, TOK:]], axis=1
        ).astype(BF16)


def dispatch(terms, residual, gain, placing):
    return call(
        dispatch_kernel,
        (shape((TOK, SLICE), F32), shape((EXPERTS, CAP + AUX, SLICE))),
        4,
        2 * 10**8,
        5 * 10**6,
    )(terms, residual, gain, placing)


def norm_kernel(arrived_ref, *refs):
    out_ref = refs[-1]
    rows = lax.broadcasted_iota(jnp.int32, (CAP, TOK), 0)
    lanes = lax.broadcasted_iota(jnp.int32, (CAP, TOK), 1)
    diagonal = (rows == lanes).astype(BF16)
    means = []
    total = jnp.zeros((CAP, 1), F32)
    for j in range(EXPERTS):
        turned = lax.dot_general(
            diagonal, arrived_ref[j, CAP:, :TOK], (((1,), (1,)), ((), ())), preferred_element_type=F32
        )
        means.append(turned[:, 0:1] + turned[:, 1:2] + turned[:, 2:3])
        total = total + SLICE * means[j]
        total = total + jnp.sum(arrived_ref[j, :CAP].astype(F32), axis=1, keepdims=True)
    mean = total / D
    spread = jnp.zeros((CAP, 1), F32)
    for j in range(EXPERTS):
        apart = arrived_ref[j, :CAP].astype(F32) + (means[j] - mean)
        spread = spread + jnp.sum(apart * apart, axis=1, keepdims=True)
    scale = lax.rsqrt(spread / D + EPS)
    for j in range(EXPERTS):
        aux = arrived_ref[j, CAP:].astype(F32)
        gain = aux[3:4] + aux[4:5] + aux[5:6]
        apart = arrived_ref[j, :CAP].astype(F32) + (means[j] - mean)
        out_ref[j] = (apart * scale * gain).astype(BF16)


def norm(arrived, after):
    return call(
        norm_kernel,
        shape((EXPERTS, CAP, SLICE)),
        4,
        10**7,
        2 * 10**6,
        in_specs=[pl.BlockSpec(memory_space=pltpu.VMEM)]
        + [pl.BlockSpec(memory_space=pl.ANY)] * len(after),
    )(arrived, *after)


HELD = 2 * UNITS


def hold_kernel(*refs):
    weights, held, ready = refs[:6], refs[-4:-1], refs[-1]
    copies = [
        pltpu.make_async_copy(
            weights[2 * number + core],
            held[number].at[pl.ds(core * UNITS, UNITS)],
            ready.at[2 * number + core],
        )
        for number in range(3)
        for core in range(2)
    ]
    for copy in copies:
        copy.start()
    for copy in copies:
        copy.wait()


def hold(weights, after):
    apart = pl.BlockSpec(memory_space=pl.ANY)
    return call(
        hold_kernel,
        tuple(pltpu.VMEM((HELD, D), BF16) for _ in range(3)),
        1,
        10**6,
        25 * 10**6,
        in_specs=[apart] * (6 + len(after)),
        out_specs=(pl.BlockSpec(memory_space=pltpu.VMEM),) * 3,
        scratch_shapes=[pltpu.SemaphoreType.DMA((6,))],
    )(*weights, *after)


def expert_kernel(pieces_in, pieces_out, n_in, n_out, *refs):
    xs, refs = refs[:n_in], refs[n_in:]
    gate_ref, up_ref, down_ref = refs[:3]
    outs, rows_ref = refs[len(refs) - n_out - 1 : -1], refs[-1]
    for shard, split in enumerate(pieces_in):
        block = 0
        for number, first, count in split:
            for k in range(first, first + count):
                rows_ref[
                    shard * CAP : (shard + 1) * CAP, block * SLICE : (block + 1) * SLICE
                ] = xs[number][k]
                block += 1
    turned = (((1,), (1,)), ((), ()))
    rows = rows_ref[...]
    gate = lax.dot_general(rows, gate_ref[...], turned, preferred_element_type=F32)
    up = lax.dot_general(rows, up_ref[...], turned, preferred_element_type=F32)
    act = (gate / (1.0 + jnp.exp(-gate)) * up).astype(BF16)
    for now in range(EXPERTS):
        result = jnp.dot(
            act, down_ref[:, now * SLICE : (now + 1) * SLICE], preferred_element_type=F32
        ).astype(BF16)
        for shard, split in enumerate(pieces_out):
            block = 0
            for number, first, count in split:
                if block <= now < block + count:
                    outs[number][first + now - block] = result[shard * CAP : (shard + 1) * CAP]
                block += count


def expert(arrays, pieces_in, sizes, pieces_out, held, after=()):
    total = CAP * len(pieces_in)
    whole = pl.BlockSpec(memory_space=pltpu.VMEM)
    return call(
        functools.partial(expert_kernel, pieces_in, pieces_out, len(arrays), len(sizes)),
        tuple(shape((size, CAP, SLICE)) for size in sizes),
        10,
        total * D * 2 * UNITS * 6,
        25 * 10**6,
        in_specs=[whole] * (len(arrays) + 3) + [pl.BlockSpec(memory_space=pl.ANY)] * len(after),
        out_specs=(whole,) * len(sizes),
        scratch_shapes=[pltpu.VMEM((total, D), BF16)],
    )(*arrays, *held, *after)


def join_kernel(plans, *refs):
    ins, outs = refs, refs[len(refs) - len(plans) :]
    for (size, terms), out in zip(plans, outs):
        for block in range(size):
            total = None
            for number, first, into, count in terms:
                if into <= block < into + count:
                    value = ins[number][first + block - into]
                    if total is None:
                        total = value
                    else:
                        total = total.astype(F32) + value.astype(F32)
            out[block] = total.astype(BF16)


def join(plans, *arrays, after=()):
    whole = pl.BlockSpec(memory_space=pltpu.VMEM)
    return call(
        functools.partial(join_kernel, plans),
        tuple(shape((size, CAP, SLICE)) for size, _ in plans),
        2,
        10**7,
        8 * 10**6,
        in_specs=[whole] * len(arrays) + [pl.BlockSpec(memory_space=pl.ANY)] * len(after),
        out_specs=(whole,) * len(plans),
    )(*arrays, *after)


def combine_kernel(hidden_ref, high_ref, low_ref, outputs_ref, mixed_ref):
    outputs = outputs_ref[...].reshape(EXPERTS * CAP, SLICE)
    moe = jnp.dot(high_ref[...], outputs, preferred_element_type=F32)
    moe += jnp.dot(low_ref[...], outputs, preferred_element_type=F32)
    mixed_ref[...] = (hidden_ref[...] + moe).astype(BF16)


def combine(hidden, high, low, outputs):
    return call(combine_kernel, shape((TOK, SLICE)), 4, 3 * 10**8, 2 * 10**6)(
        hidden, high, low, outputs
    )


def body(
    queries,
    keys,
    values,
    residual,
    ln_gain,
    out_weight,
    gate_weight,
    up_weight,
    down_weight,
    expert_ids,
    gate_scores,
):
    ctx = lax.axis_index("ctx")
    own = jnp.stack((keys, values))[None]
    first = jnp.concatenate([own, send(own, dz=1)])
    near = jnp.concatenate([first, send(first, dy=1), send(first, dy=-1), send(first, dy=2)])
    paired = jnp.concatenate([near, send(near, dc=1)])
    y, z, c = ctx // 4, (ctx // 2) % 2, ctx % 2
    starts = [
        ((((y - dy) % 4) * 2 + (z + dz) % 2) * 2 + (c + dc) % 2) * TOK
        for dc in (0, 1)
        for dy in (0, 1, -1, 2)
        for dz in (0, 1)
    ]
    starts = jnp.stack(starts + [ctx * TOK]).astype(jnp.int32)
    placing, share_high, share_low = routing(expert_ids, gate_scores)
    weights = []
    for weight in (gate_weight[0].T, up_weight[0].T, down_weight[0]):
        weights += [weight, send(weight, dc=1)]

    terms = attention(starts, queries, paired, out_weight)
    terms = lax.all_to_all(terms, "exp", 0, 0, tiled=True)
    hidden, outgoing = dispatch(terms, residual, ln_gain[None], placing)
    mine = norm(lax.all_to_all(outgoing, "exp", 0, 0, tiled=True), weights[5:])

    across, back, ahead = send(mine, dz=1), send(mine, dy=1), send(mine, dy=-1)
    held = hold(weights, (mine,))
    up, down, over = join(
        (
            (9, ((0, 0, 0, 4), (2, 0, 4, 3), (2, 4, 7, 2))),
            (9, ((1, 4, 0, 4), (2, 0, 4, 3), (2, 4, 7, 2))),
            (6, ((0, 3, 0, 1), (0, 6, 1, 2), (1, 3, 3, 1), (1, 6, 4, 2))),
        ),
        back,
        ahead,
        across,
        after=(held[0],),
    )
    low, high, both = send(up, dy=1), send(down, dy=-1), send(over, dz=1)
    mine, across, back, ahead = expert(
        [mine, across, back, ahead],
        [[(k, 0, 8)] for k in range(4)],
        (8,) * 4,
        [[(k, 0, 8)] for k in range(4)],
        held,
    )
    up, down, over = join(
        (
            (3, ((0, 4, 0, 3),)),
            (2, ((1, 7, 0, 2),)),
            (3, ((0, 3, 0, 1), (1, 2, 1, 2))),
        ),
        low,
        high,
        both,
        after=(mine,),
    )
    across_far = [send(up, dy=1), send(down, dy=-1), send(over, dz=1)]
    far_low, far_high, far_rest, across_back, across_ahead, over = expert(
        [low, high, both],
        [
            [(0, 0, 4), (1, 0, 4)],
            [(0, 4, 3), (2, 0, 1), (0, 7, 2), (2, 1, 2)],
            [(1, 4, 3), (2, 3, 1), (1, 7, 2), (2, 4, 2)],
        ],
        (3, 2, 3, 5, 5, 6),
        [
            [(0, 0, 3), (2, 0, 1), (1, 0, 2), (2, 1, 2)],
            [(3, 0, 3), (5, 0, 1), (3, 3, 2), (5, 1, 2)],
            [(4, 0, 3), (5, 3, 1), (4, 3, 2), (5, 4, 2)],
        ],
        held,
    )
    low, high, over = send(far_low, dy=1), send(far_high, dy=-1), send(over, dz=1)
    last_low, last_high, last_over = expert(
        across_far,
        [[(0, 0, 3), (2, 0, 1), (1, 0, 2), (2, 1, 2)]],
        (3, 2, 3),
        [[(0, 0, 3), (2, 0, 1), (1, 0, 2), (2, 1, 2)]],
        held,
        (far_low,),
    )
    up, down = join(
        (
            (6, ((0, 0, 0, 5), (3, 0, 0, 3), (2, 0, 5, 1), (5, 0, 5, 1))),
            (7, ((1, 0, 0, 5), (4, 0, 3, 2), (2, 1, 5, 2), (5, 1, 5, 2))),
        ),
        across_ahead,
        across_back,
        far_rest,
        send(last_low, dy=1),
        send(last_high, dy=-1),
        send(last_over, dz=1),
        after=(low, high, over),
    )
    up, down = send(up, dy=1), send(down, dy=-1)
    across, ahead, back = join(
        (
            (
                8,
                ((0, 0, 0, 8), (3, 0, 0, 3), (3, 3, 4, 2), (4, 0, 0, 3), (4, 3, 4, 2)),
            ),
            (8, ((1, 0, 0, 8), (5, 0, 0, 3), (3, 5, 3, 1), (7, 3, 3, 1), (7, 4, 6, 2))),
            (8, ((2, 0, 0, 8), (6, 0, 4, 2), (4, 5, 6, 2), (7, 0, 3, 1), (7, 1, 6, 2))),
        ),
        across,
        ahead,
        back,
        up,
        down,
        low,
        high,
        over,
    )
    (result,) = join(
        ((8, tuple((number, 0, 0, 8) for number in range(4))),),
        mine,
        send(across, dz=1),
        send(ahead, dy=1),
        send(back, dy=-1),
    )
    outputs = lax.all_to_all(result, "exp", 0, 0, tiled=True)
    return combine(hidden, share_high, share_low, outputs)


def solution(mesh):
    return jax.shard_map(
        body,
        mesh=mesh,
        in_specs=(
            P("ctx", "exp"),
            P("ctx", "exp"),
            P("ctx", "exp"),
            P("ctx", "exp"),
            P("exp"),
            P("exp", None),
            P("exp", None, "ctx"),
            P("exp", None, "ctx"),
            P("exp", "ctx", None),
            P("ctx", None),
            P("ctx", None),
        ),
        out_specs=P("ctx", "exp"),
        check_vma=False,
    )
```

```python
import functools

import jax
import jax.numpy as jnp
from jax import lax
from jax.experimental import pallas as pl
from jax.experimental.pallas import tpu as pltpu
from jax.sharding import PartitionSpec as P

D = 6144
HD = 128
EXPERTS = 8
TOPK = 4
CAP = 80
AUX = 16
TOK = 128
SLICE = 768
SHARDS = 16
UNITS = 336
EPS = 1e-05
LOG2E = 1.4426950408889634
F32 = jnp.float32
BF16 = jnp.bfloat16
MIB = 1 << 20


def place(index):
    return index // 4, (index // 2) % 2, index % 2


def route(dy, dz, dc):
    pairs = []
    for index in range(SHARDS):
        y, z, c = place(index)
        pairs.append((index, (((y + dy) % 4) * 2 + (z + dz) % 2) * 2 + (c + dc) % 2))
    return pairs


def send(block, dy=0, dz=0, dc=0):
    return lax.ppermute(block, "ctx", route(dy, dz, dc))


def call(kernel, out_shape, limit, flops, moved, **kwargs):
    return pl.pallas_call(
        kernel,
        out_shape=out_shape,
        compiler_params=pltpu.CompilerParams(vmem_limit_bytes=limit * MIB),
        cost_estimate=pl.CostEstimate(flops=flops, bytes_accessed=moved, transcendentals=0),
        **kwargs,
    )


def shape(dims, dtype=BF16):
    return jax.ShapeDtypeStruct(dims, dtype)


def pieces(value):
    high = value.astype(BF16).astype(F32)
    left = value - high
    mid = left.astype(BF16).astype(F32)
    return high, mid, left - mid


def routing_kernel(ids_ref, scores_ref, placing_ref, high_ref, low_ref):
    ids = ids_ref[...]
    scores = scores_ref[...]
    total = scores[:, 0:1] + scores[:, 1:2] + scores[:, 2:3] + scores[:, 3:4]
    lanes = lax.broadcasted_iota(jnp.int32, (TOK, TOK), 1)
    rows = lax.broadcasted_iota(jnp.int32, (TOK, TOK), 0)
    named = [(lanes == ids[:, k : k + 1]).astype(F32) for k in range(TOPK)]
    member = named[0] + named[1] + named[2] + named[3]
    lower = (lanes < rows).astype(BF16)
    slots = jnp.dot(lower, member.astype(BF16), preferred_element_type=F32)
    wide = lax.broadcasted_iota(jnp.int32, (TOK, EXPERTS * TOK), 1)
    columns = lax.broadcasted_iota(jnp.int32, (TOK, EXPERTS * CAP), 1)
    placed = jnp.zeros((TOK, EXPERTS * TOK), F32)
    shares = jnp.zeros((TOK, EXPERTS * CAP), F32)
    for k in range(TOPK):
        slot = jnp.sum(named[k] * slots, axis=1, keepdims=True).astype(jnp.int32)
        expert = ids[:, k : k + 1]
        placed = placed + (wide == expert * TOK + slot).astype(F32)
        share = scores[:, k : k + 1] / total
        shares = shares + jnp.where(columns == expert * CAP + slot, share, 0.0)
    for e in range(EXPERTS):
        placing_ref[e] = placed[:, e * TOK : (e + 1) * TOK].T.astype(BF16)
    high = shares.astype(BF16)
    high_ref[...] = high
    low_ref[...] = (shares - high.astype(F32)).astype(BF16)


def routing(expert_ids, gate_scores):
    return call(
        routing_kernel,
        (
            shape((EXPERTS, TOK, TOK)),
            shape((TOK, EXPERTS * CAP)),
            shape((TOK, EXPERTS * CAP)),
        ),
        6,
        10**7,
        10**6,
    )(expert_ids, gate_scores)


def attention_kernel(starts_ref, queries_ref, paired_ref, weight_ref, terms_ref, held, ready):
    rows = SLICE // 4
    copies = [
        pltpu.make_async_copy(
            weight_ref.at[pl.ds(k * rows, rows)], held.at[pl.ds(k * rows, rows)], ready.at[k]
        )
        for k in range(4)
    ]
    for copy in copies:
        copy.start()
    keys = paired_ref[:, 0].reshape(SHARDS * TOK, HD)
    values = paired_ref[:, 1].reshape(SHARDS * TOK, HD)
    rows = lax.broadcasted_iota(jnp.int32, (TOK, TOK), 0)
    lanes = lax.broadcasted_iota(jnp.int32, (TOK, TOK), 1)
    ahead = rows - lanes + starts_ref[SHARDS]
    keep = jnp.concatenate([ahead >= starts_ref[b] for b in range(SHARDS)], axis=1)
    heads = []
    for h in range(queries_ref.shape[1] // HD):
        query = queries_ref[:, h * HD : (h + 1) * HD]
        scores = lax.dot_general(
            query, keys, (((1,), (1,)), ((), ())), preferred_element_type=F32
        )
        scores = jnp.where(keep, scores, -1e30)
        top = jnp.max(scores, axis=1, keepdims=True)
        expw = jnp.exp2((scores - top) * (HD**-0.5 * LOG2E))
        denom = jnp.sum(expw, axis=1, keepdims=True)
        summed = jnp.dot(expw.astype(BF16), values, preferred_element_type=F32)
        heads.append((summed / denom).astype(BF16))
    attended = jnp.concatenate(heads, axis=1)
    for copy in copies:
        copy.wait()
    for j in range(EXPERTS):
        terms_ref[j] = jnp.dot(
            attended, held[:, j * SLICE : (j + 1) * SLICE], preferred_element_type=F32
        ).astype(BF16)


def attention(starts, queries, paired, weight):
    whole = pl.BlockSpec(memory_space=pltpu.VMEM)
    return call(
        attention_kernel,
        shape((EXPERTS, TOK, SLICE)),
        48,
        2 * 10**9,
        13 * 10**6,
        in_specs=[pl.BlockSpec(memory_space=pltpu.SMEM), whole, whole]
        + [pl.BlockSpec(memory_space=pl.ANY)],
        out_specs=whole,
        scratch_shapes=[pltpu.VMEM((SLICE, D), BF16), pltpu.SemaphoreType.DMA((4,))],
    )(starts, queries, paired, weight)


def dispatch_kernel(terms_ref, residual_ref, gain_ref, placing_ref, hidden_ref, out_ref):
    hidden = residual_ref[...].astype(F32)
    for j in range(EXPERTS):
        hidden = hidden + terms_ref[j].astype(F32)
    hidden_ref[...] = hidden
    mean = jnp.sum(hidden, axis=1, keepdims=True) * (1.0 / SLICE)
    apart = (hidden - mean).astype(BF16)
    lanes = lax.broadcasted_iota(jnp.int32, (TOK, TOK), 1)
    high, mid, low = pieces(mean)
    spread = jnp.where(lanes == 0, high, jnp.where(lanes == 1, mid, jnp.where(lanes == 2, low, 0.0)))
    means = spread.T[:AUX].astype(BF16)
    rows = lax.broadcasted_iota(jnp.int32, (AUX, SLICE), 0)
    high, mid, low = pieces(gain_ref[...])
    gains = jnp.where(rows == 3, high, jnp.where(rows == 4, mid, jnp.where(rows == 5, low, 0.0)))
    for e in range(EXPERTS):
        placing = placing_ref[e]
        out_ref[e, :CAP] = jnp.dot(placing[:CAP], apart, preferred_element_type=F32).astype(BF16)
        sent = lax.dot_general(means, placing, (((1,), (1,)), ((), ())), preferred_element_type=F32)
        out_ref[e, CAP:] = jnp.concatenate(
            [sent + gains[:, :TOK], gains[:, TOK:]], axis=1
        ).astype(BF16)


def dispatch(terms, residual, gain, placing):
    return call(
        dispatch_kernel,
        (shape((TOK, SLICE), F32), shape((EXPERTS, CAP + AUX, SLICE))),
        4,
        2 * 10**8,
        5 * 10**6,
    )(terms, residual, gain, placing)


def norm_kernel(arrived_ref, *refs):
    out_ref = refs[-1]
    rows = lax.broadcasted_iota(jnp.int32, (CAP, TOK), 0)
    lanes = lax.broadcasted_iota(jnp.int32, (CAP, TOK), 1)
    diagonal = (rows == lanes).astype(BF16)
    means = []
    total = jnp.zeros((CAP, 1), F32)
    for j in range(EXPERTS):
        turned = lax.dot_general(
            diagonal, arrived_ref[j, CAP:, :TOK], (((1,), (1,)), ((), ())), preferred_element_type=F32
        )
        means.append(turned[:, 0:1] + turned[:, 1:2] + turned[:, 2:3])
        total = total + SLICE * means[j]
        total = total + jnp.sum(arrived_ref[j, :CAP].astype(F32), axis=1, keepdims=True)
    mean = total / D
    spread = jnp.zeros((CAP, 1), F32)
    for j in range(EXPERTS):
        apart = arrived_ref[j, :CAP].astype(F32) + (means[j] - mean)
        spread = spread + jnp.sum(apart * apart, axis=1, keepdims=True)
    scale = lax.rsqrt(spread / D + EPS)
    for j in range(EXPERTS):
        aux = arrived_ref[j, CAP:].astype(F32)
        gain = aux[3:4] + aux[4:5] + aux[5:6]
        apart = arrived_ref[j, :CAP].astype(F32) + (means[j] - mean)
        out_ref[j] = (apart * scale * gain).astype(BF16)


def norm(arrived, after):
    return call(
        norm_kernel,
        shape((EXPERTS, CAP, SLICE)),
        4,
        10**7,
        2 * 10**6,
        in_specs=[pl.BlockSpec(memory_space=pltpu.VMEM)]
        + [pl.BlockSpec(memory_space=pl.ANY)] * len(after),
    )(arrived, *after)


HELD = 2 * UNITS


def hold_kernel(*refs):
    weights, held, ready = refs[:6], refs[-4:-1], refs[-1]
    copies = [
        pltpu.make_async_copy(
            weights[2 * number + core],
            held[number].at[pl.ds(core * UNITS, UNITS)],
            ready.at[2 * number + core],
        )
        for number in range(3)
        for core in range(2)
    ]
    for copy in copies:
        copy.start()
    for copy in copies:
        copy.wait()


def hold(weights, after):
    apart = pl.BlockSpec(memory_space=pl.ANY)
    return call(
        hold_kernel,
        tuple(pltpu.VMEM((HELD, D), BF16) for _ in range(3)),
        1,
        10**6,
        25 * 10**6,
        in_specs=[apart] * (6 + len(after)),
        out_specs=(pl.BlockSpec(memory_space=pltpu.VMEM),) * 3,
        scratch_shapes=[pltpu.SemaphoreType.DMA((6,))],
    )(*weights, *after)


def expert_kernel(pieces_in, pieces_out, n_in, n_out, *refs):
    xs, refs = refs[:n_in], refs[n_in:]
    gate_ref, up_ref, down_ref = refs[:3]
    outs, rows_ref = refs[len(refs) - n_out - 1 : -1], refs[-1]
    for shard, split in enumerate(pieces_in):
        block = 0
        for number, first, count in split:
            for k in range(first, first + count):
                rows_ref[
                    shard * CAP : (shard + 1) * CAP, block * SLICE : (block + 1) * SLICE
                ] = xs[number][k]
                block += 1
    turned = (((1,), (1,)), ((), ()))
    rows = rows_ref[...]
    gate = lax.dot_general(rows, gate_ref[...], turned, preferred_element_type=F32)
    up = lax.dot_general(rows, up_ref[...], turned, preferred_element_type=F32)
    act = (gate / (1.0 + jnp.exp(-gate)) * up).astype(BF16)
    for now in range(EXPERTS):
        result = jnp.dot(
            act, down_ref[:, now * SLICE : (now + 1) * SLICE], preferred_element_type=F32
        ).astype(BF16)
        for shard, split in enumerate(pieces_out):
            block = 0
            for number, first, count in split:
                if block <= now < block + count:
                    outs[number][first + now - block] = result[shard * CAP : (shard + 1) * CAP]
                block += count


def expert(arrays, pieces_in, sizes, pieces_out, held, after=()):
    total = CAP * len(pieces_in)
    whole = pl.BlockSpec(memory_space=pltpu.VMEM)
    return call(
        functools.partial(expert_kernel, pieces_in, pieces_out, len(arrays), len(sizes)),
        tuple(shape((size, CAP, SLICE)) for size in sizes),
        10,
        total * D * 2 * UNITS * 6,
        25 * 10**6,
        in_specs=[whole] * (len(arrays) + 3) + [pl.BlockSpec(memory_space=pl.ANY)] * len(after),
        out_specs=(whole,) * len(sizes),
        scratch_shapes=[pltpu.VMEM((total, D), BF16)],
    )(*arrays, *held, *after)


def join_kernel(plans, *refs):
    ins, outs = refs, refs[len(refs) - len(plans) :]
    for (size, terms), out in zip(plans, outs):
        for block in range(size):
            total = None
            for number, first, into, count in terms:
                if into <= block < into + count:
                    value = ins[number][first + block - into]
                    if total is None:
                        total = value
                    else:
                        total = total.astype(F32) + value.astype(F32)
            out[block] = total.astype(BF16)


def join(plans, *arrays, after=()):
    whole = pl.BlockSpec(memory_space=pltpu.VMEM)
    return call(
        functools.partial(join_kernel, plans),
        tuple(shape((size, CAP, SLICE)) for size, _ in plans),
        2,
        10**7,
        8 * 10**6,
        in_specs=[whole] * len(arrays) + [pl.BlockSpec(memory_space=pl.ANY)] * len(after),
        out_specs=(whole,) * len(plans),
    )(*arrays, *after)


def combine_kernel(hidden_ref, high_ref, low_ref, outputs_ref, mixed_ref):
    outputs = outputs_ref[...].reshape(EXPERTS * CAP, SLICE)
    moe = jnp.dot(high_ref[...], outputs, preferred_element_type=F32)
    moe += jnp.dot(low_ref[...], outputs, preferred_element_type=F32)
    mixed_ref[...] = (hidden_ref[...] + moe).astype(BF16)


def combine(hidden, high, low, outputs):
    return call(combine_kernel, shape((TOK, SLICE)), 4, 3 * 10**8, 2 * 10**6)(
        hidden, high, low, outputs
    )


def body(
    queries,
    keys,
    values,
    residual,
    ln_gain,
    out_weight,
    gate_weight,
    up_weight,
    down_weight,
    expert_ids,
    gate_scores,
):
    ctx = lax.axis_index("ctx")
    own = jnp.stack((keys, values))[None]
    first = jnp.concatenate([own, send(own, dz=1)])
    near = jnp.concatenate([first, send(first, dy=1), send(first, dy=-1), send(first, dy=2)])
    paired = jnp.concatenate([near, send(near, dc=1)])
    y, z, c = ctx // 4, (ctx // 2) % 2, ctx % 2
    starts = [
        ((((y - dy) % 4) * 2 + (z + dz) % 2) * 2 + (c + dc) % 2) * TOK
        for dc in (0, 1)
        for dy in (0, 1, -1, 2)
        for dz in (0, 1)
    ]
    starts = jnp.stack(starts + [ctx * TOK]).astype(jnp.int32)
    placing, share_high, share_low = routing(expert_ids, gate_scores)
    weights = []
    for weight in (gate_weight[0].T, up_weight[0].T, down_weight[0]):
        weights += [weight, send(weight, dc=1)]

    terms = attention(starts, queries, paired, out_weight)
    terms = lax.all_to_all(terms, "exp", 0, 0, tiled=True)
    hidden, outgoing = dispatch(terms, residual, ln_gain[None], placing)
    mine = norm(lax.all_to_all(outgoing, "exp", 0, 0, tiled=True), weights[5:])

    across, back, ahead = send(mine, dz=1), send(mine, dy=1), send(mine, dy=-1)
    held = hold(weights, (mine,))
    up, down, over = join(
        (
            (8, ((0, 0, 0, 4), (2, 0, 4, 2), (2, 4, 6, 2))),
            (8, ((1, 4, 0, 4), (2, 0, 4, 2), (2, 4, 6, 2))),
            (8, ((0, 2, 0, 2), (0, 6, 2, 2), (1, 2, 4, 2), (1, 6, 6, 2))),
        ),
        back,
        ahead,
        across,
        after=(held[0],),
    )
    both, low, high = send(over, dz=1), send(up, dy=1), send(down, dy=-1)
    mine, across, back, ahead = expert(
        [mine, across, back, ahead],
        [[(k, 0, 8)] for k in range(4)],
        (8,) * 4,
        [[(k, 0, 8)] for k in range(4)],
        held,
    )
    up, down, over = join(
        (
            (3, ((0, 4, 0, 2), (2, 0, 2, 1))),
            (2, ((1, 6, 0, 2),)),
            (3, ((0, 3, 0, 1), (1, 2, 1, 2))),
        ),
        low,
        high,
        both,
        after=(mine,),
    )
    across_far = [send(up, dy=1), send(down, dy=-1), send(over, dz=1)]
    far_low, far_high, far_rest, across_back, across_ahead, back_b, ahead_b = expert(
        [low, high, both],
        [
            [(0, 0, 4), (1, 0, 4)],
            [(0, 4, 2), (2, 0, 2), (0, 6, 2), (2, 2, 2)],
            [(1, 4, 2), (2, 4, 2), (1, 6, 2), (2, 6, 2)],
        ],
        (3, 2, 3, 4, 4, 4, 4),
        [
            [(0, 0, 3), (2, 0, 1), (1, 0, 2), (2, 1, 2)],
            [(3, 0, 2), (5, 0, 2), (3, 2, 2), (5, 2, 2)],
            [(4, 0, 2), (6, 0, 2), (4, 2, 2), (6, 2, 2)],
        ],
        held,
    )
    low, high, back_b = send(far_low, dy=1), send(far_high, dy=-1), send(back_b, dz=1)
    last_low, last_high, last_over = expert(
        across_far,
        [[(0, 0, 3), (2, 0, 1), (1, 0, 2), (2, 1, 2)]],
        (3, 2, 3),
        [[(0, 0, 3), (2, 0, 1), (1, 0, 2), (2, 1, 2)]],
        held,
        (far_low,),
    )
    up, down, over = join(
        (
            (5, ((0, 0, 0, 4), (4, 0, 0, 2), (2, 0, 4, 1), (6, 0, 4, 1))),
            (6, ((1, 0, 0, 4), (5, 0, 2, 2), (2, 1, 4, 2), (6, 1, 4, 2))),
            (4, ((3, 0, 0, 4), (4, 2, 0, 1))),
        ),
        across_ahead,
        across_back,
        far_rest,
        ahead_b,
        send(last_low, dy=1),
        send(last_high, dy=-1),
        send(last_over, dz=1),
        after=(low, high, back_b),
    )
    across, ahead, back = join(
        (
            (8, ((0, 0, 0, 8), (3, 0, 0, 2), (3, 2, 4, 2), (4, 0, 0, 2), (4, 2, 4, 2))),
            (8, ((1, 0, 0, 8), (5, 0, 0, 3), (3, 4, 3, 1), (7, 0, 2, 2), (7, 2, 6, 2))),
            (8, ((2, 0, 0, 8), (6, 0, 4, 2), (4, 4, 6, 2), (8, 0, 2, 2), (8, 2, 6, 2))),
        ),
        across,
        ahead,
        back,
        send(up, dy=1),
        send(down, dy=-1),
        low,
        high,
        send(over, dz=1),
        back_b,
    )
    (result,) = join(
        ((8, tuple((number, 0, 0, 8) for number in range(4))),),
        mine,
        send(across, dz=1),
        send(ahead, dy=1),
        send(back, dy=-1),
    )
    outputs = lax.all_to_all(result, "exp", 0, 0, tiled=True)
    return combine(hidden, share_high, share_low, outputs)


def solution(mesh):
    return jax.shard_map(
        body,
        mesh=mesh,
        in_specs=(
            P("ctx", "exp"),
            P("ctx", "exp"),
            P("ctx", "exp"),
            P("ctx", "exp"),
            P("exp"),
            P("exp", None),
            P("exp", None, "ctx"),
            P("exp", None, "ctx"),
            P("exp", "ctx", None),
            P("ctx", None),
            P("ctx", None),
        ),
        out_specs=P("ctx", "exp"),
        check_vma=False,
    )
```

```python
import functools

import jax
import jax.numpy as jnp
from jax import lax
from jax.experimental import pallas as pl
from jax.experimental.pallas import tpu as pltpu
from jax.sharding import PartitionSpec as P

D = 6144
HD = 128
EXPERTS = 8
TOPK = 4
CAP = 80
AUX = 16
TOK = 128
SLICE = 768
SHARDS = 16
UNITS = 336
EPS = 1e-05
LOG2E = 1.4426950408889634
F32 = jnp.float32
BF16 = jnp.bfloat16
MIB = 1 << 20


def place(index):
    return index // 4, (index // 2) % 2, index % 2


def route(dy, dz, dc):
    pairs = []
    for index in range(SHARDS):
        y, z, c = place(index)
        pairs.append((index, (((y + dy) % 4) * 2 + (z + dz) % 2) * 2 + (c + dc) % 2))
    return pairs


def send(block, dy=0, dz=0, dc=0):
    return lax.ppermute(block, "ctx", route(dy, dz, dc))


def call(kernel, out_shape, limit, flops, moved, **kwargs):
    return pl.pallas_call(
        kernel,
        out_shape=out_shape,
        compiler_params=pltpu.CompilerParams(vmem_limit_bytes=limit * MIB),
        cost_estimate=pl.CostEstimate(flops=flops, bytes_accessed=moved, transcendentals=0),
        **kwargs,
    )


def shape(dims, dtype=BF16):
    return jax.ShapeDtypeStruct(dims, dtype)


def pieces(value):
    high = value.astype(BF16).astype(F32)
    left = value - high
    mid = left.astype(BF16).astype(F32)
    return high, mid, left - mid


def routing_kernel(ids_ref, scores_ref, placing_ref, high_ref, low_ref):
    ids = ids_ref[...]
    scores = scores_ref[...]
    total = scores[:, 0:1] + scores[:, 1:2] + scores[:, 2:3] + scores[:, 3:4]
    lanes = lax.broadcasted_iota(jnp.int32, (TOK, TOK), 1)
    rows = lax.broadcasted_iota(jnp.int32, (TOK, TOK), 0)
    named = [(lanes == ids[:, k : k + 1]).astype(F32) for k in range(TOPK)]
    member = named[0] + named[1] + named[2] + named[3]
    lower = (lanes < rows).astype(BF16)
    slots = jnp.dot(lower, member.astype(BF16), preferred_element_type=F32)
    wide = lax.broadcasted_iota(jnp.int32, (TOK, EXPERTS * TOK), 1)
    columns = lax.broadcasted_iota(jnp.int32, (TOK, EXPERTS * CAP), 1)
    placed = jnp.zeros((TOK, EXPERTS * TOK), F32)
    shares = jnp.zeros((TOK, EXPERTS * CAP), F32)
    for k in range(TOPK):
        slot = jnp.sum(named[k] * slots, axis=1, keepdims=True).astype(jnp.int32)
        expert = ids[:, k : k + 1]
        placed = placed + (wide == expert * TOK + slot).astype(F32)
        share = scores[:, k : k + 1] / total
        shares = shares + jnp.where(columns == expert * CAP + slot, share, 0.0)
    for e in range(EXPERTS):
        placing_ref[e] = placed[:, e * TOK : (e + 1) * TOK].T.astype(BF16)
    high = shares.astype(BF16)
    high_ref[...] = high
    low_ref[...] = (shares - high.astype(F32)).astype(BF16)


def routing(expert_ids, gate_scores):
    return call(
        routing_kernel,
        (
            shape((EXPERTS, TOK, TOK)),
            shape((TOK, EXPERTS * CAP)),
            shape((TOK, EXPERTS * CAP)),
        ),
        6,
        10**7,
        10**6,
    )(expert_ids, gate_scores)


def attention_kernel(starts_ref, queries_ref, paired_ref, weight_ref, terms_ref, held, ready):
    rows = SLICE // 4
    copies = [
        pltpu.make_async_copy(
            weight_ref.at[pl.ds(k * rows, rows)], held.at[pl.ds(k * rows, rows)], ready.at[k]
        )
        for k in range(4)
    ]
    for copy in copies:
        copy.start()
    keys = paired_ref[:, 0].reshape(SHARDS * TOK, HD)
    values = paired_ref[:, 1].reshape(SHARDS * TOK, HD)
    rows = lax.broadcasted_iota(jnp.int32, (TOK, TOK), 0)
    lanes = lax.broadcasted_iota(jnp.int32, (TOK, TOK), 1)
    ahead = rows - lanes + starts_ref[SHARDS]
    keep = jnp.concatenate([ahead >= starts_ref[b] for b in range(SHARDS)], axis=1)
    heads = []
    for h in range(queries_ref.shape[1] // HD):
        query = queries_ref[:, h * HD : (h + 1) * HD]
        scores = lax.dot_general(
            query, keys, (((1,), (1,)), ((), ())), preferred_element_type=F32
        )
        scores = jnp.where(keep, scores, -1e30)
        top = jnp.max(scores, axis=1, keepdims=True)
        expw = jnp.exp2((scores - top) * (HD**-0.5 * LOG2E))
        denom = jnp.sum(expw, axis=1, keepdims=True)
        summed = jnp.dot(expw.astype(BF16), values, preferred_element_type=F32)
        heads.append((summed / denom).astype(BF16))
    attended = jnp.concatenate(heads, axis=1)
    for copy in copies:
        copy.wait()
    for j in range(EXPERTS):
        terms_ref[j] = jnp.dot(
            attended, held[:, j * SLICE : (j + 1) * SLICE], preferred_element_type=F32
        ).astype(BF16)


def attention(starts, queries, paired, weight):
    whole = pl.BlockSpec(memory_space=pltpu.VMEM)
    return call(
        attention_kernel,
        shape((EXPERTS, TOK, SLICE)),
        48,
        2 * 10**9,
        13 * 10**6,
        in_specs=[pl.BlockSpec(memory_space=pltpu.SMEM), whole, whole]
        + [pl.BlockSpec(memory_space=pl.ANY)],
        out_specs=whole,
        scratch_shapes=[pltpu.VMEM((SLICE, D), BF16), pltpu.SemaphoreType.DMA((4,))],
    )(starts, queries, paired, weight)


def dispatch_kernel(terms_ref, residual_ref, gain_ref, placing_ref, hidden_ref, out_ref):
    hidden = residual_ref[...].astype(F32)
    for j in range(EXPERTS):
        hidden = hidden + terms_ref[j].astype(F32)
    hidden_ref[...] = hidden
    mean = jnp.sum(hidden, axis=1, keepdims=True) * (1.0 / SLICE)
    apart = (hidden - mean).astype(BF16)
    lanes = lax.broadcasted_iota(jnp.int32, (TOK, TOK), 1)
    high, mid, low = pieces(mean)
    spread = jnp.where(lanes == 0, high, jnp.where(lanes == 1, mid, jnp.where(lanes == 2, low, 0.0)))
    means = spread.T[:AUX].astype(BF16)
    rows = lax.broadcasted_iota(jnp.int32, (AUX, SLICE), 0)
    high, mid, low = pieces(gain_ref[...])
    gains = jnp.where(rows == 3, high, jnp.where(rows == 4, mid, jnp.where(rows == 5, low, 0.0)))
    for e in range(EXPERTS):
        placing = placing_ref[e]
        out_ref[e, :CAP] = jnp.dot(placing[:CAP], apart, preferred_element_type=F32).astype(BF16)
        sent = lax.dot_general(means, placing, (((1,), (1,)), ((), ())), preferred_element_type=F32)
        out_ref[e, CAP:] = jnp.concatenate(
            [sent + gains[:, :TOK], gains[:, TOK:]], axis=1
        ).astype(BF16)


def dispatch(terms, residual, gain, placing):
    return call(
        dispatch_kernel,
        (shape((TOK, SLICE), F32), shape((EXPERTS, CAP + AUX, SLICE))),
        4,
        2 * 10**8,
        5 * 10**6,
    )(terms, residual, gain, placing)


def norm_kernel(arrived_ref, *refs):
    out_ref = refs[-1]
    rows = lax.broadcasted_iota(jnp.int32, (CAP, TOK), 0)
    lanes = lax.broadcasted_iota(jnp.int32, (CAP, TOK), 1)
    diagonal = (rows == lanes).astype(BF16)
    means = []
    total = jnp.zeros((CAP, 1), F32)
    for j in range(EXPERTS):
        turned = lax.dot_general(
            diagonal, arrived_ref[j, CAP:, :TOK], (((1,), (1,)), ((), ())), preferred_element_type=F32
        )
        means.append(turned[:, 0:1] + turned[:, 1:2] + turned[:, 2:3])
        total = total + SLICE * means[j]
    mean = total / D
    spread = jnp.zeros((CAP, 1), F32)
    for j in range(EXPERTS):
        apart = arrived_ref[j, :CAP].astype(F32) + (means[j] - mean)
        spread = spread + jnp.sum(apart * apart, axis=1, keepdims=True)
    scale = lax.rsqrt(spread / D + EPS)
    for j in range(EXPERTS):
        aux = arrived_ref[j, CAP:].astype(F32)
        gain = aux[3:4] + aux[4:5] + aux[5:6]
        apart = arrived_ref[j, :CAP].astype(F32) + (means[j] - mean)
        out_ref[j] = (apart * scale * gain).astype(BF16)


def norm(arrived, after):
    return call(
        norm_kernel,
        shape((EXPERTS, CAP, SLICE)),
        4,
        10**7,
        2 * 10**6,
        in_specs=[pl.BlockSpec(memory_space=pltpu.VMEM)]
        + [pl.BlockSpec(memory_space=pl.ANY)] * len(after),
    )(arrived, *after)


HELD = 2 * UNITS


def hold_kernel(*refs):
    weights, held, ready = refs[:6], refs[-4:-1], refs[-1]
    copies = [
        pltpu.make_async_copy(
            weights[2 * number + core],
            held[number].at[pl.ds(core * UNITS, UNITS)],
            ready.at[2 * number + core],
        )
        for number in range(3)
        for core in range(2)
    ]
    for copy in copies:
        copy.start()
    for copy in copies:
        copy.wait()


def hold(weights, after):
    apart = pl.BlockSpec(memory_space=pl.ANY)
    return call(
        hold_kernel,
        tuple(pltpu.VMEM((HELD, D), BF16) for _ in range(3)),
        1,
        10**6,
        25 * 10**6,
        in_specs=[apart] * (6 + len(after)),
        out_specs=(pl.BlockSpec(memory_space=pltpu.VMEM),) * 3,
        scratch_shapes=[pltpu.SemaphoreType.DMA((6,))],
    )(*weights, *after)


def expert_kernel(pieces_in, pieces_out, n_in, n_out, *refs):
    xs, refs = refs[:n_in], refs[n_in:]
    gate_ref, up_ref, down_ref = refs[:3]
    outs, rows_ref = refs[len(refs) - n_out - 1 : -1], refs[-1]
    for shard, split in enumerate(pieces_in):
        block = 0
        for number, first, count in split:
            for k in range(first, first + count):
                rows_ref[
                    shard * CAP : (shard + 1) * CAP, block * SLICE : (block + 1) * SLICE
                ] = xs[number][k]
                block += 1
    turned = (((1,), (1,)), ((), ()))
    rows = rows_ref[...]
    gate = lax.dot_general(rows, gate_ref[...], turned, preferred_element_type=F32)
    up = lax.dot_general(rows, up_ref[...], turned, preferred_element_type=F32)
    act = (gate / (1.0 + jnp.exp(-gate)) * up).astype(BF16)
    for now in range(EXPERTS):
        result = jnp.dot(
            act, down_ref[:, now * SLICE : (now + 1) * SLICE], preferred_element_type=F32
        ).astype(BF16)
        for shard, split in enumerate(pieces_out):
            block = 0
            for number, first, count in split:
                if block <= now < block + count:
                    outs[number][first + now - block] = result[shard * CAP : (shard + 1) * CAP]
                block += count


def expert(arrays, pieces_in, sizes, pieces_out, held, after=()):
    total = CAP * len(pieces_in)
    whole = pl.BlockSpec(memory_space=pltpu.VMEM)
    return call(
        functools.partial(expert_kernel, pieces_in, pieces_out, len(arrays), len(sizes)),
        tuple(shape((size, CAP, SLICE)) for size in sizes),
        10,
        total * D * 2 * UNITS * 6,
        25 * 10**6,
        in_specs=[whole] * (len(arrays) + 3) + [pl.BlockSpec(memory_space=pl.ANY)] * len(after),
        out_specs=(whole,) * len(sizes),
        scratch_shapes=[pltpu.VMEM((total, D), BF16)],
    )(*arrays, *held, *after)


def join_kernel(plans, *refs):
    ins, outs = refs, refs[len(refs) - len(plans) :]
    for (size, terms), out in zip(plans, outs):
        for block in range(size):
            total = None
            for number, first, into, count in terms:
                if into <= block < into + count:
                    value = ins[number][first + block - into]
                    if total is None:
                        total = value
                    else:
                        total = total.astype(F32) + value.astype(F32)
            out[block] = total.astype(BF16)


def join(plans, *arrays, after=()):
    whole = pl.BlockSpec(memory_space=pltpu.VMEM)
    return call(
        functools.partial(join_kernel, plans),
        tuple(shape((size, CAP, SLICE)) for size, _ in plans),
        2,
        10**7,
        8 * 10**6,
        in_specs=[whole] * len(arrays) + [pl.BlockSpec(memory_space=pl.ANY)] * len(after),
        out_specs=(whole,) * len(plans),
    )(*arrays, *after)


def combine_kernel(hidden_ref, high_ref, low_ref, outputs_ref, mixed_ref):
    outputs = outputs_ref[...].reshape(EXPERTS * CAP, SLICE)
    moe = jnp.dot(high_ref[...], outputs, preferred_element_type=F32)
    moe += jnp.dot(low_ref[...], outputs, preferred_element_type=F32)
    mixed_ref[...] = (hidden_ref[...] + moe).astype(BF16)


def combine(hidden, high, low, outputs):
    return call(combine_kernel, shape((TOK, SLICE)), 4, 3 * 10**8, 2 * 10**6)(
        hidden, high, low, outputs
    )


def body(
    queries,
    keys,
    values,
    residual,
    ln_gain,
    out_weight,
    gate_weight,
    up_weight,
    down_weight,
    expert_ids,
    gate_scores,
):
    ctx = lax.axis_index("ctx")
    own = jnp.stack((keys, values))[None]
    first = jnp.concatenate([own, send(own, dz=1)])
    near = jnp.concatenate([first, send(first, dy=1), send(first, dy=-1), send(first, dy=2)])
    paired = jnp.concatenate([near, send(near, dc=1)])
    y, z, c = ctx // 4, (ctx // 2) % 2, ctx % 2
    starts = [
        ((((y - dy) % 4) * 2 + (z + dz) % 2) * 2 + (c + dc) % 2) * TOK
        for dc in (0, 1)
        for dy in (0, 1, -1, 2)
        for dz in (0, 1)
    ]
    starts = jnp.stack(starts + [ctx * TOK]).astype(jnp.int32)
    placing, share_high, share_low = routing(expert_ids, gate_scores)
    weights = []
    for weight in (gate_weight[0].T, up_weight[0].T, down_weight[0]):
        weights += [weight, send(weight, dc=1)]

    terms = attention(starts, queries, paired, out_weight)
    terms = lax.all_to_all(terms, "exp", 0, 0, tiled=True)
    hidden, outgoing = dispatch(terms, residual, ln_gain[None], placing)
    mine = norm(lax.all_to_all(outgoing, "exp", 0, 0, tiled=True), weights[5:])

    across, back, ahead = send(mine, dz=1), send(mine, dy=1), send(mine, dy=-1)
    held = hold(weights, (mine,))
    up, down, over = join(
        (
            (9, ((0, 0, 0, 4), (2, 0, 4, 3), (2, 4, 7, 2))),
            (9, ((1, 4, 0, 4), (2, 0, 4, 3), (2, 4, 7, 2))),
            (6, ((0, 3, 0, 1), (0, 6, 1, 2), (1, 3, 3, 1), (1, 6, 4, 2))),
        ),
        back,
        ahead,
        across,
        after=(held[0],),
    )
    low, high, both = send(up, dy=1), send(down, dy=-1), send(over, dz=1)
    mine, across, back, ahead, across_b = expert(
        [mine, across, back, ahead],
        [[(k, 0, 8)] for k in range(4)],
        (8, 5, 8, 8, 3),
        [[(0, 0, 8)], [(1, 0, 3), (4, 0, 1), (1, 3, 2), (4, 1, 2)], [(2, 0, 8)], [(3, 0, 8)]],
        held,
    )
    up, down, over = join(
        (
            (3, ((0, 4, 0, 3),)),
            (2, ((1, 7, 0, 2),)),
            (3, ((0, 3, 0, 1), (1, 2, 1, 2))),
        ),
        low,
        high,
        both,
        after=(mine,),
    )
    across_far = [send(up, dy=1), send(down, dy=-1), send(over, dz=1)]
    far_low, far_high, far_rest, across_back, across_ahead, over = expert(
        [low, high, both],
        [
            [(0, 0, 4), (1, 0, 4)],
            [(0, 4, 3), (2, 0, 1), (0, 7, 2), (2, 1, 2)],
            [(1, 4, 3), (2, 3, 1), (1, 7, 2), (2, 4, 2)],
        ],
        (3, 2, 3, 5, 5, 6),
        [
            [(0, 0, 3), (2, 0, 1), (1, 0, 2), (2, 1, 2)],
            [(3, 0, 3), (5, 0, 1), (3, 3, 2), (5, 1, 2)],
            [(4, 0, 3), (5, 3, 1), (4, 3, 2), (5, 4, 2)],
        ],
        held,
    )
    low, high, over = send(far_low, dy=1), send(far_high, dy=-1), send(over, dz=1)
    last_low, last_high, last_over = expert(
        across_far,
        [[(0, 0, 3), (2, 0, 1), (1, 0, 2), (2, 1, 2)]],
        (3, 2, 3),
        [[(0, 0, 3), (2, 0, 1), (1, 0, 2), (2, 1, 2)]],
        held,
        (far_low,),
    )
    up, down = join(
        (
            (6, ((0, 0, 0, 5), (3, 0, 0, 3), (2, 0, 5, 1), (5, 0, 5, 1))),
            (7, ((1, 0, 0, 5), (4, 0, 3, 2), (2, 1, 5, 2), (5, 1, 5, 2))),
        ),
        across_ahead,
        across_back,
        far_rest,
        send(last_low, dy=1),
        send(last_high, dy=-1),
        send(last_over, dz=1),
        after=(low, high, over),
    )
    up, down, across_b = send(up, dy=1), send(down, dy=-1), send(across_b, dz=1)
    across, ahead, back = join(
        (
            (5, ((0, 0, 0, 5), (3, 0, 0, 5), (4, 0, 0, 5))),
            (8, ((1, 0, 0, 8), (5, 0, 0, 3), (3, 5, 3, 1), (7, 3, 3, 1), (7, 4, 6, 2))),
            (8, ((2, 0, 0, 8), (6, 0, 4, 2), (4, 5, 6, 2), (7, 0, 3, 1), (7, 1, 6, 2))),
        ),
        across,
        ahead,
        back,
        up,
        down,
        low,
        high,
        over,
        after=(across_b,),
    )
    (result,) = join(
        (
            (
                8,
                (
                    (0, 0, 0, 8),
                    (1, 0, 0, 8),
                    (2, 0, 0, 8),
                    (3, 0, 0, 3),
                    (3, 3, 4, 2),
                    (4, 0, 3, 1),
                    (4, 1, 6, 2),
                ),
            ),
        ),
        mine,
        send(ahead, dy=1),
        send(back, dy=-1),
        send(across, dz=1),
        across_b,
    )
    outputs = lax.all_to_all(result, "exp", 0, 0, tiled=True)
    return combine(hidden, share_high, share_low, outputs)


def solution(mesh):
    return jax.shard_map(
        body,
        mesh=mesh,
        in_specs=(
            P("ctx", "exp"),
            P("ctx", "exp"),
            P("ctx", "exp"),
            P("ctx", "exp"),
            P("exp"),
            P("exp", None),
            P("exp", None, "ctx"),
            P("exp", None, "ctx"),
            P("exp", "ctx", None),
            P("ctx", None),
            P("ctx", None),
        ),
        out_specs=P("ctx", "exp"),
        check_vma=False,
    )
```

```python
import functools

import jax
import jax.numpy as jnp
from jax import lax
from jax.experimental import pallas as pl
from jax.experimental.pallas import tpu as pltpu
from jax.sharding import PartitionSpec as P

D = 6144
HD = 128
EXPERTS = 8
TOPK = 4
CAP = 80
AUX = 16
TOK = 128
SLICE = 768
SHARDS = 16
UNITS = 336
EPS = 1e-05
LOG2E = 1.4426950408889634
F32 = jnp.float32
BF16 = jnp.bfloat16
MIB = 1 << 20


def place(index):
    return index // 4, (index // 2) % 2, index % 2


def route(dy, dz, dc):
    pairs = []
    for index in range(SHARDS):
        y, z, c = place(index)
        pairs.append((index, (((y + dy) % 4) * 2 + (z + dz) % 2) * 2 + (c + dc) % 2))
    return pairs


def send(block, dy=0, dz=0, dc=0):
    return lax.ppermute(block, "ctx", route(dy, dz, dc))


def call(kernel, out_shape, limit, flops, moved, **kwargs):
    return pl.pallas_call(
        kernel,
        out_shape=out_shape,
        compiler_params=pltpu.CompilerParams(vmem_limit_bytes=limit * MIB),
        cost_estimate=pl.CostEstimate(flops=flops, bytes_accessed=moved, transcendentals=0),
        **kwargs,
    )


def shape(dims, dtype=BF16):
    return jax.ShapeDtypeStruct(dims, dtype)


def pieces(value):
    high = value.astype(BF16).astype(F32)
    left = value - high
    mid = left.astype(BF16).astype(F32)
    return high, mid, left - mid


def routing_kernel(ids_ref, scores_ref, placing_ref, high_ref, low_ref):
    ids = ids_ref[...]
    scores = scores_ref[...]
    total = scores[:, 0:1] + scores[:, 1:2] + scores[:, 2:3] + scores[:, 3:4]
    lanes = lax.broadcasted_iota(jnp.int32, (TOK, TOK), 1)
    rows = lax.broadcasted_iota(jnp.int32, (TOK, TOK), 0)
    named = [(lanes == ids[:, k : k + 1]).astype(F32) for k in range(TOPK)]
    member = named[0] + named[1] + named[2] + named[3]
    lower = (lanes < rows).astype(BF16)
    slots = jnp.dot(lower, member.astype(BF16), preferred_element_type=F32)
    wide = lax.broadcasted_iota(jnp.int32, (TOK, EXPERTS * TOK), 1)
    columns = lax.broadcasted_iota(jnp.int32, (TOK, EXPERTS * CAP), 1)
    placed = jnp.zeros((TOK, EXPERTS * TOK), F32)
    shares = jnp.zeros((TOK, EXPERTS * CAP), F32)
    for k in range(TOPK):
        slot = jnp.sum(named[k] * slots, axis=1, keepdims=True).astype(jnp.int32)
        expert = ids[:, k : k + 1]
        placed = placed + (wide == expert * TOK + slot).astype(F32)
        share = scores[:, k : k + 1] / total
        shares = shares + jnp.where(columns == expert * CAP + slot, share, 0.0)
    for e in range(EXPERTS):
        placing_ref[e] = placed[:, e * TOK : (e + 1) * TOK].T.astype(BF16)
    high = shares.astype(BF16)
    high_ref[...] = high
    low_ref[...] = (shares - high.astype(F32)).astype(BF16)


def routing(expert_ids, gate_scores):
    return call(
        routing_kernel,
        (
            shape((EXPERTS, TOK, TOK)),
            shape((TOK, EXPERTS * CAP)),
            shape((TOK, EXPERTS * CAP)),
        ),
        6,
        10**7,
        10**6,
    )(expert_ids, gate_scores)


def attention_kernel(starts_ref, queries_ref, paired_ref, weight_ref, terms_ref, held, ready):
    rows = SLICE // 4
    copies = [
        pltpu.make_async_copy(
            weight_ref.at[pl.ds(k * rows, rows)], held.at[pl.ds(k * rows, rows)], ready.at[k]
        )
        for k in range(4)
    ]
    for copy in copies:
        copy.start()
    keys = paired_ref[:, 0].reshape(SHARDS * TOK, HD)
    values = paired_ref[:, 1].reshape(SHARDS * TOK, HD)
    rows = lax.broadcasted_iota(jnp.int32, (TOK, TOK), 0)
    lanes = lax.broadcasted_iota(jnp.int32, (TOK, TOK), 1)
    ahead = rows - lanes + starts_ref[SHARDS]
    keep = jnp.concatenate([ahead >= starts_ref[b] for b in range(SHARDS)], axis=1)
    heads = []
    for h in range(queries_ref.shape[1] // HD):
        query = queries_ref[:, h * HD : (h + 1) * HD]
        scores = lax.dot_general(
            query, keys, (((1,), (1,)), ((), ())), preferred_element_type=F32
        )
        scores = jnp.where(keep, scores, -1e30)
        top = jnp.max(scores, axis=1, keepdims=True)
        expw = jnp.exp2((scores - top) * (HD**-0.5 * LOG2E))
        denom = jnp.sum(expw, axis=1, keepdims=True)
        summed = jnp.dot(expw.astype(BF16), values, preferred_element_type=F32)
        heads.append((summed / denom).astype(BF16))
    attended = jnp.concatenate(heads, axis=1)
    for copy in copies:
        copy.wait()
    for j in range(EXPERTS):
        terms_ref[j] = jnp.dot(
            attended, held[:, j * SLICE : (j + 1) * SLICE], preferred_element_type=F32
        ).astype(BF16)


def attention(starts, queries, paired, weight):
    whole = pl.BlockSpec(memory_space=pltpu.VMEM)
    return call(
        attention_kernel,
        shape((EXPERTS, TOK, SLICE)),
        48,
        2 * 10**9,
        13 * 10**6,
        in_specs=[pl.BlockSpec(memory_space=pltpu.SMEM), whole, whole]
        + [pl.BlockSpec(memory_space=pl.ANY)],
        out_specs=whole,
        scratch_shapes=[pltpu.VMEM((SLICE, D), BF16), pltpu.SemaphoreType.DMA((4,))],
    )(starts, queries, paired, weight)


def dispatch_kernel(terms_ref, residual_ref, gain_ref, placing_ref, hidden_ref, out_ref):
    hidden = residual_ref[...].astype(F32)
    for j in range(EXPERTS):
        hidden = hidden + terms_ref[j].astype(F32)
    hidden_ref[...] = hidden
    mean = jnp.sum(hidden, axis=1, keepdims=True) * (1.0 / SLICE)
    apart = (hidden - mean).astype(BF16)
    lanes = lax.broadcasted_iota(jnp.int32, (TOK, TOK), 1)
    high, mid, low = pieces(mean)
    spread = jnp.where(lanes == 0, high, jnp.where(lanes == 1, mid, jnp.where(lanes == 2, low, 0.0)))
    means = spread.T[:AUX].astype(BF16)
    rows = lax.broadcasted_iota(jnp.int32, (AUX, SLICE), 0)
    high, mid, low = pieces(gain_ref[...])
    gains = jnp.where(rows == 3, high, jnp.where(rows == 4, mid, jnp.where(rows == 5, low, 0.0)))
    for e in range(EXPERTS):
        placing = placing_ref[e]
        out_ref[e, :CAP] = jnp.dot(placing[:CAP], apart, preferred_element_type=F32).astype(BF16)
        sent = lax.dot_general(means, placing, (((1,), (1,)), ((), ())), preferred_element_type=F32)
        out_ref[e, CAP:] = jnp.concatenate(
            [sent + gains[:, :TOK], gains[:, TOK:]], axis=1
        ).astype(BF16)


def dispatch(terms, residual, gain, placing):
    return call(
        dispatch_kernel,
        (shape((TOK, SLICE), F32), shape((EXPERTS, CAP + AUX, SLICE))),
        4,
        2 * 10**8,
        5 * 10**6,
    )(terms, residual, gain, placing)


def norm_kernel(arrived_ref, *refs):
    out_ref = refs[-1]
    rows = lax.broadcasted_iota(jnp.int32, (CAP, TOK), 0)
    lanes = lax.broadcasted_iota(jnp.int32, (CAP, TOK), 1)
    diagonal = (rows == lanes).astype(BF16)
    means = []
    total = jnp.zeros((CAP, 1), F32)
    for j in range(EXPERTS):
        turned = lax.dot_general(
            diagonal, arrived_ref[j, CAP:, :TOK], (((1,), (1,)), ((), ())), preferred_element_type=F32
        )
        means.append(turned[:, 0:1] + turned[:, 1:2] + turned[:, 2:3])
        total = total + SLICE * means[j]
    mean = total / D
    spread = jnp.zeros((CAP, 1), F32)
    for j in range(EXPERTS):
        apart = arrived_ref[j, :CAP].astype(F32) + (means[j] - mean)
        spread = spread + jnp.sum(apart * apart, axis=1, keepdims=True)
    scale = lax.rsqrt(spread / D + EPS)
    for j in range(EXPERTS):
        aux = arrived_ref[j, CAP:].astype(F32)
        gain = aux[3:4] + aux[4:5] + aux[5:6]
        apart = arrived_ref[j, :CAP].astype(F32) + (means[j] - mean)
        out_ref[j] = (apart * scale * gain).astype(BF16)


def norm(arrived, after):
    return call(
        norm_kernel,
        shape((EXPERTS, CAP, SLICE)),
        4,
        10**7,
        2 * 10**6,
        in_specs=[pl.BlockSpec(memory_space=pltpu.VMEM)]
        + [pl.BlockSpec(memory_space=pl.ANY)] * len(after),
    )(arrived, *after)


HELD = 2 * UNITS


def hold_kernel(*refs):
    weights, held, ready = refs[:6], refs[-4:-1], refs[-1]
    copies = [
        pltpu.make_async_copy(
            weights[2 * number + core],
            held[number].at[pl.ds(core * UNITS, UNITS)],
            ready.at[2 * number + core],
        )
        for number in range(3)
        for core in range(2)
    ]
    for copy in copies:
        copy.start()
    for copy in copies:
        copy.wait()


def hold(weights, after):
    apart = pl.BlockSpec(memory_space=pl.ANY)
    return call(
        hold_kernel,
        tuple(pltpu.VMEM((HELD, D), BF16) for _ in range(3)),
        1,
        10**6,
        25 * 10**6,
        in_specs=[apart] * (6 + len(after)),
        out_specs=(pl.BlockSpec(memory_space=pltpu.VMEM),) * 3,
        scratch_shapes=[pltpu.SemaphoreType.DMA((6,))],
    )(*weights, *after)


def expert_kernel(pieces_in, pieces_out, n_in, n_out, *refs):
    xs, refs = refs[:n_in], refs[n_in:]
    gate_ref, up_ref, down_ref = refs[:3]
    outs, rows_ref = refs[len(refs) - n_out - 1 : -1], refs[-1]
    for shard, split in enumerate(pieces_in):
        block = 0
        for number, first, count in split:
            for k in range(first, first + count):
                rows_ref[
                    shard * CAP : (shard + 1) * CAP, block * SLICE : (block + 1) * SLICE
                ] = xs[number][k]
                block += 1
    turned = (((1,), (1,)), ((), ()))
    rows = rows_ref[...]
    gate = lax.dot_general(rows, gate_ref[...], turned, preferred_element_type=F32)
    up = lax.dot_general(rows, up_ref[...], turned, preferred_element_type=F32)
    act = (gate / (1.0 + jnp.exp(-gate)) * up).astype(BF16)
    for now in range(EXPERTS):
        result = jnp.dot(
            act, down_ref[:, now * SLICE : (now + 1) * SLICE], preferred_element_type=F32
        ).astype(BF16)
        for shard, split in enumerate(pieces_out):
            block = 0
            for number, first, count in split:
                if block <= now < block + count:
                    outs[number][first + now - block] = result[shard * CAP : (shard + 1) * CAP]
                block += count


def expert(arrays, pieces_in, sizes, pieces_out, held, after=()):
    total = CAP * len(pieces_in)
    whole = pl.BlockSpec(memory_space=pltpu.VMEM)
    return call(
        functools.partial(expert_kernel, pieces_in, pieces_out, len(arrays), len(sizes)),
        tuple(shape((size, CAP, SLICE)) for size in sizes),
        10,
        total * D * 2 * UNITS * 6,
        25 * 10**6,
        in_specs=[whole] * (len(arrays) + 3) + [pl.BlockSpec(memory_space=pl.ANY)] * len(after),
        out_specs=(whole,) * len(sizes),
        scratch_shapes=[pltpu.VMEM((total, D), BF16)],
    )(*arrays, *held, *after)


def join_kernel(plans, *refs):
    ins, outs = refs, refs[len(refs) - len(plans) :]
    for (size, terms), out in zip(plans, outs):
        for block in range(size):
            total = None
            for number, first, into, count in terms:
                if into <= block < into + count:
                    value = ins[number][first + block - into]
                    if total is None:
                        total = value
                    else:
                        total = total.astype(F32) + value.astype(F32)
            out[block] = total.astype(BF16)


def join(plans, *arrays, after=()):
    whole = pl.BlockSpec(memory_space=pltpu.VMEM)
    return call(
        functools.partial(join_kernel, plans),
        tuple(shape((size, CAP, SLICE)) for size, _ in plans),
        2,
        10**7,
        8 * 10**6,
        in_specs=[whole] * len(arrays) + [pl.BlockSpec(memory_space=pl.ANY)] * len(after),
        out_specs=(whole,) * len(plans),
    )(*arrays, *after)


def combine_kernel(hidden_ref, high_ref, low_ref, outputs_ref, mixed_ref):
    outputs = outputs_ref[...].reshape(EXPERTS * CAP, SLICE)
    moe = jnp.dot(high_ref[...], outputs, preferred_element_type=F32)
    moe += jnp.dot(low_ref[...], outputs, preferred_element_type=F32)
    mixed_ref[...] = (hidden_ref[...] + moe).astype(BF16)


def combine(hidden, high, low, outputs):
    return call(combine_kernel, shape((TOK, SLICE)), 4, 3 * 10**8, 2 * 10**6)(
        hidden, high, low, outputs
    )


def body(
    queries,
    keys,
    values,
    residual,
    ln_gain,
    out_weight,
    gate_weight,
    up_weight,
    down_weight,
    expert_ids,
    gate_scores,
):
    ctx = lax.axis_index("ctx")
    own = jnp.stack((keys, values))[None]
    first = jnp.concatenate([own, send(own, dz=1)])
    near = jnp.concatenate([first, send(first, dy=1), send(first, dy=-1), send(first, dy=2)])
    paired = jnp.concatenate([near, send(near, dc=1)])
    y, z, c = ctx // 4, (ctx // 2) % 2, ctx % 2
    starts = [
        ((((y - dy) % 4) * 2 + (z + dz) % 2) * 2 + (c + dc) % 2) * TOK
        for dc in (0, 1)
        for dy in (0, 1, -1, 2)
        for dz in (0, 1)
    ]
    starts = jnp.stack(starts + [ctx * TOK]).astype(jnp.int32)
    placing, share_high, share_low = routing(expert_ids, gate_scores)
    weights = []
    for weight in (gate_weight[0].T, up_weight[0].T, down_weight[0]):
        weights += [weight, send(weight, dc=1)]

    terms = attention(starts, queries, paired, out_weight)
    terms = lax.all_to_all(terms, "exp", 0, 0, tiled=True)
    hidden, outgoing = dispatch(terms, residual, ln_gain[None], placing)
    mine = norm(lax.all_to_all(outgoing, "exp", 0, 0, tiled=True), weights[5:])

    across, back, ahead = send(mine, dz=1), send(mine, dy=1), send(mine, dy=-1)
    held = hold(weights, (mine,))
    up, down, over = join(
        (
            (9, ((0, 0, 0, 4), (2, 0, 4, 3), (2, 4, 7, 2))),
            (9, ((1, 4, 0, 4), (2, 0, 4, 3), (2, 4, 7, 2))),
            (6, ((0, 3, 0, 1), (0, 6, 1, 2), (1, 3, 3, 1), (1, 6, 4, 2))),
        ),
        back,
        ahead,
        across,
        after=(held[0],),
    )
    low, high, both = send(up, dy=1), send(down, dy=-1), send(over, dz=1)
    mine, across, back, ahead, across_b = expert(
        [mine, across, back, ahead],
        [[(k, 0, 8)] for k in range(4)],
        (8, 5, 8, 8, 3),
        [[(0, 0, 8)], [(1, 0, 3), (4, 0, 1), (1, 3, 2), (4, 1, 2)], [(2, 0, 8)], [(3, 0, 8)]],
        held,
    )
    up, down, over = join(
        (
            (5, ((0, 4, 0, 3), (3, 4, 3, 2))),
            (5, ((1, 7, 0, 2), (4, 0, 2, 3))),
            (3, ((0, 3, 0, 1), (1, 2, 1, 2))),
        ),
        low,
        high,
        both,
        ahead,
        back,
    )
    across_far = [send(up, dy=1), send(down, dy=-1), send(over, dz=1)]
    far_low, far_high, far_rest, across_back, across_ahead, back_b, ahead_b = expert(
        [low, high, both],
        [
            [(0, 0, 4), (1, 0, 4)],
            [(0, 4, 3), (2, 0, 1), (0, 7, 2), (2, 1, 2)],
            [(1, 4, 3), (2, 3, 1), (1, 7, 2), (2, 4, 2)],
        ],
        (3, 2, 3, 5, 5, 3, 3),
        [
            [(0, 0, 3), (2, 0, 1), (1, 0, 2), (2, 1, 2)],
            [(3, 0, 3), (5, 0, 1), (3, 3, 2), (5, 1, 2)],
            [(4, 0, 3), (6, 0, 1), (4, 3, 2), (6, 1, 2)],
        ],
        held,
    )
    low, high, back_b = send(far_low, dy=1), send(far_high, dy=-1), send(back_b, dz=1)
    last_low, last_high, last_over = expert(
        across_far,
        [[(0, 0, 3), (2, 0, 1), (1, 0, 2), (2, 1, 2)]],
        (3, 2, 3),
        [[(0, 0, 3), (2, 0, 1), (1, 0, 2), (2, 1, 2)]],
        held,
        (far_low,),
    )
    up, down, over = join(
        (
            (6, ((0, 0, 0, 5), (3, 0, 0, 3), (2, 0, 5, 1), (5, 0, 5, 1))),
            (7, ((1, 0, 0, 5), (4, 0, 3, 2), (2, 1, 5, 2), (5, 1, 5, 2))),
            (6, ((6, 0, 0, 3), (7, 0, 3, 3))),
        ),
        across_ahead,
        across_back,
        far_rest,
        send(last_low, dy=1),
        send(last_high, dy=-1),
        send(last_over, dz=1),
        ahead_b,
        across_b,
        after=(low, high, back_b),
    )
    up, down, over = send(up, dy=1), send(down, dy=-1), send(over, dz=1)
    across, ahead, back = join(
        (
            (5, ((0, 0, 0, 5), (3, 0, 0, 5), (4, 0, 0, 5))),
            (6, ((1, 0, 0, 4), (1, 6, 4, 2), (5, 0, 0, 3), (3, 5, 3, 1), (7, 0, 3, 3))),
            (
                5,
                ((2, 3, 0, 5), (6, 0, 1, 2), (4, 5, 3, 2), (8, 0, 0, 1), (8, 1, 3, 2)),
            ),
        ),
        across,
        ahead,
        back,
        up,
        down,
        low,
        high,
        over,
        back_b,
    )
    (result,) = join(
        (
            (
                8,
                (
                    (0, 0, 0, 8),
                    (1, 0, 0, 4),
                    (1, 4, 6, 2),
                    (2, 0, 3, 5),
                    (3, 0, 0, 3),
                    (3, 3, 4, 2),
                    (4, 3, 3, 1),
                    (4, 4, 6, 2),
                    (5, 3, 4, 2),
                    (6, 2, 0, 3),
                ),
            ),
        ),
        mine,
        send(ahead, dy=1),
        send(back, dy=-1),
        send(across, dz=1),
        over,
        across_far[0],
        across_far[1],
    )
    outputs = lax.all_to_all(result, "exp", 0, 0, tiled=True)
    return combine(hidden, share_high, share_low, outputs)


def solution(mesh):
    return jax.shard_map(
        body,
        mesh=mesh,
        in_specs=(
            P("ctx", "exp"),
            P("ctx", "exp"),
            P("ctx", "exp"),
            P("ctx", "exp"),
            P("exp"),
            P("exp", None),
            P("exp", None, "ctx"),
            P("exp", None, "ctx"),
            P("exp", "ctx", None),
            P("ctx", None),
            P("ctx", None),
        ),
        out_specs=P("ctx", "exp"),
        check_vma=False,
    )
```

```python
import functools

import jax
import jax.numpy as jnp
from jax import lax
from jax.experimental import pallas as pl
from jax.experimental.pallas import tpu as pltpu
from jax.sharding import PartitionSpec as P

D = 6144
HD = 128
EXPERTS = 8
TOPK = 4
CAP = 80
AUX = 16
TOK = 128
SLICE = 768
SHARDS = 16
UNITS = 336
EPS = 1e-05
LOG2E = 1.4426950408889634
F32 = jnp.float32
BF16 = jnp.bfloat16
MIB = 1 << 20


def place(index):
    return index // 4, (index // 2) % 2, index % 2


def route(dy, dz, dc):
    pairs = []
    for index in range(SHARDS):
        y, z, c = place(index)
        pairs.append((index, (((y + dy) % 4) * 2 + (z + dz) % 2) * 2 + (c + dc) % 2))
    return pairs


def send(block, dy=0, dz=0, dc=0):
    return lax.ppermute(block, "ctx", route(dy, dz, dc))


def call(kernel, out_shape, limit, flops, moved, **kwargs):
    return pl.pallas_call(
        kernel,
        out_shape=out_shape,
        compiler_params=pltpu.CompilerParams(vmem_limit_bytes=limit * MIB),
        cost_estimate=pl.CostEstimate(flops=flops, bytes_accessed=moved, transcendentals=0),
        **kwargs,
    )


def shape(dims, dtype=BF16):
    return jax.ShapeDtypeStruct(dims, dtype)


def pieces(value):
    high = value.astype(BF16).astype(F32)
    left = value - high
    mid = left.astype(BF16).astype(F32)
    return high, mid, left - mid


def routing_kernel(ids_ref, scores_ref, placing_ref, high_ref, low_ref):
    ids = ids_ref[...]
    scores = scores_ref[...]
    total = scores[:, 0:1] + scores[:, 1:2] + scores[:, 2:3] + scores[:, 3:4]
    lanes = lax.broadcasted_iota(jnp.int32, (TOK, TOK), 1)
    rows = lax.broadcasted_iota(jnp.int32, (TOK, TOK), 0)
    named = [(lanes == ids[:, k : k + 1]).astype(F32) for k in range(TOPK)]
    member = named[0] + named[1] + named[2] + named[3]
    lower = (lanes < rows).astype(BF16)
    slots = jnp.dot(lower, member.astype(BF16), preferred_element_type=F32)
    wide = lax.broadcasted_iota(jnp.int32, (TOK, EXPERTS * TOK), 1)
    columns = lax.broadcasted_iota(jnp.int32, (TOK, EXPERTS * CAP), 1)
    placed = jnp.zeros((TOK, EXPERTS * TOK), F32)
    shares = jnp.zeros((TOK, EXPERTS * CAP), F32)
    for k in range(TOPK):
        slot = jnp.sum(named[k] * slots, axis=1, keepdims=True).astype(jnp.int32)
        expert = ids[:, k : k + 1]
        placed = placed + (wide == expert * TOK + slot).astype(F32)
        share = scores[:, k : k + 1] / total
        shares = shares + jnp.where(columns == expert * CAP + slot, share, 0.0)
    for e in range(EXPERTS):
        placing_ref[e] = placed[:, e * TOK : (e + 1) * TOK].T.astype(BF16)
    high = shares.astype(BF16)
    high_ref[...] = high
    low_ref[...] = (shares - high.astype(F32)).astype(BF16)


def routing(expert_ids, gate_scores):
    return call(
        routing_kernel,
        (
            shape((EXPERTS, TOK, TOK)),
            shape((TOK, EXPERTS * CAP)),
            shape((TOK, EXPERTS * CAP)),
        ),
        6,
        10**7,
        10**6,
    )(expert_ids, gate_scores)


def attention_kernel(starts_ref, queries_ref, paired_ref, weight_ref, terms_ref, held, ready):
    rows = SLICE // 8
    copies = [
        pltpu.make_async_copy(
            weight_ref.at[pl.ds(k * rows, rows)], held.at[pl.ds(k * rows, rows)], ready.at[k]
        )
        for k in range(8)
    ]
    for copy in copies:
        copy.start()
    keys = paired_ref[:, 0].reshape(SHARDS * TOK, HD)
    values = paired_ref[:, 1].reshape(SHARDS * TOK, HD)
    rows = lax.broadcasted_iota(jnp.int32, (TOK, TOK), 0)
    lanes = lax.broadcasted_iota(jnp.int32, (TOK, TOK), 1)
    ahead = rows - lanes + starts_ref[SHARDS]
    keep = jnp.concatenate([ahead >= starts_ref[b] for b in range(SHARDS)], axis=1)
    heads = []
    for h in range(SLICE // HD):
        query = queries_ref[:, h * HD : (h + 1) * HD]
        scores = lax.dot_general(
            query, keys, (((1,), (1,)), ((), ())), preferred_element_type=F32
        )
        scores = jnp.where(keep, scores, -1e30)
        top = jnp.max(scores, axis=1, keepdims=True)
        expw = jnp.exp2((scores - top) * (HD**-0.5 * LOG2E))
        denom = jnp.sum(expw, axis=1, keepdims=True)
        summed = jnp.dot(expw.astype(BF16), values, preferred_element_type=F32)
        heads.append((summed / denom).astype(BF16))
    attended = jnp.concatenate(heads, axis=1)
    for copy in copies:
        copy.wait()
    for j in range(EXPERTS):
        terms_ref[j] = jnp.dot(
            attended, held[:, j * SLICE : (j + 1) * SLICE], preferred_element_type=F32
        ).astype(BF16)


def attention(starts, queries, paired, weight):
    whole = pl.BlockSpec(memory_space=pltpu.VMEM)
    return call(
        attention_kernel,
        shape((EXPERTS, TOK, SLICE)),
        48,
        2 * 10**9,
        13 * 10**6,
        in_specs=[
            pl.BlockSpec(memory_space=pltpu.SMEM),
            whole,
            whole,
            pl.BlockSpec(memory_space=pl.ANY),
        ],
        out_specs=whole,
        scratch_shapes=[
            pltpu.VMEM((SLICE, D), BF16),
            pltpu.SemaphoreType.DMA((8,)),
        ],
    )(starts, queries, paired, weight)


def dispatch_kernel(terms_ref, residual_ref, gain_ref, placing_ref, hidden_ref, out_ref):
    hidden = residual_ref[...].astype(F32)
    for j in range(EXPERTS):
        hidden = hidden + terms_ref[j].astype(F32)
    hidden_ref[...] = hidden
    mean = jnp.sum(hidden, axis=1, keepdims=True) * (1.0 / SLICE)
    apart = (hidden - mean).astype(BF16)
    lanes = lax.broadcasted_iota(jnp.int32, (TOK, TOK), 1)
    high, mid, low = pieces(mean)
    spread = jnp.where(lanes == 0, high, jnp.where(lanes == 1, mid, jnp.where(lanes == 2, low, 0.0)))
    means = spread.T[:AUX].astype(BF16)
    rows = lax.broadcasted_iota(jnp.int32, (AUX, SLICE), 0)
    high, mid, low = pieces(gain_ref[...])
    gains = jnp.where(rows == 3, high, jnp.where(rows == 4, mid, jnp.where(rows == 5, low, 0.0)))
    for e in range(EXPERTS):
        placing = placing_ref[e]
        out_ref[e, :CAP] = jnp.dot(placing[:CAP], apart, preferred_element_type=F32).astype(BF16)
        sent = lax.dot_general(means, placing, (((1,), (1,)), ((), ())), preferred_element_type=F32)
        out_ref[e, CAP:] = jnp.concatenate(
            [sent + gains[:, :TOK], gains[:, TOK:]], axis=1
        ).astype(BF16)


def dispatch(terms, residual, gain, placing):
    return call(
        dispatch_kernel,
        (shape((TOK, SLICE), F32), shape((EXPERTS, CAP + AUX, SLICE))),
        4,
        2 * 10**8,
        5 * 10**6,
    )(terms, residual, gain, placing)


def norm_kernel(arrived_ref, *refs):
    out_ref = refs[-1]
    rows = lax.broadcasted_iota(jnp.int32, (CAP, TOK), 0)
    lanes = lax.broadcasted_iota(jnp.int32, (CAP, TOK), 1)
    diagonal = (rows == lanes).astype(BF16)
    means = []
    total = jnp.zeros((CAP, 1), F32)
    for j in range(EXPERTS):
        turned = lax.dot_general(
            diagonal, arrived_ref[j, CAP:, :TOK], (((1,), (1,)), ((), ())), preferred_element_type=F32
        )
        means.append(turned[:, 0:1] + turned[:, 1:2] + turned[:, 2:3])
        total = total + SLICE * means[j]
    mean = total / D
    spread = jnp.zeros((CAP, 1), F32)
    for j in range(EXPERTS):
        apart = arrived_ref[j, :CAP].astype(F32) + (means[j] - mean)
        spread = spread + jnp.sum(apart * apart, axis=1, keepdims=True)
    scale = lax.rsqrt(spread / D + EPS)
    for j in range(EXPERTS):
        aux = arrived_ref[j, CAP:].astype(F32)
        gain = aux[3:4] + aux[4:5] + aux[5:6]
        apart = arrived_ref[j, :CAP].astype(F32) + (means[j] - mean)
        out_ref[j] = (apart * scale * gain).astype(BF16)


def norm(arrived, after):
    return call(
        norm_kernel,
        shape((EXPERTS, CAP, SLICE)),
        4,
        10**7,
        2 * 10**6,
        in_specs=[pl.BlockSpec(memory_space=pltpu.VMEM)]
        + [pl.BlockSpec(memory_space=pl.ANY)] * len(after),
    )(arrived, *after)


HELD = 2 * UNITS


def hold_kernel(*refs):
    weights, held, ready = refs[:6], refs[-4:-1], refs[-1]
    copies = [
        pltpu.make_async_copy(
            weights[2 * number + core],
            held[number].at[pl.ds(core * UNITS, UNITS)],
            ready.at[2 * number + core],
        )
        for number in range(3)
        for core in range(2)
    ]
    for copy in copies:
        copy.start()
    for copy in copies:
        copy.wait()


def hold(weights, after):
    apart = pl.BlockSpec(memory_space=pl.ANY)
    return call(
        hold_kernel,
        tuple(pltpu.VMEM((HELD, D), BF16) for _ in range(3)),
        1,
        10**6,
        25 * 10**6,
        in_specs=[apart] * (6 + len(after)),
        out_specs=(pl.BlockSpec(memory_space=pltpu.VMEM),) * 3,
        scratch_shapes=[pltpu.SemaphoreType.DMA((6,))],
    )(*weights, *after)


def expert_kernel(pieces_in, pieces_out, n_in, n_out, *refs):
    xs, refs = refs[:n_in], refs[n_in:]
    gate_ref, up_ref, down_ref = refs[:3]
    outs, rows_ref = refs[len(refs) - n_out - 1 : -1], refs[-1]
    for shard, split in enumerate(pieces_in):
        block = 0
        for number, first, count in split:
            for k in range(first, first + count):
                rows_ref[
                    shard * CAP : (shard + 1) * CAP, block * SLICE : (block + 1) * SLICE
                ] = xs[number][k]
                block += 1
    turned = (((1,), (1,)), ((), ()))
    rows = rows_ref[...]
    few = rows.shape[0] <= 256
    pairs = [(held[...], rows) if few else (rows, held[...]) for held in (gate_ref, up_ref)]
    gate, up = [
        lax.dot_general(left, right, turned, preferred_element_type=F32) for left, right in pairs
    ]
    act = gate / (1.0 + jnp.exp(-gate)) * up
    act = (act.T if few else act).astype(BF16)
    for now in range(EXPERTS):
        result = jnp.dot(
            act, down_ref[:, now * SLICE : (now + 1) * SLICE], preferred_element_type=F32
        ).astype(BF16)
        for shard, split in enumerate(pieces_out):
            block = 0
            for number, first, count in split:
                if block <= now < block + count:
                    outs[number][first + now - block] = result[shard * CAP : (shard + 1) * CAP]
                block += count


def expert(arrays, pieces_in, sizes, pieces_out, held, after=()):
    total = CAP * len(pieces_in)
    whole = pl.BlockSpec(memory_space=pltpu.VMEM)
    return call(
        functools.partial(expert_kernel, pieces_in, pieces_out, len(arrays), len(sizes)),
        tuple(shape((size, CAP, SLICE)) for size in sizes),
        10,
        total * D * 2 * UNITS * 6,
        25 * 10**6,
        in_specs=[whole] * (len(arrays) + 3) + [pl.BlockSpec(memory_space=pl.ANY)] * len(after),
        out_specs=(whole,) * len(sizes),
        scratch_shapes=[pltpu.VMEM((total, D), BF16)],
    )(*arrays, *held, *after)


def join_kernel(plans, *refs):
    ins, outs = refs, refs[len(refs) - len(plans) :]
    for (size, terms), out in zip(plans, outs):
        for block in range(size):
            total = None
            for number, first, into, count in terms:
                if into <= block < into + count:
                    value = ins[number][first + block - into]
                    if total is None:
                        total = value
                    else:
                        total = total.astype(F32) + value.astype(F32)
            out[block] = total.astype(BF16)


def join(plans, *arrays, after=()):
    whole = pl.BlockSpec(memory_space=pltpu.VMEM)
    return call(
        functools.partial(join_kernel, plans),
        tuple(shape((size, CAP, SLICE)) for size, _ in plans),
        2,
        10**7,
        8 * 10**6,
        in_specs=[whole] * len(arrays) + [pl.BlockSpec(memory_space=pl.ANY)] * len(after),
        out_specs=(whole,) * len(plans),
    )(*arrays, *after)


def combine_kernel(hidden_ref, high_ref, low_ref, outputs_ref, mixed_ref):
    outputs = outputs_ref[...].reshape(EXPERTS * CAP, SLICE)
    moe = jnp.dot(high_ref[...], outputs, preferred_element_type=F32)
    moe += jnp.dot(low_ref[...], outputs, preferred_element_type=F32)
    mixed_ref[...] = (hidden_ref[...] + moe).astype(BF16)


def combine(hidden, high, low, outputs):
    return call(combine_kernel, shape((TOK, SLICE)), 4, 3 * 10**8, 2 * 10**6)(
        hidden, high, low, outputs
    )


def body(
    queries,
    keys,
    values,
    residual,
    ln_gain,
    out_weight,
    gate_weight,
    up_weight,
    down_weight,
    expert_ids,
    gate_scores,
):
    ctx = lax.axis_index("ctx")
    own = jnp.stack((keys, values))[None]
    first = jnp.concatenate([own, send(own, dz=1)])
    near = jnp.concatenate([first, send(first, dy=1), send(first, dy=-1), send(first, dy=2)])
    paired = jnp.concatenate([near, send(near, dc=1)])
    y, z, c = ctx // 4, (ctx // 2) % 2, ctx % 2
    starts = [
        ((((y - dy) % 4) * 2 + (z + dz) % 2) * 2 + (c + dc) % 2) * TOK
        for dc in (0, 1)
        for dy in (0, 1, -1, 2)
        for dz in (0, 1)
    ]
    starts = jnp.stack(starts + [ctx * TOK]).astype(jnp.int32)
    placing, share_high, share_low = routing(expert_ids, gate_scores)
    weights = []
    for weight in (gate_weight[0].T, up_weight[0].T, down_weight[0]):
        weights += [weight, send(weight, dc=1)]

    terms = attention(starts, queries, paired, out_weight)
    terms = lax.all_to_all(terms, "exp", 0, 0, tiled=True)
    hidden, outgoing = dispatch(terms, residual, ln_gain[None], placing)
    mine = norm(lax.all_to_all(outgoing, "exp", 0, 0, tiled=True), weights[5:])

    across, back, ahead = send(mine, dz=1), send(mine, dy=1), send(mine, dy=-1)
    held = hold(weights, (mine,))
    up, down, over = join(
        (
            (9, ((0, 0, 0, 4), (2, 0, 4, 3), (2, 4, 7, 2))),
            (9, ((1, 4, 0, 4), (2, 0, 4, 3), (2, 4, 7, 2))),
            (6, ((0, 3, 0, 1), (0, 6, 1, 2), (1, 3, 3, 1), (1, 6, 4, 2))),
        ),
        back,
        ahead,
        across,
        after=(held[0],),
    )
    low, high, both = send(up, dy=1), send(down, dy=-1), send(over, dz=1)
    mine, across, back, ahead, across_b = expert(
        [mine, across, back, ahead],
        [[(k, 0, 8)] for k in range(4)],
        (8, 5, 8, 8, 3),
        [[(0, 0, 8)], [(1, 0, 3), (4, 0, 1), (1, 3, 2), (4, 1, 2)], [(2, 0, 8)], [(3, 0, 8)]],
        held,
    )
    up, down, over = join(
        (
            (3, ((0, 4, 0, 3),)),
            (2, ((1, 7, 0, 2),)),
            (3, ((0, 3, 0, 1), (1, 2, 1, 2))),
        ),
        low,
        high,
        both,
        after=(mine,),
    )
    across_far = [send(up, dy=1), send(down, dy=-1), send(over, dz=1)]
    far_low, far_high, far_rest, across_back, across_ahead, over = expert(
        [low, high, both],
        [
            [(0, 0, 4), (1, 0, 4)],
            [(0, 4, 3), (2, 0, 1), (0, 7, 2), (2, 1, 2)],
            [(1, 4, 3), (2, 3, 1), (1, 7, 2), (2, 4, 2)],
        ],
        (3, 2, 3, 5, 5, 6),
        [
            [(0, 0, 3), (2, 0, 1), (1, 0, 2), (2, 1, 2)],
            [(3, 0, 3), (5, 0, 1), (3, 3, 2), (5, 1, 2)],
            [(4, 0, 3), (5, 3, 1), (4, 3, 2), (5, 4, 2)],
        ],
        held,
    )
    low, high, over = send(far_low, dy=1), send(far_high, dy=-1), send(over, dz=1)
    last_low, last_high, last_over = expert(
        across_far,
        [[(0, 0, 3), (2, 0, 1), (1, 0, 2), (2, 1, 2)]],
        (3, 2, 3),
        [[(0, 0, 3), (2, 0, 1), (1, 0, 2), (2, 1, 2)]],
        held,
        (far_low,),
    )
    up, down = join(
        (
            (6, ((0, 0, 0, 5), (3, 0, 0, 3), (2, 0, 5, 1), (5, 0, 5, 1))),
            (7, ((1, 0, 0, 5), (4, 0, 3, 2), (2, 1, 5, 2), (5, 1, 5, 2))),
        ),
        across_ahead,
        across_back,
        far_rest,
        send(last_low, dy=1),
        send(last_high, dy=-1),
        send(last_over, dz=1),
        after=(low, high, over),
    )
    up, down, across_b = send(up, dy=1), send(down, dy=-1), send(across_b, dz=1)
    across, ahead, back = join(
        (
            (5, ((0, 0, 0, 5), (3, 0, 0, 5), (4, 0, 0, 5))),
            (8, ((1, 0, 0, 8), (5, 0, 0, 3), (3, 5, 3, 1), (7, 3, 3, 1), (7, 4, 6, 2))),
            (8, ((2, 0, 0, 8), (6, 0, 4, 2), (4, 5, 6, 2), (7, 0, 3, 1), (7, 1, 6, 2))),
        ),
        across,
        ahead,
        back,
        up,
        down,
        low,
        high,
        over,
        after=(across_b,),
    )
    (result,) = join(
        (
            (
                8,
                (
                    (0, 0, 0, 8),
                    (1, 0, 0, 8),
                    (2, 0, 0, 8),
                    (3, 0, 0, 3),
                    (3, 3, 4, 2),
                    (4, 0, 3, 1),
                    (4, 1, 6, 2),
                ),
            ),
        ),
        mine,
        send(ahead, dy=1),
        send(back, dy=-1),
        send(across, dz=1),
        across_b,
    )
    outputs = lax.all_to_all(result, "exp", 0, 0, tiled=True)
    return combine(hidden, share_high, share_low, outputs)


def solution(mesh):
    return jax.shard_map(
        body,
        mesh=mesh,
        in_specs=(
            P("ctx", "exp"),
            P("ctx", "exp"),
            P("ctx", "exp"),
            P("ctx", "exp"),
            P("exp"),
            P("exp", None),
            P("exp", None, "ctx"),
            P("exp", None, "ctx"),
            P("exp", "ctx", None),
            P("ctx", None),
            P("ctx", None),
        ),
        out_specs=P("ctx", "exp"),
        check_vma=False,
    )
```

```python
import functools

import jax
import jax.numpy as jnp
from jax import lax
from jax.experimental import pallas as pl
from jax.experimental.pallas import tpu as pltpu
from jax.sharding import PartitionSpec as P

D = 6144
HD = 128
EXPERTS = 8
TOPK = 4
CAP = 80
AUX = 16
TOK = 128
SLICE = 768
SHARDS = 16
UNITS = 336
EPS = 1e-05
LOG2E = 1.4426950408889634
F32 = jnp.float32
BF16 = jnp.bfloat16
MIB = 1 << 20


def place(index):
    return index // 4, (index // 2) % 2, index % 2


def route(dy, dz, dc):
    pairs = []
    for index in range(SHARDS):
        y, z, c = place(index)
        pairs.append((index, (((y + dy) % 4) * 2 + (z + dz) % 2) * 2 + (c + dc) % 2))
    return pairs


def send(block, dy=0, dz=0, dc=0):
    return lax.ppermute(block, "ctx", route(dy, dz, dc))


def call(kernel, out_shape, limit, flops, moved, **kwargs):
    return pl.pallas_call(
        kernel,
        out_shape=out_shape,
        compiler_params=pltpu.CompilerParams(vmem_limit_bytes=limit * MIB),
        cost_estimate=pl.CostEstimate(flops=flops, bytes_accessed=moved, transcendentals=0),
        **kwargs,
    )


def shape(dims, dtype=BF16):
    return jax.ShapeDtypeStruct(dims, dtype)


def pieces(value):
    high = value.astype(BF16).astype(F32)
    left = value - high
    mid = left.astype(BF16).astype(F32)
    return high, mid, left - mid


def routing_kernel(ids_ref, scores_ref, placing_ref, high_ref, low_ref):
    ids = ids_ref[...]
    scores = scores_ref[...]
    total = scores[:, 0:1] + scores[:, 1:2] + scores[:, 2:3] + scores[:, 3:4]
    lanes = lax.broadcasted_iota(jnp.int32, (TOK, TOK), 1)
    rows = lax.broadcasted_iota(jnp.int32, (TOK, TOK), 0)
    named = [(lanes == ids[:, k : k + 1]).astype(F32) for k in range(TOPK)]
    member = named[0] + named[1] + named[2] + named[3]
    lower = (lanes < rows).astype(BF16)
    slots = jnp.dot(lower, member.astype(BF16), preferred_element_type=F32)
    wide = lax.broadcasted_iota(jnp.int32, (TOK, EXPERTS * TOK), 1)
    columns = lax.broadcasted_iota(jnp.int32, (TOK, EXPERTS * CAP), 1)
    placed = jnp.zeros((TOK, EXPERTS * TOK), F32)
    shares = jnp.zeros((TOK, EXPERTS * CAP), F32)
    for k in range(TOPK):
        slot = jnp.sum(named[k] * slots, axis=1, keepdims=True).astype(jnp.int32)
        expert = ids[:, k : k + 1]
        placed = placed + (wide == expert * TOK + slot).astype(F32)
        share = scores[:, k : k + 1] / total
        shares = shares + jnp.where(columns == expert * CAP + slot, share, 0.0)
    for e in range(EXPERTS):
        placing_ref[e] = placed[:, e * TOK : (e + 1) * TOK].T.astype(BF16)
    high = shares.astype(BF16)
    high_ref[...] = high
    low_ref[...] = (shares - high.astype(F32)).astype(BF16)


def routing(expert_ids, gate_scores):
    return call(
        routing_kernel,
        (
            shape((EXPERTS, TOK, TOK)),
            shape((TOK, EXPERTS * CAP)),
            shape((TOK, EXPERTS * CAP)),
        ),
        6,
        10**7,
        10**6,
    )(expert_ids, gate_scores)


def attention_kernel(starts_ref, queries_ref, paired_ref, weight_ref, terms_ref, held, ready):
    rows = SLICE // 4
    copies = [
        pltpu.make_async_copy(
            weight_ref.at[pl.ds(k * rows, rows)], held.at[pl.ds(k * rows, rows)], ready.at[k]
        )
        for k in range(4)
    ]
    for copy in copies:
        copy.start()
    keys = paired_ref[:, 0].reshape(SHARDS * TOK, HD)
    values = paired_ref[:, 1].reshape(SHARDS * TOK, HD)
    rows = lax.broadcasted_iota(jnp.int32, (TOK, TOK), 0)
    lanes = lax.broadcasted_iota(jnp.int32, (TOK, TOK), 1)
    ahead = rows - lanes + starts_ref[SHARDS]
    keep = jnp.concatenate([ahead >= starts_ref[b] for b in range(SHARDS)], axis=1)
    heads = []
    for h in range(SLICE // HD):
        query = queries_ref[:, h * HD : (h + 1) * HD]
        scores = lax.dot_general(
            query, keys, (((1,), (1,)), ((), ())), preferred_element_type=F32
        )
        scores = jnp.where(keep, scores, -1e30)
        top = jnp.max(scores, axis=1, keepdims=True)
        expw = jnp.exp2((scores - top) * (HD**-0.5 * LOG2E))
        denom = jnp.sum(expw, axis=1, keepdims=True)
        summed = jnp.dot(expw.astype(BF16), values, preferred_element_type=F32)
        heads.append((summed / denom).astype(BF16))
    attended = jnp.concatenate(heads, axis=1)
    for copy in copies:
        copy.wait()
    for j in range(EXPERTS):
        terms_ref[j] = jnp.dot(
            attended, held[:, j * SLICE : (j + 1) * SLICE], preferred_element_type=F32
        ).astype(BF16)


def attention(starts, queries, paired, weight):
    whole = pl.BlockSpec(memory_space=pltpu.VMEM)
    return call(
        attention_kernel,
        shape((EXPERTS, TOK, SLICE)),
        48,
        2 * 10**9,
        13 * 10**6,
        in_specs=[
            pl.BlockSpec(memory_space=pltpu.SMEM),
            whole,
            whole,
            pl.BlockSpec(memory_space=pl.ANY),
        ],
        out_specs=whole,
        scratch_shapes=[
            pltpu.VMEM((SLICE, D), BF16),
            pltpu.SemaphoreType.DMA((4,)),
        ],
    )(starts, queries, paired, weight)


def dispatch_kernel(terms_ref, residual_ref, gain_ref, placing_ref, hidden_ref, out_ref):
    hidden = residual_ref[...].astype(F32)
    for j in range(EXPERTS):
        hidden = hidden + terms_ref[j].astype(F32)
    hidden_ref[...] = hidden
    mean = jnp.sum(hidden, axis=1, keepdims=True) * (1.0 / SLICE)
    apart = (hidden - mean).astype(BF16)
    lanes = lax.broadcasted_iota(jnp.int32, (TOK, TOK), 1)
    high, mid, low = pieces(mean)
    spread = jnp.where(lanes == 0, high, jnp.where(lanes == 1, mid, jnp.where(lanes == 2, low, 0.0)))
    means = spread.T[:AUX].astype(BF16)
    rows = lax.broadcasted_iota(jnp.int32, (AUX, SLICE), 0)
    high, mid, low = pieces(gain_ref[...])
    gains = jnp.where(rows == 3, high, jnp.where(rows == 4, mid, jnp.where(rows == 5, low, 0.0)))
    for e in range(EXPERTS):
        placing = placing_ref[e]
        out_ref[e, :CAP] = jnp.dot(placing[:CAP], apart, preferred_element_type=F32).astype(BF16)
        sent = lax.dot_general(means, placing, (((1,), (1,)), ((), ())), preferred_element_type=F32)
        out_ref[e, CAP:] = jnp.concatenate(
            [sent + gains[:, :TOK], gains[:, TOK:]], axis=1
        ).astype(BF16)


def dispatch(terms, residual, gain, placing):
    return call(
        dispatch_kernel,
        (shape((TOK, SLICE), F32), shape((EXPERTS, CAP + AUX, SLICE))),
        4,
        2 * 10**8,
        5 * 10**6,
    )(terms, residual, gain, placing)


def norm_kernel(arrived_ref, *refs):
    out_ref = refs[-1]
    rows = lax.broadcasted_iota(jnp.int32, (CAP, TOK), 0)
    lanes = lax.broadcasted_iota(jnp.int32, (CAP, TOK), 1)
    diagonal = (rows == lanes).astype(BF16)
    means = []
    total = jnp.zeros((CAP, 1), F32)
    for j in range(EXPERTS):
        turned = lax.dot_general(
            diagonal, arrived_ref[j, CAP:, :TOK], (((1,), (1,)), ((), ())), preferred_element_type=F32
        )
        means.append(turned[:, 0:1] + turned[:, 1:2] + turned[:, 2:3])
        total = total + SLICE * means[j]
    mean = total / D
    spread = jnp.zeros((CAP, 1), F32)
    for j in range(EXPERTS):
        apart = arrived_ref[j, :CAP].astype(F32) + (means[j] - mean)
        spread = spread + jnp.sum(apart * apart, axis=1, keepdims=True)
    scale = lax.rsqrt(spread / D + EPS)
    for j in range(EXPERTS):
        aux = arrived_ref[j, CAP:].astype(F32)
        gain = aux[3:4] + aux[4:5] + aux[5:6]
        apart = arrived_ref[j, :CAP].astype(F32) + (means[j] - mean)
        out_ref[j] = (apart * scale * gain).astype(BF16)


def norm(arrived, after):
    return call(
        norm_kernel,
        shape((EXPERTS, CAP, SLICE)),
        4,
        10**7,
        2 * 10**6,
        in_specs=[pl.BlockSpec(memory_space=pltpu.VMEM)]
        + [pl.BlockSpec(memory_space=pl.ANY)] * len(after),
    )(arrived, *after)


HELD = 2 * UNITS


def hold_kernel(*refs):
    weights, held, ready = refs[:6], refs[-4:-1], refs[-1]
    copies = [
        pltpu.make_async_copy(
            weights[2 * number + core],
            held[number].at[pl.ds(core * UNITS, UNITS)],
            ready.at[2 * number + core],
        )
        for number in range(3)
        for core in range(2)
    ]
    for copy in copies:
        copy.start()
    for copy in copies:
        copy.wait()


def hold(weights, after):
    apart = pl.BlockSpec(memory_space=pl.ANY)
    return call(
        hold_kernel,
        tuple(pltpu.VMEM((HELD, D), BF16) for _ in range(3)),
        1,
        10**6,
        25 * 10**6,
        in_specs=[apart] * (6 + len(after)),
        out_specs=(pl.BlockSpec(memory_space=pltpu.VMEM),) * 3,
        scratch_shapes=[pltpu.SemaphoreType.DMA((6,))],
    )(*weights, *after)


def expert_kernel(pieces_in, pieces_out, n_in, n_out, *refs):
    xs, refs = refs[:n_in], refs[n_in:]
    gate_ref, up_ref, down_ref = refs[:3]
    outs, rows_ref = refs[len(refs) - n_out - 1 : -1], refs[-1]
    for shard, split in enumerate(pieces_in):
        block = 0
        for number, first, count in split:
            for k in range(first, first + count):
                rows_ref[
                    shard * CAP : (shard + 1) * CAP, block * SLICE : (block + 1) * SLICE
                ] = xs[number][k]
                block += 1
    turned = (((1,), (1,)), ((), ()))
    rows = rows_ref[...]
    few = rows.shape[0] <= 256
    pairs = [(held[...], rows) if few else (rows, held[...]) for held in (gate_ref, up_ref)]
    gate, up = [
        lax.dot_general(left, right, turned, preferred_element_type=F32) for left, right in pairs
    ]
    act = gate / (1.0 + jnp.exp(-gate)) * up
    act = (act.T if few else act).astype(BF16)
    for now in range(EXPERTS):
        result = jnp.dot(
            act, down_ref[:, now * SLICE : (now + 1) * SLICE], preferred_element_type=F32
        ).astype(BF16)
        for shard, split in enumerate(pieces_out):
            block = 0
            for number, first, count in split:
                if block <= now < block + count:
                    outs[number][first + now - block] = result[shard * CAP : (shard + 1) * CAP]
                block += count


def expert(arrays, pieces_in, sizes, pieces_out, held, after=()):
    total = CAP * len(pieces_in)
    whole = pl.BlockSpec(memory_space=pltpu.VMEM)
    return call(
        functools.partial(expert_kernel, pieces_in, pieces_out, len(arrays), len(sizes)),
        tuple(shape((size, CAP, SLICE)) for size in sizes),
        10,
        total * D * 2 * UNITS * 6,
        25 * 10**6,
        in_specs=[whole] * (len(arrays) + 3) + [pl.BlockSpec(memory_space=pl.ANY)] * len(after),
        out_specs=(whole,) * len(sizes),
        scratch_shapes=[pltpu.VMEM((total, D), BF16)],
    )(*arrays, *held, *after)


def join_kernel(plans, *refs):
    ins, outs = refs, refs[len(refs) - len(plans) :]
    for (size, terms), out in zip(plans, outs):
        for block in range(size):
            total = None
            for number, first, into, count in terms:
                if into <= block < into + count:
                    value = ins[number][first + block - into]
                    if total is None:
                        total = value
                    else:
                        total = total.astype(F32) + value.astype(F32)
            out[block] = total.astype(BF16)


def join(plans, *arrays, after=()):
    whole = pl.BlockSpec(memory_space=pltpu.VMEM)
    return call(
        functools.partial(join_kernel, plans),
        tuple(shape((size, CAP, SLICE)) for size, _ in plans),
        2,
        10**7,
        8 * 10**6,
        in_specs=[whole] * len(arrays) + [pl.BlockSpec(memory_space=pl.ANY)] * len(after),
        out_specs=(whole,) * len(plans),
    )(*arrays, *after)


def combine_kernel(hidden_ref, high_ref, low_ref, outputs_ref, mixed_ref):
    outputs = outputs_ref[...].reshape(EXPERTS * CAP, SLICE)
    moe = jnp.dot(high_ref[...], outputs, preferred_element_type=F32)
    moe += jnp.dot(low_ref[...], outputs, preferred_element_type=F32)
    mixed_ref[...] = (hidden_ref[...] + moe).astype(BF16)


def combine(hidden, high, low, outputs):
    return call(combine_kernel, shape((TOK, SLICE)), 4, 3 * 10**8, 2 * 10**6)(
        hidden, high, low, outputs
    )


def body(
    queries,
    keys,
    values,
    residual,
    ln_gain,
    out_weight,
    gate_weight,
    up_weight,
    down_weight,
    expert_ids,
    gate_scores,
):
    ctx = lax.axis_index("ctx")
    own = jnp.stack((keys, values))[None]
    first = jnp.concatenate([own, send(own, dz=1)])
    near = jnp.concatenate([first, send(first, dy=1), send(first, dy=-1), send(first, dy=2)])
    paired = jnp.concatenate([near, send(near, dc=1)])
    y, z, c = ctx // 4, (ctx // 2) % 2, ctx % 2
    starts = [
        ((((y - dy) % 4) * 2 + (z + dz) % 2) * 2 + (c + dc) % 2) * TOK
        for dc in (0, 1)
        for dy in (0, 1, -1, 2)
        for dz in (0, 1)
    ]
    starts = jnp.stack(starts + [ctx * TOK]).astype(jnp.int32)
    placing, share_high, share_low = routing(expert_ids, gate_scores)
    weights = []
    for weight in (gate_weight[0].T, up_weight[0].T, down_weight[0]):
        weights += [weight, send(weight, dc=1)]

    terms = attention(starts, queries, paired, out_weight)
    terms = lax.all_to_all(terms, "exp", 0, 0, tiled=True)
    hidden, outgoing = dispatch(terms, residual, ln_gain[None], placing)
    mine = norm(lax.all_to_all(outgoing, "exp", 0, 0, tiled=True), weights[5:])

    across, back, ahead = send(mine, dz=1), send(mine, dy=1), send(mine, dy=-1)
    held = hold(weights, (mine,))
    up, down, over = join(
        (
            (9, ((0, 0, 0, 4), (2, 0, 4, 3), (2, 4, 7, 2))),
            (9, ((1, 4, 0, 4), (2, 0, 4, 3), (2, 4, 7, 2))),
            (6, ((0, 3, 0, 1), (0, 6, 1, 2), (1, 3, 3, 1), (1, 6, 4, 2))),
        ),
        back,
        ahead,
        across,
        after=(held[0],),
    )
    low, high, both = send(up, dy=1), send(down, dy=-1), send(over, dz=1)
    mine, across, back, ahead, across_b = expert(
        [mine, across, back, ahead],
        [[(k, 0, 8)] for k in range(4)],
        (8, 5, 8, 8, 3),
        [[(0, 0, 8)], [(1, 0, 3), (4, 0, 1), (1, 3, 2), (4, 1, 2)], [(2, 0, 8)], [(3, 0, 8)]],
        held,
    )
    across_b = send(across_b, dz=1)
    up, down, over = join(
        (
            (3, ((0, 4, 0, 3),)),
            (2, ((1, 7, 0, 2),)),
            (3, ((0, 3, 0, 1), (1, 2, 1, 2))),
        ),
        low,
        high,
        both,
        after=(mine,),
    )
    across_far = [send(up, dy=1), send(down, dy=-1), send(over, dz=1)]
    far_low, far_high, far_rest, across_back, across_ahead, back_b, ahead_b = expert(
        [low, high, both],
        [
            [(0, 0, 4), (1, 0, 4)],
            [(0, 4, 3), (2, 0, 1), (0, 7, 2), (2, 1, 2)],
            [(1, 4, 3), (2, 3, 1), (1, 7, 2), (2, 4, 2)],
        ],
        (3, 2, 3, 5, 5, 3, 3),
        [
            [(0, 0, 3), (2, 0, 1), (1, 0, 2), (2, 1, 2)],
            [(3, 0, 3), (5, 0, 1), (3, 3, 2), (5, 1, 2)],
            [(4, 0, 3), (6, 0, 1), (4, 3, 2), (6, 1, 2)],
        ],
        held,
        (across_b,),
    )
    low, high, back_b = send(far_low, dy=1), send(far_high, dy=-1), send(back_b, dz=1)
    last_low, last_high, last_over = expert(
        across_far,
        [[(0, 0, 3), (2, 0, 1), (1, 0, 2), (2, 1, 2)]],
        (3, 2, 3),
        [[(0, 0, 3), (2, 0, 1), (1, 0, 2), (2, 1, 2)]],
        held,
        (far_low,),
    )
    up, down = join(
        (
            (6, ((0, 0, 0, 5), (3, 0, 0, 3), (2, 0, 5, 1), (5, 0, 5, 1))),
            (7, ((1, 0, 0, 5), (4, 0, 3, 2), (2, 1, 5, 2), (5, 1, 5, 2))),
        ),
        across_ahead,
        across_back,
        far_rest,
        send(last_low, dy=1),
        send(last_high, dy=-1),
        send(last_over, dz=1),
        after=(low, high, back_b),
    )
    up, down, ahead_b = send(up, dy=1), send(down, dy=-1), send(ahead_b, dz=1)
    across, ahead, back = join(
        (
            (5, ((0, 0, 0, 5), (3, 0, 0, 5), (4, 0, 0, 5))),
            (8, ((1, 0, 0, 8), (5, 0, 0, 3), (3, 5, 3, 1), (7, 0, 3, 1), (7, 1, 6, 2))),
            (8, ((2, 0, 0, 8), (6, 0, 4, 2), (4, 5, 6, 2), (8, 0, 3, 1), (8, 1, 6, 2))),
        ),
        across,
        ahead,
        back,
        up,
        down,
        low,
        high,
        ahead_b,
        back_b,
    )
    (result,) = join(
        (
            (
                8,
                (
                    (0, 0, 0, 8),
                    (1, 0, 0, 8),
                    (2, 0, 0, 8),
                    (3, 0, 0, 3),
                    (3, 3, 4, 2),
                    (4, 0, 3, 1),
                    (4, 1, 6, 2),
                ),
            ),
        ),
        mine,
        send(ahead, dy=1),
        send(back, dy=-1),
        send(across, dz=1),
        across_b,
    )
    outputs = lax.all_to_all(result, "exp", 0, 0, tiled=True)
    return combine(hidden, share_high, share_low, outputs)


def solution(mesh):
    return jax.shard_map(
        body,
        mesh=mesh,
        in_specs=(
            P("ctx", "exp"),
            P("ctx", "exp"),
            P("ctx", "exp"),
            P("ctx", "exp"),
            P("exp"),
            P("exp", None),
            P("exp", None, "ctx"),
            P("exp", None, "ctx"),
            P("exp", "ctx", None),
            P("ctx", None),
            P("ctx", None),
        ),
        out_specs=P("ctx", "exp"),
        check_vma=False,
    )
```

```python
import functools

import jax
import jax.numpy as jnp
from jax import lax
from jax.experimental import pallas as pl
from jax.experimental.pallas import tpu as pltpu
from jax.sharding import PartitionSpec as P

D = 6144
HD = 128
EXPERTS = 8
TOPK = 4
CAP = 80
AUX = 16
TOK = 128
SLICE = 768
SHARDS = 16
UNITS = 336
EPS = 1e-05
LOG2E = 1.4426950408889634
F32 = jnp.float32
BF16 = jnp.bfloat16
MIB = 1 << 20


def place(index):
    return index // 4, (index // 2) % 2, index % 2


def route(dy, dz, dc):
    pairs = []
    for index in range(SHARDS):
        y, z, c = place(index)
        pairs.append((index, (((y + dy) % 4) * 2 + (z + dz) % 2) * 2 + (c + dc) % 2))
    return pairs


def send(block, dy=0, dz=0, dc=0):
    return lax.ppermute(block, "ctx", route(dy, dz, dc))


def call(kernel, out_shape, limit, flops, moved, **kwargs):
    return pl.pallas_call(
        kernel,
        out_shape=out_shape,
        compiler_params=pltpu.CompilerParams(vmem_limit_bytes=limit * MIB),
        cost_estimate=pl.CostEstimate(flops=flops, bytes_accessed=moved, transcendentals=0),
        **kwargs,
    )


def shape(dims, dtype=BF16):
    return jax.ShapeDtypeStruct(dims, dtype)


def pieces(value):
    high = value.astype(BF16).astype(F32)
    left = value - high
    mid = left.astype(BF16).astype(F32)
    return high, mid, left - mid


def routing_kernel(ids_ref, scores_ref, placing_ref, high_ref, low_ref):
    ids = ids_ref[...]
    scores = scores_ref[...]
    total = scores[:, 0:1] + scores[:, 1:2] + scores[:, 2:3] + scores[:, 3:4]
    lanes = lax.broadcasted_iota(jnp.int32, (TOK, TOK), 1)
    rows = lax.broadcasted_iota(jnp.int32, (TOK, TOK), 0)
    named = [(lanes == ids[:, k : k + 1]).astype(F32) for k in range(TOPK)]
    member = named[0] + named[1] + named[2] + named[3]
    lower = (lanes < rows).astype(BF16)
    slots = jnp.dot(lower, member.astype(BF16), preferred_element_type=F32)
    wide = lax.broadcasted_iota(jnp.int32, (TOK, EXPERTS * TOK), 1)
    columns = lax.broadcasted_iota(jnp.int32, (TOK, EXPERTS * CAP), 1)
    placed = jnp.zeros((TOK, EXPERTS * TOK), F32)
    shares = jnp.zeros((TOK, EXPERTS * CAP), F32)
    for k in range(TOPK):
        slot = jnp.sum(named[k] * slots, axis=1, keepdims=True).astype(jnp.int32)
        expert = ids[:, k : k + 1]
        placed = placed + (wide == expert * TOK + slot).astype(F32)
        share = scores[:, k : k + 1] / total
        shares = shares + jnp.where(columns == expert * CAP + slot, share, 0.0)
    for e in range(EXPERTS):
        placing_ref[e] = placed[:, e * TOK : (e + 1) * TOK].T.astype(BF16)
    high = shares.astype(BF16)
    high_ref[...] = high
    low_ref[...] = (shares - high.astype(F32)).astype(BF16)


def routing(expert_ids, gate_scores):
    return call(
        routing_kernel,
        (
            shape((EXPERTS, TOK, TOK)),
            shape((TOK, EXPERTS * CAP)),
            shape((TOK, EXPERTS * CAP)),
        ),
        6,
        10**7,
        10**6,
    )(expert_ids, gate_scores)


def attention_kernel(starts_ref, queries_ref, paired_ref, weight_ref, terms_ref, held, ready):
    rows = SLICE // 4
    copies = [
        pltpu.make_async_copy(
            weight_ref.at[pl.ds(k * rows, rows)], held.at[pl.ds(k * rows, rows)], ready.at[k]
        )
        for k in range(4)
    ]
    for copy in copies:
        copy.start()
    keys = paired_ref[:, 0].reshape(SHARDS * TOK, HD)
    values = paired_ref[:, 1].reshape(SHARDS * TOK, HD)
    rows = lax.broadcasted_iota(jnp.int32, (TOK, TOK), 0)
    lanes = lax.broadcasted_iota(jnp.int32, (TOK, TOK), 1)
    ahead = rows - lanes + starts_ref[SHARDS]
    keep = jnp.concatenate([ahead >= starts_ref[b] for b in range(SHARDS)], axis=1)
    heads = []
    for h in range(SLICE // HD):
        query = queries_ref[:, h * HD : (h + 1) * HD]
        scores = lax.dot_general(
            query, keys, (((1,), (1,)), ((), ())), preferred_element_type=F32
        )
        scores = jnp.where(keep, scores, -1e30)
        top = jnp.max(scores, axis=1, keepdims=True)
        expw = jnp.exp2((scores - top) * (HD**-0.5 * LOG2E))
        denom = jnp.sum(expw, axis=1, keepdims=True)
        summed = jnp.dot(expw.astype(BF16), values, preferred_element_type=F32)
        heads.append((summed / denom).astype(BF16))
    attended = jnp.concatenate(heads, axis=1)
    for copy in copies:
        copy.wait()
    for j in range(EXPERTS):
        terms_ref[j] = jnp.dot(
            attended, held[:, j * SLICE : (j + 1) * SLICE], preferred_element_type=F32
        ).astype(BF16)


def attention(starts, queries, paired, weight):
    whole = pl.BlockSpec(memory_space=pltpu.VMEM)
    return call(
        attention_kernel,
        shape((EXPERTS, TOK, SLICE)),
        48,
        2 * 10**9,
        13 * 10**6,
        in_specs=[
            pl.BlockSpec(memory_space=pltpu.SMEM),
            whole,
            whole,
            pl.BlockSpec(memory_space=pl.ANY),
        ],
        out_specs=whole,
        scratch_shapes=[
            pltpu.VMEM((SLICE, D), BF16),
            pltpu.SemaphoreType.DMA((4,)),
        ],
    )(starts, queries, paired, weight)


def dispatch_kernel(terms_ref, residual_ref, gain_ref, placing_ref, hidden_ref, out_ref):
    hidden = residual_ref[...].astype(F32)
    for j in range(EXPERTS):
        hidden = hidden + terms_ref[j].astype(F32)
    hidden_ref[...] = hidden
    mean = jnp.sum(hidden, axis=1, keepdims=True) * (1.0 / SLICE)
    apart = (hidden - mean).astype(BF16)
    lanes = lax.broadcasted_iota(jnp.int32, (TOK, TOK), 1)
    high, mid, low = pieces(mean)
    spread = jnp.where(lanes == 0, high, jnp.where(lanes == 1, mid, jnp.where(lanes == 2, low, 0.0)))
    means = spread.T[:AUX].astype(BF16)
    rows = lax.broadcasted_iota(jnp.int32, (AUX, SLICE), 0)
    high, mid, low = pieces(gain_ref[...])
    gains = jnp.where(rows == 3, high, jnp.where(rows == 4, mid, jnp.where(rows == 5, low, 0.0)))
    for e in range(EXPERTS):
        placing = placing_ref[e]
        out_ref[e, :CAP] = jnp.dot(placing[:CAP], apart, preferred_element_type=F32).astype(BF16)
        sent = lax.dot_general(means, placing, (((1,), (1,)), ((), ())), preferred_element_type=F32)
        out_ref[e, CAP:] = jnp.concatenate(
            [sent + gains[:, :TOK], gains[:, TOK:]], axis=1
        ).astype(BF16)


def dispatch(terms, residual, gain, placing):
    return call(
        dispatch_kernel,
        (shape((TOK, SLICE), F32), shape((EXPERTS, CAP + AUX, SLICE))),
        4,
        2 * 10**8,
        5 * 10**6,
    )(terms, residual, gain, placing)


def norm_kernel(arrived_ref, *refs):
    out_ref = refs[-1]
    rows = lax.broadcasted_iota(jnp.int32, (CAP, TOK), 0)
    lanes = lax.broadcasted_iota(jnp.int32, (CAP, TOK), 1)
    diagonal = (rows == lanes).astype(BF16)
    means = []
    total = jnp.zeros((CAP, 1), F32)
    for j in range(EXPERTS):
        turned = lax.dot_general(
            diagonal, arrived_ref[j, CAP:, :TOK], (((1,), (1,)), ((), ())), preferred_element_type=F32
        )
        means.append(turned[:, 0:1] + turned[:, 1:2] + turned[:, 2:3])
        total = total + SLICE * means[j]
    mean = total / D
    spread = jnp.zeros((CAP, 1), F32)
    for j in range(EXPERTS):
        apart = arrived_ref[j, :CAP].astype(F32) + (means[j] - mean)
        spread = spread + jnp.sum(apart * apart, axis=1, keepdims=True)
    scale = lax.rsqrt(spread / D + EPS)
    for j in range(EXPERTS):
        aux = arrived_ref[j, CAP:].astype(F32)
        gain = aux[3:4] + aux[4:5] + aux[5:6]
        apart = arrived_ref[j, :CAP].astype(F32) + (means[j] - mean)
        out_ref[j] = (apart * scale * gain).astype(BF16)


def norm(arrived, after):
    return call(
        norm_kernel,
        shape((EXPERTS, CAP, SLICE)),
        4,
        10**7,
        2 * 10**6,
        in_specs=[pl.BlockSpec(memory_space=pltpu.VMEM)]
        + [pl.BlockSpec(memory_space=pl.ANY)] * len(after),
    )(arrived, *after)


HELD = 2 * UNITS


def hold_kernel(*refs):
    weights, held, ready = refs[:6], refs[-4:-1], refs[-1]
    copies = [
        pltpu.make_async_copy(
            weights[2 * number + core],
            held[number].at[pl.ds(core * UNITS, UNITS)],
            ready.at[2 * number + core],
        )
        for number in range(3)
        for core in range(2)
    ]
    for copy in copies:
        copy.start()
    for copy in copies:
        copy.wait()


def hold(weights, after):
    apart = pl.BlockSpec(memory_space=pl.ANY)
    return call(
        hold_kernel,
        tuple(pltpu.VMEM((HELD, D), BF16) for _ in range(3)),
        1,
        10**6,
        25 * 10**6,
        in_specs=[apart] * (6 + len(after)),
        out_specs=(pl.BlockSpec(memory_space=pltpu.VMEM),) * 3,
        scratch_shapes=[pltpu.SemaphoreType.DMA((6,))],
    )(*weights, *after)


def expert_kernel(pieces_in, pieces_out, n_in, n_out, *refs):
    xs, refs = refs[:n_in], refs[n_in:]
    gate_ref, up_ref, down_ref = refs[:3]
    outs, rows_ref = refs[len(refs) - n_out - 1 : -1], refs[-1]
    for shard, split in enumerate(pieces_in):
        block = 0
        for number, first, count in split:
            for k in range(first, first + count):
                rows_ref[
                    shard * CAP : (shard + 1) * CAP, block * SLICE : (block + 1) * SLICE
                ] = xs[number][k]
                block += 1
    turned = (((1,), (1,)), ((), ()))
    rows = rows_ref[...]
    few = rows.shape[0] <= 256
    pairs = [(held[...], rows) if few else (rows, held[...]) for held in (gate_ref, up_ref)]
    gate, up = [
        lax.dot_general(left, right, turned, preferred_element_type=F32) for left, right in pairs
    ]
    act = gate / (1.0 + jnp.exp(-gate)) * up
    act = (act.T if few else act).astype(BF16)
    for now in range(EXPERTS):
        result = jnp.dot(
            act, down_ref[:, now * SLICE : (now + 1) * SLICE], preferred_element_type=F32
        ).astype(BF16)
        for shard, split in enumerate(pieces_out):
            block = 0
            for number, first, count in split:
                if block <= now < block + count:
                    outs[number][first + now - block] = result[shard * CAP : (shard + 1) * CAP]
                block += count


def expert(arrays, pieces_in, sizes, pieces_out, held, after=()):
    total = CAP * len(pieces_in)
    whole = pl.BlockSpec(memory_space=pltpu.VMEM)
    return call(
        functools.partial(expert_kernel, pieces_in, pieces_out, len(arrays), len(sizes)),
        tuple(shape((size, CAP, SLICE)) for size in sizes),
        10,
        total * D * 2 * UNITS * 6,
        25 * 10**6,
        in_specs=[whole] * (len(arrays) + 3) + [pl.BlockSpec(memory_space=pl.ANY)] * len(after),
        out_specs=(whole,) * len(sizes),
        scratch_shapes=[pltpu.VMEM((total, D), BF16)],
    )(*arrays, *held, *after)


def join_kernel(plans, *refs):
    ins, outs = refs, refs[len(refs) - len(plans) :]
    for (size, terms), out in zip(plans, outs):
        for block in range(size):
            total = None
            for number, first, into, count in terms:
                if into <= block < into + count:
                    value = ins[number][first + block - into]
                    if total is None:
                        total = value
                    else:
                        total = total.astype(F32) + value.astype(F32)
            out[block] = total.astype(BF16)


def join(plans, *arrays, after=()):
    whole = pl.BlockSpec(memory_space=pltpu.VMEM)
    return call(
        functools.partial(join_kernel, plans),
        tuple(shape((size, CAP, SLICE)) for size, _ in plans),
        2,
        10**7,
        8 * 10**6,
        in_specs=[whole] * len(arrays) + [pl.BlockSpec(memory_space=pl.ANY)] * len(after),
        out_specs=(whole,) * len(plans),
    )(*arrays, *after)


def combine_kernel(hidden_ref, high_ref, low_ref, outputs_ref, mixed_ref):
    outputs = outputs_ref[...].reshape(EXPERTS * CAP, SLICE)
    moe = jnp.dot(high_ref[...], outputs, preferred_element_type=F32)
    moe += jnp.dot(low_ref[...], outputs, preferred_element_type=F32)
    mixed_ref[...] = (hidden_ref[...] + moe).astype(BF16)


def combine(hidden, high, low, outputs):
    return call(combine_kernel, shape((TOK, SLICE)), 4, 3 * 10**8, 2 * 10**6)(
        hidden, high, low, outputs
    )


def body(
    queries,
    keys,
    values,
    residual,
    ln_gain,
    out_weight,
    gate_weight,
    up_weight,
    down_weight,
    expert_ids,
    gate_scores,
):
    ctx = lax.axis_index("ctx")
    own = jnp.stack((keys, values))[None]
    first = jnp.concatenate([own, send(own, dz=1)])
    near = jnp.concatenate([first, send(first, dy=1), send(first, dy=-1), send(first, dy=2)])
    paired = jnp.concatenate([near, send(near, dc=1)])
    y, z, c = ctx // 4, (ctx // 2) % 2, ctx % 2
    starts = [
        ((((y - dy) % 4) * 2 + (z + dz) % 2) * 2 + (c + dc) % 2) * TOK
        for dc in (0, 1)
        for dy in (0, 1, -1, 2)
        for dz in (0, 1)
    ]
    starts = jnp.stack(starts + [ctx * TOK]).astype(jnp.int32)
    placing, share_high, share_low = routing(expert_ids, gate_scores)
    weights = []
    for weight in (gate_weight[0].T, up_weight[0].T, down_weight[0]):
        weights += [weight, send(weight, dc=1)]

    terms = attention(starts, queries, paired, out_weight)
    terms = lax.all_to_all(terms, "exp", 0, 0, tiled=True)
    hidden, outgoing = dispatch(terms, residual, ln_gain[None], placing)
    mine = norm(lax.all_to_all(outgoing, "exp", 0, 0, tiled=True), weights[5:])

    across, back, ahead = send(mine, dz=1), send(mine, dy=1), send(mine, dy=-1)
    held = hold(weights, (mine,))
    up, down, over = join(
        (
            (9, ((0, 0, 0, 4), (2, 0, 4, 3), (2, 4, 7, 2))),
            (9, ((1, 4, 0, 4), (2, 0, 4, 3), (2, 4, 7, 2))),
            (6, ((0, 3, 0, 1), (0, 6, 1, 2), (1, 3, 3, 1), (1, 6, 4, 2))),
        ),
        back,
        ahead,
        across,
        after=(held[0],),
    )
    low, high, both = send(up, dy=1), send(down, dy=-1), send(over, dz=1)
    mine, across, back, ahead, across_b = expert(
        [mine, across, back, ahead],
        [[(k, 0, 8)] for k in range(4)],
        (8, 5, 8, 8, 3),
        [[(0, 0, 8)], [(1, 0, 3), (4, 0, 1), (1, 3, 2), (4, 1, 2)], [(2, 0, 8)], [(3, 0, 8)]],
        held,
    )
    up, down, over = join(
        (
            (3, ((0, 4, 0, 3),)),
            (2, ((1, 7, 0, 2),)),
            (3, ((0, 3, 0, 1), (1, 2, 1, 2))),
        ),
        low,
        high,
        both,
        after=(mine,),
    )
    across_far = [send(up, dy=1), send(down, dy=-1), send(over, dz=1)]
    far_low, far_high, far_rest, across_back, across_ahead, over = expert(
        [low, high, both],
        [
            [(0, 0, 4), (1, 0, 4)],
            [(0, 4, 3), (2, 0, 1), (0, 7, 2), (2, 1, 2)],
            [(1, 4, 3), (2, 3, 1), (1, 7, 2), (2, 4, 2)],
        ],
        (3, 2, 3, 5, 5, 6),
        [
            [(0, 0, 3), (2, 0, 1), (1, 0, 2), (2, 1, 2)],
            [(3, 0, 3), (5, 0, 1), (3, 3, 2), (5, 1, 2)],
            [(4, 0, 3), (5, 3, 1), (4, 3, 2), (5, 4, 2)],
        ],
        held,
    )
    low, high, over = send(far_low, dy=1), send(far_high, dy=-1), send(over, dz=1)
    last_low, last_high, last_over = expert(
        across_far,
        [[(0, 0, 3), (2, 0, 1), (1, 0, 2), (2, 1, 2)]],
        (3, 2, 3),
        [[(0, 0, 3), (2, 0, 1), (1, 0, 2), (2, 1, 2)]],
        held,
        (far_low,),
    )
    up, down = join(
        (
            (6, ((0, 0, 0, 5), (3, 0, 0, 3), (2, 0, 5, 1), (5, 0, 5, 1))),
            (7, ((1, 0, 0, 5), (4, 0, 3, 2), (2, 1, 5, 2), (5, 1, 5, 2))),
        ),
        across_ahead,
        across_back,
        far_rest,
        send(last_low, dy=1),
        send(last_high, dy=-1),
        send(last_over, dz=1),
        after=(low, high, over),
    )
    up, down, across_b = send(up, dy=1), send(down, dy=-1), send(across_b, dz=1)
    across, ahead, back = join(
        (
            (5, ((0, 0, 0, 5), (3, 0, 0, 5), (4, 0, 0, 5))),
            (8, ((1, 0, 0, 8), (5, 0, 0, 3), (3, 5, 3, 1), (7, 3, 3, 1), (7, 4, 6, 2))),
            (8, ((2, 0, 0, 8), (6, 0, 4, 2), (4, 5, 6, 2), (7, 0, 3, 1), (7, 1, 6, 2))),
        ),
        across,
        ahead,
        back,
        up,
        down,
        low,
        high,
        over,
        after=(across_b,),
    )
    (result,) = join(
        (
            (
                8,
                (
                    (0, 0, 0, 8),
                    (1, 0, 0, 8),
                    (2, 0, 0, 8),
                    (3, 0, 0, 3),
                    (3, 3, 4, 2),
                    (4, 0, 3, 1),
                    (4, 1, 6, 2),
                ),
            ),
        ),
        mine,
        send(ahead, dy=1),
        send(back, dy=-1),
        send(across, dz=1),
        across_b,
    )
    outputs = lax.all_to_all(result, "exp", 0, 0, tiled=True)
    return combine(hidden, share_high, share_low, outputs)


def solution(mesh):
    return jax.shard_map(
        body,
        mesh=mesh,
        in_specs=(
            P("ctx", "exp"),
            P("ctx", "exp"),
            P("ctx", "exp"),
            P("ctx", "exp"),
            P("exp"),
            P("exp", None),
            P("exp", None, "ctx"),
            P("exp", None, "ctx"),
            P("exp", "ctx", None),
            P("ctx", None),
            P("ctx", None),
        ),
        out_specs=P("ctx", "exp"),
        check_vma=False,
    )
```

```python
import functools

import jax
import jax.numpy as jnp
from jax import lax
from jax.experimental import pallas as pl
from jax.experimental.pallas import tpu as pltpu
from jax.sharding import PartitionSpec as P

D = 6144
HD = 128
EXPERTS = 8
TOPK = 4
CAP = 80
AUX = 16
TOK = 128
SLICE = 768
SHARDS = 16
UNITS = 336
EPS = 1e-05
LOG2E = 1.4426950408889634
F32 = jnp.float32
BF16 = jnp.bfloat16
MIB = 1 << 20


def place(index):
    return index // 4, (index // 2) % 2, index % 2


def route(dy, dz, dc):
    pairs = []
    for index in range(SHARDS):
        y, z, c = place(index)
        pairs.append((index, (((y + dy) % 4) * 2 + (z + dz) % 2) * 2 + (c + dc) % 2))
    return pairs


def send(block, dy=0, dz=0, dc=0):
    return lax.ppermute(block, "ctx", route(dy, dz, dc))


def call(kernel, out_shape, limit, flops, moved, **kwargs):
    return pl.pallas_call(
        kernel,
        out_shape=out_shape,
        compiler_params=pltpu.CompilerParams(vmem_limit_bytes=limit * MIB),
        cost_estimate=pl.CostEstimate(flops=flops, bytes_accessed=moved, transcendentals=0),
        **kwargs,
    )


def shape(dims, dtype=BF16):
    return jax.ShapeDtypeStruct(dims, dtype)


def pieces(value):
    high = value.astype(BF16).astype(F32)
    left = value - high
    mid = left.astype(BF16).astype(F32)
    return high, mid, left - mid


def routing_kernel(ids_ref, scores_ref, placing_ref, high_ref, low_ref):
    ids = ids_ref[...]
    scores = scores_ref[...]
    total = scores[:, 0:1] + scores[:, 1:2] + scores[:, 2:3] + scores[:, 3:4]
    lanes = lax.broadcasted_iota(jnp.int32, (TOK, TOK), 1)
    rows = lax.broadcasted_iota(jnp.int32, (TOK, TOK), 0)
    named = [(lanes == ids[:, k : k + 1]).astype(F32) for k in range(TOPK)]
    member = named[0] + named[1] + named[2] + named[3]
    lower = (lanes < rows).astype(BF16)
    slots = jnp.dot(lower, member.astype(BF16), preferred_element_type=F32)
    wide = lax.broadcasted_iota(jnp.int32, (TOK, EXPERTS * TOK), 1)
    columns = lax.broadcasted_iota(jnp.int32, (TOK, EXPERTS * CAP), 1)
    placed = jnp.zeros((TOK, EXPERTS * TOK), F32)
    shares = jnp.zeros((TOK, EXPERTS * CAP), F32)
    for k in range(TOPK):
        slot = jnp.sum(named[k] * slots, axis=1, keepdims=True).astype(jnp.int32)
        expert = ids[:, k : k + 1]
        placed = placed + (wide == expert * TOK + slot).astype(F32)
        share = scores[:, k : k + 1] / total
        shares = shares + jnp.where(columns == expert * CAP + slot, share, 0.0)
    for e in range(EXPERTS):
        placing_ref[e] = placed[:, e * TOK : (e + 1) * TOK].T.astype(BF16)
    high = shares.astype(BF16)
    high_ref[...] = high
    low_ref[...] = (shares - high.astype(F32)).astype(BF16)


def routing(expert_ids, gate_scores):
    return call(
        routing_kernel,
        (
            shape((EXPERTS, TOK, TOK)),
            shape((TOK, EXPERTS * CAP)),
            shape((TOK, EXPERTS * CAP)),
        ),
        6,
        10**7,
        10**6,
    )(expert_ids, gate_scores)


def attention_kernel(starts_ref, queries_ref, paired_ref, weight_ref, terms_ref, held, ready):
    rows = SLICE // 4
    copies = [
        pltpu.make_async_copy(
            weight_ref.at[pl.ds(k * rows, rows)], held.at[pl.ds(k * rows, rows)], ready.at[k]
        )
        for k in range(4)
    ]
    for copy in copies:
        copy.start()
    keys = paired_ref[:, 0].reshape(SHARDS * TOK, HD)
    values = paired_ref[:, 1].reshape(SHARDS * TOK, HD)
    rows = lax.broadcasted_iota(jnp.int32, (TOK, TOK), 0)
    lanes = lax.broadcasted_iota(jnp.int32, (TOK, TOK), 1)
    ahead = rows - lanes + starts_ref[SHARDS]
    keep = jnp.concatenate([ahead >= starts_ref[b] for b in range(SHARDS)], axis=1)
    heads = []
    for h in range(queries_ref.shape[1] // HD):
        query = queries_ref[:, h * HD : (h + 1) * HD]
        scores = lax.dot_general(
            query, keys, (((1,), (1,)), ((), ())), preferred_element_type=F32
        )
        scores = jnp.where(keep, scores, -1e30)
        top = jnp.max(scores, axis=1, keepdims=True)
        expw = jnp.exp2((scores - top) * (HD**-0.5 * LOG2E))
        denom = jnp.sum(expw, axis=1, keepdims=True)
        summed = jnp.dot(expw.astype(BF16), values, preferred_element_type=F32)
        heads.append((summed / denom).astype(BF16))
    attended = jnp.concatenate(heads, axis=1)
    for copy in copies:
        copy.wait()
    for j in range(EXPERTS):
        terms_ref[j] = jnp.dot(
            attended, held[:, j * SLICE : (j + 1) * SLICE], preferred_element_type=F32
        ).astype(BF16)


def attention(starts, queries, paired, weight):
    whole = pl.BlockSpec(memory_space=pltpu.VMEM)
    return call(
        attention_kernel,
        shape((EXPERTS, TOK, SLICE)),
        48,
        2 * 10**9,
        13 * 10**6,
        in_specs=[pl.BlockSpec(memory_space=pltpu.SMEM), whole, whole]
        + [pl.BlockSpec(memory_space=pl.ANY)],
        out_specs=whole,
        scratch_shapes=[pltpu.VMEM((SLICE, D), BF16), pltpu.SemaphoreType.DMA((4,))],
    )(starts, queries, paired, weight)


def dispatch_kernel(terms_ref, residual_ref, gain_ref, placing_ref, hidden_ref, out_ref):
    hidden = residual_ref[...].astype(F32)
    for j in range(EXPERTS):
        hidden = hidden + terms_ref[j].astype(F32)
    hidden_ref[...] = hidden
    mean = jnp.sum(hidden, axis=1, keepdims=True) * (1.0 / SLICE)
    apart = (hidden - mean).astype(BF16)
    lanes = lax.broadcasted_iota(jnp.int32, (TOK, TOK), 1)
    high, mid, low = pieces(mean)
    spread = jnp.where(lanes == 0, high, jnp.where(lanes == 1, mid, jnp.where(lanes == 2, low, 0.0)))
    means = spread.T[:AUX].astype(BF16)
    rows = lax.broadcasted_iota(jnp.int32, (AUX, SLICE), 0)
    high, mid, low = pieces(gain_ref[...])
    gains = jnp.where(rows == 3, high, jnp.where(rows == 4, mid, jnp.where(rows == 5, low, 0.0)))
    for e in range(EXPERTS):
        placing = placing_ref[e]
        out_ref[e, :CAP] = jnp.dot(placing[:CAP], apart, preferred_element_type=F32).astype(BF16)
        sent = lax.dot_general(means, placing, (((1,), (1,)), ((), ())), preferred_element_type=F32)
        out_ref[e, CAP:] = jnp.concatenate(
            [sent + gains[:, :TOK], gains[:, TOK:]], axis=1
        ).astype(BF16)


def dispatch(terms, residual, gain, placing):
    return call(
        dispatch_kernel,
        (shape((TOK, SLICE), F32), shape((EXPERTS, CAP + AUX, SLICE))),
        4,
        2 * 10**8,
        5 * 10**6,
    )(terms, residual, gain, placing)


def norm_kernel(arrived_ref, *refs):
    out_ref = refs[-1]
    rows = lax.broadcasted_iota(jnp.int32, (CAP, TOK), 0)
    lanes = lax.broadcasted_iota(jnp.int32, (CAP, TOK), 1)
    diagonal = (rows == lanes).astype(BF16)
    means = []
    total = jnp.zeros((CAP, 1), F32)
    for j in range(EXPERTS):
        turned = lax.dot_general(
            diagonal, arrived_ref[j, CAP:, :TOK], (((1,), (1,)), ((), ())), preferred_element_type=F32
        )
        means.append(turned[:, 0:1] + turned[:, 1:2] + turned[:, 2:3])
        total = total + SLICE * means[j]
    mean = total / D
    spread = jnp.zeros((CAP, 1), F32)
    for j in range(EXPERTS):
        apart = arrived_ref[j, :CAP].astype(F32) + (means[j] - mean)
        spread = spread + jnp.sum(apart * apart, axis=1, keepdims=True)
    scale = lax.rsqrt(spread / D + EPS)
    for j in range(EXPERTS):
        aux = arrived_ref[j, CAP:].astype(F32)
        gain = aux[3:4] + aux[4:5] + aux[5:6]
        apart = arrived_ref[j, :CAP].astype(F32) + (means[j] - mean)
        out_ref[j] = (apart * scale * gain).astype(BF16)


def norm(arrived, after):
    return call(
        norm_kernel,
        shape((EXPERTS, CAP, SLICE)),
        4,
        10**7,
        2 * 10**6,
        in_specs=[pl.BlockSpec(memory_space=pltpu.VMEM)]
        + [pl.BlockSpec(memory_space=pl.ANY)] * len(after),
    )(arrived, *after)


HELD = 2 * UNITS


def hold_kernel(*refs):
    weights, held, ready = refs[:6], refs[-4:-1], refs[-1]
    copies = [
        pltpu.make_async_copy(
            weights[2 * number + core],
            held[number].at[pl.ds(core * UNITS, UNITS)],
            ready.at[2 * number + core],
        )
        for number in range(3)
        for core in range(2)
    ]
    for copy in copies:
        copy.start()
    for copy in copies:
        copy.wait()


def hold(weights, after):
    apart = pl.BlockSpec(memory_space=pl.ANY)
    return call(
        hold_kernel,
        tuple(pltpu.VMEM((HELD, D), BF16) for _ in range(3)),
        1,
        10**6,
        25 * 10**6,
        in_specs=[apart] * (6 + len(after)),
        out_specs=(pl.BlockSpec(memory_space=pltpu.VMEM),) * 3,
        scratch_shapes=[pltpu.SemaphoreType.DMA((6,))],
    )(*weights, *after)


def expert_kernel(pieces_in, pieces_out, n_in, n_out, *refs):
    xs, refs = refs[:n_in], refs[n_in:]
    gate_ref, up_ref, down_ref = refs[:3]
    outs, rows_ref = refs[len(refs) - n_out - 1 : -1], refs[-1]
    for shard, split in enumerate(pieces_in):
        block = 0
        for number, first, count in split:
            for k in range(first, first + count):
                rows_ref[
                    shard * CAP : (shard + 1) * CAP, block * SLICE : (block + 1) * SLICE
                ] = xs[number][k]
                block += 1
    turned = (((1,), (1,)), ((), ()))
    rows = rows_ref[...]
    gate = lax.dot_general(rows, gate_ref[...], turned, preferred_element_type=F32)
    up = lax.dot_general(rows, up_ref[...], turned, preferred_element_type=F32)
    act = (gate / (1.0 + jnp.exp(-gate)) * up).astype(BF16)
    for now in range(EXPERTS):
        result = jnp.dot(
            act, down_ref[:, now * SLICE : (now + 1) * SLICE], preferred_element_type=F32
        ).astype(BF16)
        for shard, split in enumerate(pieces_out):
            block = 0
            for number, first, count in split:
                if block <= now < block + count:
                    outs[number][first + now - block] = result[shard * CAP : (shard + 1) * CAP]
                block += count


def expert(arrays, pieces_in, sizes, pieces_out, held, after=()):
    total = CAP * len(pieces_in)
    whole = pl.BlockSpec(memory_space=pltpu.VMEM)
    return call(
        functools.partial(expert_kernel, pieces_in, pieces_out, len(arrays), len(sizes)),
        tuple(shape((size, CAP, SLICE)) for size in sizes),
        10,
        total * D * 2 * UNITS * 6,
        25 * 10**6,
        in_specs=[whole] * (len(arrays) + 3) + [pl.BlockSpec(memory_space=pl.ANY)] * len(after),
        out_specs=(whole,) * len(sizes),
        scratch_shapes=[pltpu.VMEM((total, D), BF16)],
    )(*arrays, *held, *after)


def join_kernel(plans, *refs):
    ins, outs = refs, refs[len(refs) - len(plans) :]
    for (size, terms), out in zip(plans, outs):
        for block in range(size):
            total = None
            for number, first, into, count in terms:
                if into <= block < into + count:
                    value = ins[number][first + block - into]
                    if total is None:
                        total = value
                    else:
                        total = total.astype(F32) + value.astype(F32)
            out[block] = total.astype(BF16)


def join(plans, *arrays, after=()):
    whole = pl.BlockSpec(memory_space=pltpu.VMEM)
    return call(
        functools.partial(join_kernel, plans),
        tuple(shape((size, CAP, SLICE)) for size, _ in plans),
        2,
        10**7,
        8 * 10**6,
        in_specs=[whole] * len(arrays) + [pl.BlockSpec(memory_space=pl.ANY)] * len(after),
        out_specs=(whole,) * len(plans),
    )(*arrays, *after)


def combine_kernel(hidden_ref, high_ref, low_ref, outputs_ref, mixed_ref):
    outputs = outputs_ref[...].reshape(EXPERTS * CAP, SLICE)
    moe = jnp.dot(high_ref[...], outputs, preferred_element_type=F32)
    moe += jnp.dot(low_ref[...], outputs, preferred_element_type=F32)
    mixed_ref[...] = (hidden_ref[...] + moe).astype(BF16)


def combine(hidden, high, low, outputs):
    return call(combine_kernel, shape((TOK, SLICE)), 4, 3 * 10**8, 2 * 10**6)(
        hidden, high, low, outputs
    )


def body(
    queries,
    keys,
    values,
    residual,
    ln_gain,
    out_weight,
    gate_weight,
    up_weight,
    down_weight,
    expert_ids,
    gate_scores,
):
    ctx = lax.axis_index("ctx")
    own = jnp.stack((keys, values))[None]
    first = jnp.concatenate([own, send(own, dz=1)])
    near = jnp.concatenate([first, send(first, dy=1), send(first, dy=-1), send(first, dy=2)])
    paired = jnp.concatenate([near, send(near, dc=1)])
    y, z, c = ctx // 4, (ctx // 2) % 2, ctx % 2
    starts = [
        ((((y - dy) % 4) * 2 + (z + dz) % 2) * 2 + (c + dc) % 2) * TOK
        for dc in (0, 1)
        for dy in (0, 1, -1, 2)
        for dz in (0, 1)
    ]
    starts = jnp.stack(starts + [ctx * TOK]).astype(jnp.int32)
    placing, share_high, share_low = routing(expert_ids, gate_scores)
    weights = []
    for weight in (gate_weight[0].T, up_weight[0].T, down_weight[0]):
        weights += [weight, send(weight, dc=1)]

    terms = attention(starts, queries, paired, out_weight)
    terms = lax.all_to_all(terms, "exp", 0, 0, tiled=True)
    hidden, outgoing = dispatch(terms, residual, ln_gain[None], placing)
    mine = norm(lax.all_to_all(outgoing, "exp", 0, 0, tiled=True), weights[5:])

    back, ahead, across = send(mine, dy=1), send(mine, dy=-1), send(mine, dz=1)
    held = hold(weights, (mine,))
    up, down, over = join(
        (
            (9, ((0, 0, 0, 4), (2, 0, 4, 3), (2, 4, 7, 2))),
            (9, ((1, 4, 0, 4), (2, 0, 4, 3), (2, 4, 7, 2))),
            (6, ((0, 3, 0, 1), (0, 6, 1, 2), (1, 3, 3, 1), (1, 6, 4, 2))),
        ),
        back,
        ahead,
        across,
        after=(held[0],),
    )
    low, high, both = send(up, dy=1), send(down, dy=-1), send(over, dz=1)
    mine, across, back, ahead, across_b = expert(
        [mine, across, back, ahead],
        [[(k, 0, 8)] for k in range(4)],
        (8, 5, 8, 8, 3),
        [[(0, 0, 8)], [(1, 0, 3), (4, 0, 1), (1, 3, 2), (4, 1, 2)], [(2, 0, 8)], [(3, 0, 8)]],
        held,
    )
    up, down, over = join(
        (
            (3, ((0, 4, 0, 3),)),
            (2, ((1, 7, 0, 2),)),
            (3, ((0, 3, 0, 1), (1, 2, 1, 2))),
        ),
        low,
        high,
        both,
        after=(mine,),
    )
    across_far = [send(up, dy=1), send(down, dy=-1), send(over, dz=1)]
    far_low, far_high, far_rest, across_back, across_ahead, over = expert(
        [low, high, both],
        [
            [(0, 0, 4), (1, 0, 4)],
            [(0, 4, 3), (2, 0, 1), (0, 7, 2), (2, 1, 2)],
            [(1, 4, 3), (2, 3, 1), (1, 7, 2), (2, 4, 2)],
        ],
        (3, 2, 3, 5, 5, 6),
        [
            [(0, 0, 3), (2, 0, 1), (1, 0, 2), (2, 1, 2)],
            [(3, 0, 3), (5, 0, 1), (3, 3, 2), (5, 1, 2)],
            [(4, 0, 3), (5, 3, 1), (4, 3, 2), (5, 4, 2)],
        ],
        held,
    )
    low, high, over = send(far_low, dy=1), send(far_high, dy=-1), send(over, dz=1)
    last_low, last_high, last_over = expert(
        across_far,
        [[(0, 0, 3), (2, 0, 1), (1, 0, 2), (2, 1, 2)]],
        (3, 2, 3),
        [[(0, 0, 3), (2, 0, 1), (1, 0, 2), (2, 1, 2)]],
        held,
        (far_low,),
    )
    up, down = join(
        (
            (6, ((0, 0, 0, 5), (3, 0, 0, 3), (2, 0, 5, 1), (5, 0, 5, 1))),
            (7, ((1, 0, 0, 5), (4, 0, 3, 2), (2, 1, 5, 2), (5, 1, 5, 2))),
        ),
        across_ahead,
        across_back,
        far_rest,
        send(last_low, dy=1),
        send(last_high, dy=-1),
        send(last_over, dz=1),
        after=(low, high, over),
    )
    up, down, across_b = send(up, dy=1), send(down, dy=-1), send(across_b, dz=1)
    across, ahead, back = join(
        (
            (5, ((0, 0, 0, 5), (3, 0, 0, 5), (4, 0, 0, 5))),
            (8, ((1, 0, 0, 8), (5, 0, 0, 3), (3, 5, 3, 1), (7, 3, 3, 1), (7, 4, 6, 2))),
            (8, ((2, 0, 0, 8), (6, 0, 4, 2), (4, 5, 6, 2), (7, 0, 3, 1), (7, 1, 6, 2))),
        ),
        across,
        ahead,
        back,
        up,
        down,
        low,
        high,
        over,
        after=(across_b,),
    )
    (result,) = join(
        (
            (
                8,
                (
                    (0, 0, 0, 8),
                    (1, 0, 0, 8),
                    (2, 0, 0, 8),
                    (3, 0, 0, 3),
                    (3, 3, 4, 2),
                    (4, 0, 3, 1),
                    (4, 1, 6, 2),
                ),
            ),
        ),
        mine,
        send(ahead, dy=1),
        send(back, dy=-1),
        send(across, dz=1),
        across_b,
    )
    outputs = lax.all_to_all(result, "exp", 0, 0, tiled=True)
    return combine(hidden, share_high, share_low, outputs)


def solution(mesh):
    return jax.shard_map(
        body,
        mesh=mesh,
        in_specs=(
            P("ctx", "exp"),
            P("ctx", "exp"),
            P("ctx", "exp"),
            P("ctx", "exp"),
            P("exp"),
            P("exp", None),
            P("exp", None, "ctx"),
            P("exp", None, "ctx"),
            P("exp", "ctx", None),
            P("ctx", None),
            P("ctx", None),
        ),
        out_specs=P("ctx", "exp"),
        check_vma=False,
    )
```
